32 devices in a mesh: group: 2 (over x), expert: 16 (over z, y, core).
Axes of the slice: x: 2, y: 2, z: 4, core: 2. Of those that a mesh axis runs over, the one named last changes fastest.
Arguments:
- q_abs: bfloat16 [4, 256, 36864], P(None, ('group', 'expert')), parts along dimension 1, may hold values from -24 to 24
- new_lat: bfloat16 [4, 256, 576], P(None, ('group', 'expert')), parts along dimension 1, may hold values from -24 to 24
- latent_cache: bfloat16 [256, 32, 576], P('group', 'expert'), parts along dimension 0, may hold values from -24 to 24
- lengths: int32 [256], P('group'), parts along dimension 0, may hold values from 1 to 32, 2048 in all
- owner: int32 [256], P('group'), parts along dimension 0, may hold values from 0 to 127, each once
- resid: bfloat16 [4, 256, 3584], P(None, ('group', 'expert')), parts along dimension 1, may hold values from -6 to 6
- routes: int32 [4, 256, 8], P(None, ('group', 'expert')), parts along dimension 1, may hold values from 0 to 15, all different within a row; in each aligned block of 8 rows (0 to 7, 8 to 15, ..., all dimensions but the last counted through in order) at most 6 rows name the same one
- w_out: bfloat16 [512, 3584], replicated, may hold values from -0.03125 to 0.03125
- norm_gain: bfloat16 [3584], replicated, may hold values from 0.5 to 1.5
- w_router: bfloat16 [3584, 16], replicated, may hold values from -0.09375 to 0.09375
- w_gate: bfloat16 [16, 3584, 1024], P('expert'), may hold values from -0.09375 to 0.09375
- w_up: bfloat16 [16, 3584, 1024], P('expert'), may hold values from -0.09375 to 0.09375
- w_down: bfloat16 [16, 1024, 3584], P('expert'), may hold values from -0.1875 to 0.1875
Outputs:
- mixed: bfloat16 [4, 256, 3584], P(None, ('group', 'expert')), parts along dimension 1
The draws below stay inside these ranges and needn't reach their ends.
There are 2 independent parts, one for each index of `group`. The reference program is written for one: setup_inputs(seed, part) draws one part's arguments, and reference() takes and returns one part's arrays. A program takes and returns all parts, laid end to end along the dimension named above; an argument that names none is the same for every part. Nothing has to cross between parts.
Inputs may be any that keep to these rules, and one draw needn't show every extreme that they name: `routes`: each row names 8 different experts; within the rows of one device at one step no expert is named by more than 6 rows, a bound that some block reaches. `owner`: each request is served by exactly one decode row. `lengths`: some request has all 32 positions.
All inputs are finite; a program needn't handle non-finite values.
Results may differ from the reference program's by a relative error of at most 0.012.
Values may be sent and summed in bfloat16 or wider, within the bound.
No kernel may reach another device: no remote copies, remote signals or barrier semaphores. Data moves between devices by JAX's collectives and lax.ppermute only.
A program may use at most 128 MiB of HBM per device.

```python
import math
import jax
import jax.numpy as jnp
import numpy as np
from jax import lax

D = 3584
HEADS = 64
LAT = 512
KV = 576
EH = 1024
EXPERTS = 16
SPLIT = 1
EH_DEV = 1024
TOPK = 8
STEPS = 4
REQ_DEV = 8
CAP = 6
REQS = 128
CTX = 32
N_EXPERT = 16


def draw_latent_cache(key, part):
    key = jax.random.fold_in(key, 11)
    rows = jnp.clip(jax.random.normal(key, (REQS, CTX, KV), jnp.float32), -6.0, 6.0)
    return rows.astype(jnp.bfloat16)


def draw_new_lat(key, part):
    key = jax.random.fold_in(key, 12)
    rows = jnp.clip(jax.random.normal(key, (STEPS, REQS, KV), jnp.float32), -6.0, 6.0)
    return rows.astype(jnp.bfloat16)


def draw_q_abs(key, part):
    key = jax.random.fold_in(key, 13)
    noise = jnp.clip(jax.random.normal(key, (STEPS, REQS, HEADS, KV), jnp.float32), -6.0, 6.0)
    return noise.reshape(STEPS, REQS, HEADS * KV).astype(jnp.bfloat16)


def block_levels(own_key, shape, split, low, top_value):
    loudness, own = 1.0, jax.random.fold_in(own_key, 6)
    for dim, blocks in split:
        heights = jnp.exp(jax.random.uniform(jax.random.fold_in(own, dim), (blocks,), jnp.float32, low / len(split), top_value / len(split)))
        loudness = loudness * jnp.repeat(heights, shape[dim] // blocks).reshape([-1 if axis == dim else 1 for axis in range(len(shape))])
    return loudness


def split_up(amount, total, reach, lean):
    weights = [(1 << 20) // math.isqrt(grade ** lean) + 1 for grade in range(2, amount + 1)]
    surplus, holding = total - reach - (amount - 1), [1] * (amount - 1)
    while surplus > 0:
        movable = [i for i in range(amount - 1) if holding[i] < reach]
        mass, left = sum([weights[i] for i in movable]), surplus
        for i in movable:
            extra = min(reach - holding[i], max(1, left * weights[i] // mass), surplus)
            holding[i] = holding[i] + extra
            surplus = surplus - extra
    return np.array([reach] + holding)


def ragged(key, number_of, total, limit, lean):
    if number_of == 2:
        one = jax.random.randint(key, (), max(1, total - limit), min(limit, total - 1) + 1)
        return jnp.stack([one, total - one])
    sizes = jnp.asarray(split_up(number_of, total, limit, lean), jnp.int32)
    pairs = (number_of - 1) // 2
    source_of, receiver = sizes[1:1 + 2 * pairs:2], sizes[2:2 + 2 * pairs:2]
    room = jnp.minimum(source_of - 1, limit - receiver)
    passed = jax.random.randint(jax.random.fold_in(key, 1), (pairs,), 0, 1 << 20) % (room + 1)
    sizes = sizes.at[1:1 + 2 * pairs:2].set(source_of - passed).at[2:2 + 2 * pairs:2].set(receiver + passed)
    return sizes[jax.random.permutation(jax.random.fold_in(key, 2), number_of)]


def assign_block(own_key, own, number, rows, number_of, top, limit, slope):
    sequence = jax.random.permutation(own_key, number_of)
    packed, ordinary = shares(number_of, rows * top, limit, slope, True), shares(number_of, rows * top, limit, slope, False)
    places = jnp.arange(number_of)

    def named(tallies, turn):
        used = int((tallies > 0).sum())
        fixed = max(1, used // 4)
        passed = fixed + (places - fixed + turn * (used - fixed)) % max(1, number_of - fixed)
        return jnp.zeros((number_of,), jnp.int32).at[sequence[jnp.where(places < fixed, places, passed)]].set(jnp.asarray(tallies, jnp.int32))

    tallies = jnp.where(number % 4 == 0, named(packed, number // 4), named(ordinary, number - number // 4 - 1))
    mixed = jax.random.permutation(jax.random.fold_in(own, 3), number_of)
    donor, taker = mixed[0:number_of // 2 * 2:2], mixed[1:number_of // 2 * 2:2]
    slack = jnp.minimum(tallies[donor] - 1, limit - tallies[taker]) // 2
    slack = jnp.where((donor == sequence[0]) | (taker == sequence[0]) | (tallies[taker] == 0), 0, jnp.maximum(slack, 0))
    passed = jax.random.randint(jax.random.fold_in(own, 4), (number_of // 2,), 0, 1 << 20) % (slack + 1)
    tallies = tallies.at[donor].add(-passed).at[taker].add(passed)
    labels = jnp.searchsorted(jnp.cumsum(tallies), jnp.arange(rows * top), side="right").astype(jnp.int32)
    listing = labels.reshape(top, rows).T
    listing = listing[jax.random.permutation(jax.random.fold_in(own, 1), rows)]
    turn = jax.random.randint(jax.random.fold_in(own, 2), (rows, 1), 0, top)
    return jnp.take_along_axis(listing, (jnp.arange(top)[None, :] + turn) % top, axis=1)


def shares(number_of, total, most, skew, full):
    portions = [(1 << 20) // math.isqrt(grade ** skew) + 1 for grade in range(1, number_of + 1)]
    largest = most if full else min(most, max(-(-total // number_of), total * portions[0] // sum(portions)))
    least = 1 if total - largest >= number_of - 1 else 0
    given, surplus = [largest] + [least] * (number_of - 1), total - largest - least * (number_of - 1)
    while surplus > 0:
        candidates = [i for i in range(1, number_of) if given[i] < largest] or [i for i in range(1, number_of) if given[i] < most]
        pool, budget = sum([portions[i] for i in candidates]), surplus
        for i in candidates:
            extra = min(most - given[i], max(1, budget * portions[i] // pool), surplus)
            given[i] = given[i] + extra
            surplus = surplus - extra
    return np.array(given)


def bell_draw(stream_key, shape, spread, most, split=(), kind=jnp.bfloat16):
    loudness = block_levels(stream_key, shape, split, -0.22, 0.18) if split else 1.0
    values = jax.random.normal(stream_key, shape, jnp.float32) * spread * loudness
    return jnp.minimum(jnp.maximum(values, -most), most).astype(kind)


def setup_inputs(seed: int = 0, part: int = 0) -> dict:
    keys = jax.random.split(jax.random.key(seed), 14)
    part_splits = jax.random.split(jax.random.fold_in(keys[13], part), 14)
    q_abs = draw_q_abs(jax.random.fold_in(jax.random.fold_in(keys[13], part), 71), part)
    new_lat = draw_new_lat(jax.random.fold_in(jax.random.fold_in(keys[13], part), 71), part)
    latent_cache = draw_latent_cache(jax.random.fold_in(jax.random.fold_in(keys[13], part), 71), part)
    lengths = ragged(part_splits[3], REQS, REQS * CTX // 2, CTX, 2).astype(jnp.int32)
    owner = jax.random.permutation(part_splits[4], REQS).astype(jnp.int32)
    resid = bell_draw(part_splits[5], (STEPS, REQS, D), 1.0, 6.0, ((1, 16),))
    routes_keys = jax.random.split(jax.random.fold_in(part_splits[6], 1), STEPS * REQS // REQ_DEV)
    routes_turns = jax.random.permutation(jax.random.fold_in(part_splits[6], 3), STEPS * REQS // REQ_DEV)
    routes = jax.vmap(lambda own, number: assign_block(jax.random.fold_in(part_splits[6], 2), own, number, REQ_DEV, EXPERTS, TOPK, CAP, 2))(routes_keys, routes_turns).reshape((STEPS, REQS, TOPK))
    w_out = bell_draw(keys[7], (LAT, D), (LAT * HEADS) ** -0.5, 0.03125)
    norm_gain = jnp.clip(1.0 + 0.1 * jax.random.normal(keys[8], (D,), jnp.float32), 0.5, 1.5).astype(jnp.bfloat16)
    w_router = bell_draw(keys[9], (D, EXPERTS), D ** -0.5, 0.09375)
    w_gate = bell_draw(keys[10], (N_EXPERT, D, EH_DEV), D ** -0.5, 0.09375, ((0, 16),))
    w_up = bell_draw(keys[11], (N_EXPERT, D, EH_DEV), D ** -0.5, 0.09375, ((0, 16),))
    w_down = bell_draw(keys[12], (N_EXPERT, EH_DEV, D), EH ** -0.5, 0.1875, ((0, 16),))
    return dict(q_abs=q_abs, new_lat=new_lat, latent_cache=latent_cache, lengths=lengths, owner=owner, resid=resid, routes=routes, w_out=w_out, norm_gain=norm_gain, w_router=w_router, w_gate=w_gate, w_up=w_up, w_down=w_down)


qk_scale = 192.0 ** (-0.5)

def reference(q_abs, new_lat, latent_cache, lengths, owner, resid, routes, w_out, norm_gain, w_router, w_gate, w_up, w_down):
    cache_keys = latent_cache[owner].astype(jnp.float32)
    row_lengths = lengths[owner]
    queries = q_abs.reshape(STEPS, REQS, HEADS, KV).astype(jnp.float32)
    fresh_keys = new_lat.astype(jnp.float32)
    cache_scores = jnp.einsum('srhk,rpk->srhp', queries, cache_keys) * qk_scale
    visible = jnp.arange(CTX)[None, :] < row_lengths[:, None]
    cache_scores = jnp.where(visible[None, :, None, :], cache_scores, -1e+30)
    fresh_scores = jnp.einsum('srhk,trk->srht', queries, fresh_keys) * qk_scale
    causal = jnp.arange(STEPS)[:, None] >= jnp.arange(STEPS)[None, :]
    fresh_scores = jnp.where(causal[:, None, None, :], fresh_scores, -1e+30)
    scores = jnp.concatenate([cache_scores, fresh_scores], axis=-1)
    weights = jax.nn.softmax(scores, axis=-1).astype(jnp.bfloat16)
    cache_weights = weights[..., :CTX].astype(jnp.float32)
    fresh_weights = weights[..., CTX:].astype(jnp.float32)
    pooled = jnp.einsum('srhp,rpl->srl', cache_weights, cache_keys[..., :LAT])
    pooled = pooled + jnp.einsum('srht,trl->srl', fresh_weights, fresh_keys[..., :LAT])
    pooled = pooled.astype(jnp.bfloat16)
    hidden_state = resid.astype(jnp.float32) + jnp.dot(pooled.reshape(-1, LAT), w_out, preferred_element_type=jnp.float32).reshape(STEPS, REQS, D)
    normed = hidden_state * lax.rsqrt(lax.optimization_barrier(jnp.mean(hidden_state * hidden_state, axis=-1, keepdims=True)) + 1e-06) * norm_gain.astype(jnp.float32)
    normed = normed.astype(jnp.bfloat16)
    flat_rows = normed.reshape(-1, D)
    affinity = jax.nn.sigmoid(jnp.dot(flat_rows, w_router, preferred_element_type=jnp.float32))
    flat_routes = routes.reshape(-1, TOPK)
    picked = jnp.take_along_axis(affinity, flat_routes, axis=1)
    gate_weights = 2.5 * picked / lax.optimization_barrier(jnp.sum(picked, axis=1, keepdims=True))
    tokens = STEPS * REQS
    capacity = STEPS * N_EXPERT * CAP
    gate_blocks = w_gate.reshape(EXPERTS, SPLIT, D, EH_DEV)
    up_blocks = w_up.reshape(EXPERTS, SPLIT, D, EH_DEV)
    down_blocks = w_down.reshape(EXPERTS, SPLIT, EH_DEV, D)

    def apply_expert(accum, expert):
        hit_pairs = flat_routes == expert
        routed = jnp.any(hit_pairs, axis=1)
        gate_each = lax.optimization_barrier(jnp.sum(jnp.where(hit_pairs, gate_weights, 0.0), axis=1))
        position = jnp.cumsum(routed.astype(jnp.int32)) - 1
        target = jnp.where(routed, position, capacity).astype(jnp.int32)
        slot_rows = jnp.zeros((capacity,), jnp.int32).at[target].set(jnp.arange(tokens, dtype=jnp.int32), mode='drop')
        filled = jnp.sum(routed.astype(jnp.int32))
        chosen = flat_rows[slot_rows].astype(jnp.float32)
        gate_part = jnp.einsum('md,kdf->kmf', chosen, gate_blocks[expert].astype(jnp.float32))
        up_part = jnp.einsum('md,kdf->kmf', chosen, up_blocks[expert].astype(jnp.float32))
        activated = (jax.nn.silu(gate_part) * up_part).astype(jnp.bfloat16).astype(jnp.float32)
        parts = jnp.einsum('kmf,kfd->kmd', activated, down_blocks[expert].astype(jnp.float32)).astype(jnp.bfloat16).astype(jnp.float32)
        expert_out = lax.optimization_barrier(jnp.sum(parts, axis=0))
        weighting = jnp.where(jnp.arange(capacity) < filled, gate_each[slot_rows], 0.0)
        accum = accum.at[slot_rows].add(weighting[:, None] * expert_out)
        return (accum, None)
    accum, unused = lax.scan(apply_expert, jnp.zeros((tokens, D), jnp.float32), jnp.arange(EXPERTS, dtype=jnp.int32))
    return (hidden_state + accum.reshape(STEPS, REQS, D)).astype(jnp.bfloat16)
```

```python
import jax
import jax.numpy as jnp
from jax import lax
from jax.experimental import pallas as pl
from jax.experimental.pallas import tpu as pltpu
from jax.sharding import PartitionSpec as P

qk_scale = 192.0 ** (-0.5)
LANES = 128


def ring_of(chips):
    return list(range(0, chips, 2)) + list(range(chips - 1, 0, -2))


def shift_perm(chips, by):
    ring = ring_of(chips)
    return [
        (2 * ring[p] + core, 2 * ring[(p + by) % chips] + core)
        for p in range(chips)
        for core in range(2)
    ]


def sibling_perm(chips):
    return [(d, d ^ 1) for d in range(2 * chips)]


def distances(chips):
    half = chips // 2
    order = [0]
    for t in range(1, half):
        order += [t, -t]
    return order + [half]


def tile_of(size, most):
    return max(t for t in range(LANES, min(size, most) + 1, LANES) if size % t == 0)


def expert_kernel(chips, rows, gate_steps, *refs):
    blocks = 2 * chips
    resid = refs[:blocks]
    (pooled_own, pooled_sib, w_out, gain, w_router, lane_pick, w_gate, w_up, w_down) = refs[
        blocks : blocks + 9
    ]
    hidden = refs[blocks + 9]
    outs = refs[blocks + 10 : blocks + 10 + blocks]
    x, act, ssq, scale, weight = refs[blocks + 10 + blocks :]
    step = pl.program_id(0)
    width = x.shape[1]
    latent = w_out.shape[0]
    side = chips * rows
    gate_tile = w_gate.shape[2]
    chunk = min(256, side)
    chunks = 2 * side // chunk

    @pl.when(step == 0)
    def _():
        ssq[...] = jnp.zeros_like(ssq)
        cols_tile = tile_of(width, 512)

        def columns(j, carry):
            cols = pl.ds(pl.multiple_of(j * cols_tile, cols_tile), cols_tile)
            w = w_out[:, cols]
            g = gain[:, cols].astype(jnp.float32)
            for s, pooled in enumerate((pooled_own, pooled_sib)):
                proj = jnp.dot(pooled[:, :latent], w, preferred_element_type=jnp.float32)
                for b in range(chips):
                    at = pl.ds((s * chips + b) * rows, rows)
                    h = proj[b * rows : (b + 1) * rows] + resid[s * chips + b][:, cols].astype(
                        jnp.float32
                    )
                    if s == 0 and b == 0:
                        hidden[:, cols] = h
                    x[at, cols] = (h * g).astype(jnp.bfloat16)
                    sq = h * h
                    part = sq[:, :LANES]
                    for k in range(1, cols_tile // LANES):
                        part = part + sq[:, k * LANES : (k + 1) * LANES]
                    ssq[at, :] += part
            return carry

        lax.fori_loop(0, width // cols_tile, columns, 0)
        for s, pooled in enumerate((pooled_own, pooled_sib)):
            at = pl.ds(s * side, side)
            mean = jnp.sum(ssq[at, :], axis=1, keepdims=True) * (1.0 / width)
            r = lax.rsqrt(mean + 1e-06)
            logits = jnp.dot(x[at, :], w_router[...], preferred_element_type=jnp.float32) * r
            affinity = jax.nn.sigmoid(logits) * pooled[:, latent:].astype(jnp.float32)
            total = jnp.sum(affinity, axis=1, keepdims=True)
            mine = jnp.sum(affinity * lane_pick[...], axis=1, keepdims=True)
            scale[at, :] = jnp.broadcast_to(r, (side, LANES))
            weight[at, :] = jnp.broadcast_to(2.5 * mine / total, (side, LANES))

    @pl.when((step > 0) & (step <= gate_steps))
    def _():
        cols = pl.ds(pl.multiple_of((step - 1) * gate_tile, gate_tile), gate_tile)

        def body(i, carry):
            at = pl.ds(pl.multiple_of(i * chunk, chunk), chunk)
            xs = x[at, :]
            r = scale[at, :1]
            a = jnp.dot(xs, w_gate[0], preferred_element_type=jnp.float32) * r
            b = jnp.dot(xs, w_up[0], preferred_element_type=jnp.float32) * r
            act[at, cols] = (jax.nn.silu(a) * b * weight[at, :1]).astype(jnp.bfloat16)
            return carry

        lax.fori_loop(0, chunks, body, 0)

    @pl.when(step > gate_steps)
    def _():
        per = chunk // rows
        for i in range(chunks):
            y = jnp.dot(
                act[i * chunk : (i + 1) * chunk, :], w_down[0], preferred_element_type=jnp.float32
            )
            for b in range(per):
                outs[i * per + b][...] = y[b * rows : (b + 1) * rows].astype(jnp.bfloat16)


def experts(resid_blocks, pooled_own, pooled_sib, w_out, gain, w_router, lane_pick, wg, wu, wd):
    blocks = len(resid_blocks)
    chips = blocks // 2
    rows, width = resid_blocks[0].shape
    hidden_units = wg.shape[2]
    gate_tile = tile_of(hidden_units, 256)
    gate_steps = hidden_units // gate_tile
    down_tile = tile_of(width, 1024)
    down_steps = width // down_tile
    total = blocks * rows

    def whole(a):
        return pl.BlockSpec(a.shape, lambda i: (0,) * a.ndim, pipeline_mode=pl.Buffered(1))

    def gate_at(i):
        return (0, 0, jnp.clip(i - 1, 0, gate_steps - 1))

    def down_at(i):
        return (0, 0, jnp.clip(i - 1 - gate_steps, 0, down_steps - 1))

    def out_at(i):
        return (0, jnp.clip(i - 1 - gate_steps, 0, down_steps - 1))

    fixed = list(resid_blocks) + [pooled_own, pooled_sib, w_out, gain, w_router, lane_pick]
    results = pl.pallas_call(
        lambda *refs: expert_kernel(chips, rows, gate_steps, *refs),
        grid=(1 + gate_steps + down_steps,),
        in_specs=[whole(a) for a in fixed]
        + [
            pl.BlockSpec((1, width, gate_tile), gate_at),
            pl.BlockSpec((1, width, gate_tile), gate_at),
            pl.BlockSpec((1, hidden_units, down_tile), down_at),
        ],
        out_shape=[jax.ShapeDtypeStruct((rows, width), jnp.float32)]
        + [jax.ShapeDtypeStruct((rows, width), jnp.bfloat16)] * blocks,
        out_specs=[pl.BlockSpec((rows, width), lambda i: (0, 0))]
        + [pl.BlockSpec((rows, down_tile), out_at)] * blocks,
        scratch_shapes=[
            pltpu.VMEM((total, width), jnp.bfloat16),
            pltpu.VMEM((total, hidden_units), jnp.bfloat16),
            pltpu.VMEM((total, LANES), jnp.float32),
            pltpu.VMEM((total, LANES), jnp.float32),
            pltpu.VMEM((total, LANES), jnp.float32),
        ],
        compiler_params=pltpu.CompilerParams(
            dimension_semantics=("arbitrary",), vmem_limit_bytes=56 * 1024 * 1024
        ),
        cost_estimate=pl.CostEstimate(
            flops=2 * total * width * (3 * hidden_units + w_out.shape[0]),
            bytes_accessed=3 * width * hidden_units * 2 + 2 * total * width * 2,
            transcendentals=total * hidden_units,
        ),
        name="experts",
    )(*fixed, wg, wu, wd)
    return results[0], results[1 : 1 + chips], results[1 + chips :]


def attention(q_abs, new_lat, owned_cache, row_lengths, latent):
    step_count, row_count, kv_width = new_lat.shape
    head_count = q_abs.shape[2] // kv_width
    context = owned_cache.shape[1]
    queries = q_abs.reshape(step_count, row_count, head_count, kv_width)
    cache_scores = (
        jnp.einsum("srhk,rpk->srhp", queries, owned_cache, preferred_element_type=jnp.float32)
        * qk_scale
    )
    visible = jnp.arange(context)[None, :] < row_lengths[:, None]
    cache_scores = jnp.where(visible[None, :, None, :], cache_scores, -1e30)
    fresh_scores = (
        jnp.einsum("srhk,trk->srht", queries, new_lat, preferred_element_type=jnp.float32)
        * qk_scale
    )
    causal = jnp.arange(step_count)[:, None] >= jnp.arange(step_count)[None, :]
    fresh_scores = jnp.where(causal[:, None, None, :], fresh_scores, -1e30)
    scores = jnp.concatenate([cache_scores, fresh_scores], axis=-1)
    weights = jax.nn.softmax(scores, axis=-1).astype(jnp.bfloat16)
    pooled = jnp.einsum(
        "srhp,rpl->srl",
        weights[..., :context],
        owned_cache[..., :latent],
        preferred_element_type=jnp.float32,
    )
    pooled = pooled + jnp.einsum(
        "srht,trl->srl",
        weights[..., context:],
        new_lat[..., :latent],
        preferred_element_type=jnp.float32,
    )
    return pooled.astype(jnp.bfloat16)


def local(
    q_abs,
    new_lat,
    latent_cache,
    lengths,
    owner,
    resid,
    routes,
    w_out,
    norm_gain,
    w_router,
    w_gate,
    w_up,
    w_down,
):
    devices = lax.axis_size("expert")
    device_index = lax.axis_index("expert")
    step_count, row_count, width = resid.shape
    rows = step_count * row_count
    experts_all = w_router.shape[1]
    sharers = devices // experts_all
    chips = devices // 2
    half = chips // 2
    cut = rows // 2
    order = distances(chips)
    sibling = sibling_perm(chips)

    def send(a, perm):
        return lax.ppermute(a, "expert", perm)

    to_right, to_left = shift_perm(chips, 1), shift_perm(chips, -1)

    ordered = latent_cache.at[owner].get(mode="promise_in_bounds", unique_indices=True)
    owned_cache = lax.all_to_all(ordered, "expert", split_axis=0, concat_axis=1, tiled=True)

    mine = resid.reshape(rows, width)
    held = {0: mine}
    for t in range(1, half):
        held[-t] = send(held[-t + 1], to_right)
        held[t] = send(held[t - 1], to_left)
    held[half] = jnp.concatenate(
        [send(held[1 - half][:cut], to_right), send(held[half - 1][cut:], to_left)], axis=0
    )
    resid_own = [held[d] for d in order]
    resid_sib = [send(a, sibling) for a in resid_own]

    row_lengths = lax.dynamic_slice_in_dim(
        lengths.at[owner].get(mode="promise_in_bounds"), device_index * row_count, row_count
    )
    pooled = attention(q_abs, new_lat, owned_cache, row_lengths, w_out.shape[0])

    routed = jnp.any(routes[..., None] == jnp.arange(LANES, dtype=jnp.int32), axis=2)
    packet = jnp.concatenate([pooled, routed.astype(jnp.bfloat16)], axis=2).reshape(rows, -1)
    packets = [packet if d == 0 else send(packet, shift_perm(chips, -d)) for d in order]
    pooled_own = jnp.concatenate(packets, axis=0)
    pooled_sib = send(pooled_own, sibling)

    lane_pick = (jnp.arange(LANES) == device_index // sharers).astype(jnp.float32)[None, :]
    hidden, to_own, to_sib = experts(
        resid_own + resid_sib,
        pooled_own,
        pooled_sib,
        w_out,
        norm_gain[None, :],
        jnp.pad(w_router, ((0, 0), (0, LANES - experts_all))),
        lane_pick,
        w_gate,
        w_up,
        w_down,
    )

    f32 = jnp.float32
    own = dict(zip(order, to_own))
    got = {d: send(a, sibling) for d, a in reversed(list(zip(order, to_sib)))}

    def part(d, lo=0, hi=rows):
        return own[d][lo:hi].astype(f32) + got[d][lo:hi].astype(f32)

    right = send(part(half, 0, cut).astype(jnp.bfloat16), to_right).astype(f32)
    left = send(part(half, cut, rows).astype(jnp.bfloat16), to_left).astype(f32)
    right = jnp.concatenate([right, jnp.zeros((rows - cut, width), f32)], axis=0)
    left = jnp.concatenate([jnp.zeros((cut, width), f32), left], axis=0)
    for t in range(half - 1, 0, -1):
        right = send((part(t) + right).astype(jnp.bfloat16), to_right).astype(f32)
        left = send((part(-t) + left).astype(jnp.bfloat16), to_left).astype(f32)
    mixed = hidden + part(0) + right + left
    return mixed.astype(jnp.bfloat16).reshape(step_count, row_count, width)


def solution(mesh):
    return jax.shard_map(
        local,
        mesh=mesh,
        in_specs=(
            P(None, ("group", "expert"), None),
            P(None, ("group", "expert"), None),
            P("group", "expert", None),
            P("group"),
            P("group"),
            P(None, ("group", "expert"), None),
            P(None, ("group", "expert"), None),
            P(),
            P(),
            P(),
            P("expert", None, None),
            P("expert", None, None),
            P("expert", None, None),
        ),
        out_specs=P(None, ("group", "expert"), None),
        check_vma=False,
    )
```

```python
import jax
import jax.numpy as jnp
from jax import lax
from jax.experimental import pallas as pl
from jax.experimental.pallas import tpu as pltpu
from jax.sharding import PartitionSpec as P

qk_scale = 192.0 ** (-0.5)
LANES = 128


def ring_of(chips):
    return list(range(0, chips, 2)) + list(range(chips - 1, 0, -2))


def shift_perm(chips, by):
    ring = ring_of(chips)
    return [
        (2 * ring[p] + core, 2 * ring[(p + by) % chips] + core)
        for p in range(chips)
        for core in range(2)
    ]


def sibling_perm(chips):
    return [(d, d ^ 1) for d in range(2 * chips)]


def distances(chips):
    half = chips // 2
    order = [0]
    for t in range(1, half):
        order += [t, -t]
    return order + [half]


def tile_of(size, most):
    return max(t for t in range(LANES, min(size, most) + 1, LANES) if size % t == 0)


def norm_kernel(blocks, rows, latent, width, *refs):
    pick = refs[0]
    pooled = refs[1 : 1 + blocks]
    resid = refs[1 + blocks : 1 + 2 * blocks]
    w_out, gain, w_router, x, scale, weight, hidden, joined, ssq, logits = refs[1 + 2 * blocks :]
    step = pl.program_id(0)
    cols = w_out.shape[1]
    total = blocks * rows
    experts_all = w_router.shape[0]
    chunk = min(512, total)

    @pl.when(step == 0)
    def _():
        for b in range(blocks):
            joined[b * rows : (b + 1) * rows, :] = pooled[b][...]
        ssq[...] = jnp.zeros_like(ssq)
        logits[...] = jnp.zeros_like(logits)

    g = gain[...].astype(jnp.float32)
    for c in range(0, total, chunk):
        proj = jnp.dot(
            joined[c : c + chunk, :latent], w_out[...], preferred_element_type=jnp.float32
        )
        for b in range(c // rows, (c + chunk) // rows):
            at = slice(b * rows, (b + 1) * rows)
            h = proj[b * rows - c : (b + 1) * rows - c] + resid[b][...].astype(jnp.float32)
            if b == 0:
                hidden[...] = h
            x[at, :] = (h * g).astype(jnp.bfloat16)
            sq = h * h
            part = sq[:, :LANES]
            for k in range(1, cols // LANES):
                part = part + sq[:, k * LANES : (k + 1) * LANES]
            ssq[at, :] += part
        logits[c : c + chunk, :] += lax.dot_general(
            x[c : c + chunk, :],
            w_router[...],
            (((1,), (1,)), ((), ())),
            preferred_element_type=jnp.float32,
        )

    @pl.when(step == pl.num_programs(0) - 1)
    def _():
        mean = jnp.sum(ssq[...], axis=1, keepdims=True) * (1.0 / width)
        r = lax.rsqrt(mean + 1e-06)
        mask = joined[:, latent : latent + experts_all].astype(jnp.float32)
        affinity = jax.nn.sigmoid(logits[...] * r) * mask
        lane = lax.broadcasted_iota(jnp.int32, affinity.shape, 1)
        mine = jnp.sum(jnp.where(lane == pick[0], affinity, 0.0), axis=1, keepdims=True)
        gate = 2.5 * mine / jnp.sum(affinity, axis=1, keepdims=True)
        scale[...] = jnp.broadcast_to(r, (total, LANES))
        weight[...] = jnp.broadcast_to(gate, (total, LANES))


def mib(amount):
    return (int(amount) // (1 << 20) + 1) << 20


def normalize(pick, packets, resid_blocks, w_out, gain, w_router_t):
    blocks = len(packets)
    rows, width = resid_blocks[0].shape
    latent = w_out.shape[0]
    total = blocks * rows
    cols = tile_of(width, 512)
    packed = packets[0].shape[1]
    experts_all = w_router_t.shape[0]

    def whole(a):
        return pl.BlockSpec(a.shape, lambda i: (0, 0), pipeline_mode=pl.Buffered(1))

    def tiles(height):
        return pl.BlockSpec((height, cols), lambda i: (0, i))

    need = total * (cols * 24 + packed * 4 + 6 * LANES * 4) + 4 * latent * cols
    return pl.pallas_call(
        lambda *refs: norm_kernel(blocks, rows, latent, width, *refs),
        grid=(width // cols,),
        in_specs=[pl.BlockSpec(memory_space=pltpu.SMEM)]
        + [whole(a) for a in packets]
        + [tiles(rows)] * blocks
        + [tiles(latent), tiles(1), tiles(experts_all)],
        out_shape=[
            jax.ShapeDtypeStruct((total, width), jnp.bfloat16),
            jax.ShapeDtypeStruct((total, LANES), jnp.float32),
            jax.ShapeDtypeStruct((total, LANES), jnp.float32),
            jax.ShapeDtypeStruct((rows, width), jnp.float32),
        ],
        out_specs=[
            tiles(total),
            pl.BlockSpec((total, LANES), lambda i: (0, 0)),
            pl.BlockSpec((total, LANES), lambda i: (0, 0)),
            tiles(rows),
        ],
        scratch_shapes=[
            pltpu.VMEM((total, packed), jnp.bfloat16),
            pltpu.VMEM((total, LANES), jnp.float32),
            pltpu.VMEM((total, experts_all), jnp.float32),
        ],
        compiler_params=pltpu.CompilerParams(
            dimension_semantics=("arbitrary",), vmem_limit_bytes=mib(need) + (4 << 20)
        ),
        cost_estimate=pl.CostEstimate(
            flops=2 * total * width * latent,
            bytes_accessed=2 * total * width * 2 + latent * width * 2,
            transcendentals=total,
        ),
        name="normalize",
    )(pick, *packets, *resid_blocks, w_out, gain, w_router_t)


def expert_kernel(rows, gate_steps, x, scale, weight, w_gate, w_up, w_down, *refs):
    outs, act = refs[:-1], refs[-1]
    step = pl.program_id(0)
    total = x.shape[0]
    gate_tile = w_gate.shape[2]
    chunk = min(512, total)
    chunks = total // chunk

    @pl.when(step < gate_steps)
    def _():
        cols = pl.ds(pl.multiple_of(step * gate_tile, gate_tile), gate_tile)
        for i in range(chunks):
            at = pl.ds(i * chunk, chunk)
            xs = x[at, :]
            r = scale[at, :1]
            a = jnp.dot(xs, w_gate[0], preferred_element_type=jnp.float32) * r
            b = jnp.dot(xs, w_up[0], preferred_element_type=jnp.float32) * r
            act[at, cols] = (jax.nn.silu(a) * b * weight[at, :1]).astype(jnp.bfloat16)

    @pl.when(step >= gate_steps)
    def _():
        per = chunk // rows
        for i in range(chunks):
            y = jnp.dot(
                act[i * chunk : (i + 1) * chunk, :], w_down[0], preferred_element_type=jnp.float32
            )
            for b in range(per):
                outs[i * per + b][...] = y[b * rows : (b + 1) * rows].astype(jnp.bfloat16)


def experts(rows, x, scale, weight, wg, wu, wd):
    total, width = x.shape
    blocks = total // rows
    hidden_units = wg.shape[2]
    gate_tile = tile_of(hidden_units, 256)
    gate_steps = hidden_units // gate_tile
    down_tile = tile_of(width, 512)
    down_steps = width // down_tile

    def whole(a):
        return pl.BlockSpec(a.shape, lambda i: (0, 0), pipeline_mode=pl.Buffered(1))

    def gate_at(i):
        return (0, 0, jnp.clip(i, 0, gate_steps - 1))

    def down_at(i):
        return (0, 0, jnp.clip(i - gate_steps, 0, down_steps - 1))

    def out_at(i):
        return (0, jnp.clip(i - gate_steps, 0, down_steps - 1))

    need = (
        total * (2 * width + 2 * hidden_units + 8 * down_tile + 2 * LANES * 4)
        + 8 * width * gate_tile
        + 4 * hidden_units * down_tile
        + min(512, total) * gate_tile * 16
    )
    return pl.pallas_call(
        lambda *refs: expert_kernel(rows, gate_steps, *refs),
        grid=(gate_steps + down_steps,),
        in_specs=[whole(x), whole(scale), whole(weight)]
        + [
            pl.BlockSpec((1, width, gate_tile), gate_at),
            pl.BlockSpec((1, width, gate_tile), gate_at),
            pl.BlockSpec((1, hidden_units, down_tile), down_at),
        ],
        out_shape=[jax.ShapeDtypeStruct((rows, width), jnp.bfloat16)] * blocks,
        out_specs=[pl.BlockSpec((rows, down_tile), out_at)] * blocks,
        scratch_shapes=[pltpu.VMEM((total, hidden_units), jnp.bfloat16)],
        compiler_params=pltpu.CompilerParams(
            dimension_semantics=("arbitrary",), vmem_limit_bytes=mib(need) + (6 << 20)
        ),
        cost_estimate=pl.CostEstimate(
            flops=2 * total * width * 3 * hidden_units,
            bytes_accessed=3 * width * hidden_units * 2 + 2 * total * width * 2,
            transcendentals=total * hidden_units,
        ),
        name="experts",
    )(x, scale, weight, wg, wu, wd)


def attention(q_abs, new_lat, owned_cache, row_lengths, latent):
    step_count, row_count, kv_width = new_lat.shape
    head_count = q_abs.shape[2] // kv_width
    context = owned_cache.shape[1]
    queries = q_abs.reshape(step_count, row_count, head_count, kv_width)
    cache_scores = (
        jnp.einsum("srhk,rpk->srhp", queries, owned_cache, preferred_element_type=jnp.float32)
        * qk_scale
    )
    visible = jnp.arange(context)[None, :] < row_lengths[:, None]
    cache_scores = jnp.where(visible[None, :, None, :], cache_scores, -1e30)
    fresh_scores = (
        jnp.einsum("srhk,trk->srht", queries, new_lat, preferred_element_type=jnp.float32)
        * qk_scale
    )
    causal = jnp.arange(step_count)[:, None] >= jnp.arange(step_count)[None, :]
    fresh_scores = jnp.where(causal[:, None, None, :], fresh_scores, -1e30)
    scores = jnp.concatenate([cache_scores, fresh_scores], axis=-1)
    weights = jax.nn.softmax(scores, axis=-1).astype(jnp.bfloat16)
    pooled = jnp.einsum(
        "srhp,rpl->srl",
        weights[..., :context],
        owned_cache[..., :latent],
        preferred_element_type=jnp.float32,
    )
    pooled = pooled + jnp.einsum(
        "srht,trl->srl",
        weights[..., context:],
        new_lat[..., :latent],
        preferred_element_type=jnp.float32,
    )
    return pooled.astype(jnp.bfloat16)


def local(
    q_abs,
    new_lat,
    latent_cache,
    lengths,
    owner,
    resid,
    routes,
    w_out,
    norm_gain,
    w_router,
    w_gate,
    w_up,
    w_down,
):
    devices = lax.axis_size("expert")
    device_index = lax.axis_index("expert")
    step_count, row_count, width = resid.shape
    rows = step_count * row_count
    experts_all = w_router.shape[1]
    sharers = devices // experts_all
    chips = devices // 2
    half = chips // 2
    cut = rows // 2
    order = distances(chips)
    sibling = sibling_perm(chips)

    def send(a, perm):
        return lax.ppermute(a, "expert", perm)

    to_right, to_left = shift_perm(chips, 1), shift_perm(chips, -1)

    wanted = (owner[:, None] == jnp.arange(owner.shape[0], dtype=jnp.int32)).astype(jnp.bfloat16)
    ordered = jnp.einsum(
        "jr,rpk->jpk", wanted, latent_cache, preferred_element_type=jnp.float32
    ).astype(jnp.bfloat16)
    owned_cache = lax.all_to_all(ordered, "expert", split_axis=0, concat_axis=1, tiled=True)

    mine = resid.reshape(rows, width)
    held = {0: mine}
    for t in range(1, half):
        held[-t] = send(held[-t + 1], to_right)
        held[t] = send(held[t - 1], to_left)
    held[half] = jnp.concatenate(
        [send(held[1 - half][:cut], to_right), send(held[half - 1][cut:], to_left)], axis=0
    )
    resid_own = [held[d] for d in order]
    resid_sib = [send(a, sibling) for a in resid_own]

    row_owner = lax.dynamic_slice_in_dim(owner, device_index * row_count, row_count)
    row_lengths = jnp.sum(
        jnp.where(
            row_owner[:, None] == jnp.arange(owner.shape[0], dtype=jnp.int32), lengths[None, :], 0
        ),
        axis=1,
    )
    routed = jnp.any(routes[..., None] == jnp.arange(LANES, dtype=jnp.int32), axis=2)
    routed = routed.astype(jnp.bfloat16)
    gain = norm_gain[None, :]
    pick = (device_index // sharers).astype(jnp.int32)[None]
    owned_cache, row_lengths, routed, gain, pick = lax.optimization_barrier(
        (owned_cache, row_lengths, routed, gain, pick)
    )
    pooled = attention(q_abs, new_lat, owned_cache, row_lengths, w_out.shape[0])

    packet = jnp.concatenate([pooled, routed], axis=2).reshape(rows, -1)
    packets = {0: packet}
    for t in range(1, half):
        packets[-t], packets[t] = lax.optimization_barrier(
            (send(packets[1 - t], to_right), send(packets[t - 1], to_left))
        )
    packets[half] = send(packets[1 - half], to_right)
    packets_own = [packets[d] for d in order]
    packets_sib = [send(a, sibling) for a in packets_own]

    x, scale, weight, hidden = normalize(
        pick, packets_own + packets_sib, resid_own + resid_sib, w_out, gain, w_router.T
    )
    outs = experts(rows, x, scale, weight, w_gate, w_up, w_down)
    own = dict(zip(order, outs[:chips]))
    to_sib = dict(zip(order, outs[chips:]))

    f32 = jnp.float32
    got = {d: send(to_sib[d], sibling) for d in reversed(order)}

    def part(d, lo=0, hi=rows):
        return own[d][lo:hi].astype(f32) + got[d][lo:hi].astype(f32)

    def both(right, left):
        right, left = lax.optimization_barrier(
            (
                send(right.astype(jnp.bfloat16), to_right),
                send(left.astype(jnp.bfloat16), to_left),
            )
        )
        return right.astype(f32), left.astype(f32)

    right, left = both(part(half, 0, cut), part(half, cut, rows))
    right = jnp.concatenate([right, jnp.zeros((rows - cut, width), f32)], axis=0)
    left = jnp.concatenate([jnp.zeros((cut, width), f32), left], axis=0)
    for t in range(half - 1, 0, -1):
        right, left = both(part(t) + right, part(-t) + left)
    mixed = hidden + part(0) + right + left
    return mixed.astype(jnp.bfloat16).reshape(step_count, row_count, width)


def solution(mesh):
    return jax.shard_map(
        local,
        mesh=mesh,
        in_specs=(
            P(None, ("group", "expert"), None),
            P(None, ("group", "expert"), None),
            P("group", "expert", None),
            P("group"),
            P("group"),
            P(None, ("group", "expert"), None),
            P(None, ("group", "expert"), None),
            P(),
            P(),
            P(),
            P("expert", None, None),
            P("expert", None, None),
            P("expert", None, None),
        ),
        out_specs=P(None, ("group", "expert"), None),
        check_vma=False,
    )
```

```python
import jax
import jax.numpy as jnp
from jax import lax
from jax.experimental import pallas as pl
from jax.experimental.pallas import tpu as pltpu
from jax.sharding import PartitionSpec as P

qk_scale = 192.0 ** (-0.5)
LANES = 128


def ring_of(chips):
    return list(range(0, chips, 2)) + list(range(chips - 1, 0, -2))


def shift_perm(chips, by):
    ring = ring_of(chips)
    return [
        (2 * ring[p] + core, 2 * ring[(p + by) % chips] + core)
        for p in range(chips)
        for core in range(2)
    ]


def sibling_perm(chips):
    return [(d, d ^ 1) for d in range(2 * chips)]


def distances(chips):
    half = chips // 2
    far = [half, half - 1, 1 - half]
    return far, [d for d in range(half - 1) for d in ((d, -d) if d else (0,))]


def tile_of(size, most):
    return max(t for t in range(LANES, min(size, most) + 1, LANES) if size % t == 0)


def scoped(need):
    return max(52 << 20, (int(need) // (1 << 20) + 5) << 20)


def expert_rows(xs, r, gate, w_g, w_u):
    a = jnp.dot(xs, w_g, preferred_element_type=jnp.float32) * r
    b = jnp.dot(xs, w_u, preferred_element_type=jnp.float32) * r
    return (jax.nn.silu(a) * b * gate).astype(jnp.bfloat16)


def front_kernel(far, blocks, rows, latent, width, *refs):
    pick = refs[0]
    pooled = refs[1 : 1 + blocks]
    resid = refs[1 + blocks : 1 + 2 * blocks]
    w_out, gain, w_router, w_gate, w_up, w_down = refs[1 + 2 * blocks : 7 + 2 * blocks]
    x, scale, weight, hidden = refs[7 + 2 * blocks : 11 + 2 * blocks]
    outs = refs[11 + 2 * blocks : 11 + 2 * blocks + far]
    joined, ssq, logits, x_far, act, wg, wu, wd, sems = refs[11 + 2 * blocks + far :]
    step = pl.program_id(0)
    cols = w_out.shape[1]
    tiles = width // cols
    total = blocks * rows
    far_rows = far * rows
    experts_all = w_router.shape[0]
    units = wg.shape[1]
    chunk = min(512, total)

    copies = []
    for k in range(2):
        part = slice(k * units // 2, (k + 1) * units // 2)
        copies.append(pltpu.make_async_copy(w_gate.at[0, :, part], wg.at[:, part], sems.at[2 * k]))
        copies.append(pltpu.make_async_copy(w_up.at[0, :, part], wu.at[:, part], sems.at[2 * k + 1]))
    for k in range(2):
        part = slice(k * width // 2, (k + 1) * width // 2)
        copies.append(pltpu.make_async_copy(w_down.at[0, :, part], wd.at[:, part], sems.at[4 + k]))
    for j, copy in enumerate(copies):
        pl.when(step == min(j, tiles - 1))(copy.start)

    @pl.when(step == 0)
    def _():
        for b in range(blocks):
            joined[b * rows : (b + 1) * rows, :] = pooled[b][...]
        ssq[...] = jnp.zeros_like(ssq)
        logits[...] = jnp.zeros_like(logits)

    @pl.when(step < tiles)
    def _():
        g = gain[...].astype(jnp.float32)
        here = pl.ds(pl.multiple_of(step * cols, cols), cols)
        for c in range(0, total, chunk):
            end = min(c + chunk, total)
            proj = jnp.dot(joined[c:end, :latent], w_out[...], preferred_element_type=jnp.float32)
            for b in range(c // rows, end // rows):
                at = slice(b * rows, (b + 1) * rows)
                h = proj[b * rows - c : (b + 1) * rows - c] + resid[b][...].astype(jnp.float32)
                if b == far:
                    hidden[...] = h
                scaled = (h * g).astype(jnp.bfloat16)
                if b < far:
                    x_far[at, here] = scaled
                else:
                    x[(b - far) * rows : (b - far + 1) * rows, :] = scaled
                sq = h * h
                part = sq[:, :LANES]
                for k in range(1, cols // LANES):
                    part = part + sq[:, k * LANES : (k + 1) * LANES]
                ssq[at, :] += part
        nt = (((1,), (1,)), ((), ()))
        logits[:far_rows, :] += lax.dot_general(
            x_far[:, here], w_router[...], nt, preferred_element_type=jnp.float32
        )
        logits[far_rows:, :] += lax.dot_general(
            x[...], w_router[...], nt, preferred_element_type=jnp.float32
        )

    @pl.when(step == tiles)
    def _():
        mean = jnp.sum(ssq[...], axis=1, keepdims=True) * (1.0 / width)
        r = lax.rsqrt(mean + 1e-06)
        mask = joined[:, latent : latent + experts_all].astype(jnp.float32)
        affinity = jax.nn.sigmoid(logits[...] * r) * mask
        lane = lax.broadcasted_iota(jnp.int32, affinity.shape, 1)
        mine = jnp.sum(jnp.where(lane == pick[0], affinity, 0.0), axis=1, keepdims=True)
        gate = 2.5 * mine / jnp.sum(affinity, axis=1, keepdims=True)
        scale[...] = jnp.broadcast_to(r[far_rows:], (total - far_rows, LANES))
        weight[...] = jnp.broadcast_to(gate[far_rows:], (total - far_rows, LANES))
        for k in range(2):
            part = slice(k * units // 2, (k + 1) * units // 2)
            copies[2 * k].wait()
            copies[2 * k + 1].wait()
            act[:, part] = expert_rows(
                x_far[...], r[:far_rows], gate[:far_rows], wg[:, part], wu[:, part]
            )
        down = tile_of(width // 2, 1024)
        for k in range(2):
            copies[4 + k].wait()
            for c in range(k * width // 2, (k + 1) * width // 2, down):
                y = jnp.dot(act[...], wd[:, c : c + down], preferred_element_type=jnp.float32)
                for b in range(far):
                    outs[b][:, c : c + down] = y[b * rows : (b + 1) * rows].astype(jnp.bfloat16)


def front(far, pick, packets, resid_blocks, w_out, gain, w_router_t, wg, wu, wd):
    blocks = len(packets)
    rows, width = resid_blocks[0].shape
    latent = w_out.shape[0]
    total = blocks * rows
    rest = total - far * rows
    cols = tile_of(width, 512)
    tile_count = width // cols
    packed = packets[0].shape[1]
    experts_all = w_router_t.shape[0]
    units = wg.shape[2]

    def whole(shape):
        return pl.BlockSpec(shape, lambda i: (0, 0), pipeline_mode=pl.Buffered(1))

    def tiles(height):
        return pl.BlockSpec((height, cols), lambda i: (0, jnp.minimum(i, tile_count - 1)))

    in_hbm = pl.BlockSpec(memory_space=pltpu.HBM)
    need = (
        total * (cols * 24 + packed * 4 + 8 * LANES * 4)
        + 4 * latent * cols
        + far * rows * (width * 8 + units * 16)
        + 6 * width * units
    )
    results = pl.pallas_call(
        lambda *refs: front_kernel(far, blocks, rows, latent, width, *refs),
        grid=(tile_count + 1,),
        in_specs=[pl.BlockSpec(memory_space=pltpu.SMEM)]
        + [whole(a.shape) for a in packets]
        + [tiles(rows)] * blocks
        + [tiles(latent), tiles(1), tiles(experts_all)]
        + [in_hbm] * 3,
        out_shape=[
            jax.ShapeDtypeStruct((rest, width), jnp.bfloat16),
            jax.ShapeDtypeStruct((rest, LANES), jnp.float32),
            jax.ShapeDtypeStruct((rest, LANES), jnp.float32),
            jax.ShapeDtypeStruct((rows, width), jnp.float32),
        ]
        + [jax.ShapeDtypeStruct((rows, width), jnp.bfloat16)] * far,
        out_specs=[tiles(rest), whole((rest, LANES)), whole((rest, LANES)), tiles(rows)]
        + [whole((rows, width))] * far,
        scratch_shapes=[
            pltpu.VMEM((total, packed), jnp.bfloat16),
            pltpu.VMEM((total, LANES), jnp.float32),
            pltpu.VMEM((total, experts_all), jnp.float32),
            pltpu.VMEM((far * rows, width), jnp.bfloat16),
            pltpu.VMEM((far * rows, units), jnp.bfloat16),
            pltpu.VMEM((width, units), jnp.bfloat16),
            pltpu.VMEM((width, units), jnp.bfloat16),
            pltpu.VMEM((units, width), jnp.bfloat16),
            pltpu.SemaphoreType.DMA((6,)),
        ],
        compiler_params=pltpu.CompilerParams(
            dimension_semantics=("arbitrary",), vmem_limit_bytes=scoped(need)
        ),
        cost_estimate=pl.CostEstimate(
            flops=2 * total * width * latent + 6 * far * rows * width * units,
            bytes_accessed=2 * total * width * 2 + latent * width * 2 + 6 * width * units,
            transcendentals=total,
        ),
        name="front",
    )(pick, *packets, *resid_blocks, w_out, gain, w_router_t, wg, wu, wd)
    return results[:4], results[4:]


def gate_up_kernel(tile, x, scale, weight, w_gate, w_up, act, wg, wu, sems):
    total = x.shape[0]
    copies = []
    for k in range(wg.shape[1] // tile):
        part = slice(k * tile, (k + 1) * tile)
        copies.append(pltpu.make_async_copy(w_gate.at[0, :, part], wg.at[:, part], sems.at[2 * k]))
        copies.append(pltpu.make_async_copy(w_up.at[0, :, part], wu.at[:, part], sems.at[2 * k + 1]))
    for copy in copies:
        copy.start()
    for k in range(wg.shape[1] // tile):
        part = slice(k * tile, (k + 1) * tile)
        copies[2 * k].wait()
        copies[2 * k + 1].wait()
        for c in range(0, total, 512):
            at = slice(c, min(c + 512, total))
            act[at, part] = expert_rows(
                x[at, :], scale[at, :1], weight[at, :1], wg[:, part], wu[:, part]
            )


def gate_up(x, scale, weight, wg, wu):
    total, width = x.shape
    units = wg.shape[2]
    tile = tile_of(units, 256)
    in_hbm, in_vmem = pl.BlockSpec(memory_space=pltpu.HBM), pl.BlockSpec(memory_space=pltpu.VMEM)
    need = total * (2 * width + 4 * units + 8 * LANES) + 4 * width * units + 512 * tile * 16
    return pl.pallas_call(
        lambda *refs: gate_up_kernel(tile, *refs),
        in_specs=[in_vmem] * 3 + [in_hbm] * 2,
        out_specs=in_vmem,
        out_shape=jax.ShapeDtypeStruct((total, units), jnp.bfloat16),
        scratch_shapes=[
            pltpu.VMEM((width, units), jnp.bfloat16),
            pltpu.VMEM((width, units), jnp.bfloat16),
            pltpu.SemaphoreType.DMA((2 * (units // tile),)),
        ],
        compiler_params=pltpu.CompilerParams(vmem_limit_bytes=scoped(need)),
        cost_estimate=pl.CostEstimate(
            flops=4 * total * width * units,
            bytes_accessed=4 * width * units + 2 * total * width,
            transcendentals=total * units,
        ),
        name="gate_up",
    )(x, scale, weight, wg, wu)


def down_kernel(rows, tile, act, w_down, *refs):
    outs, wd, sems = refs[:-2], refs[-2], refs[-1]
    total = act.shape[0]
    copies = []
    for k in range(wd.shape[1] // tile):
        part = slice(k * tile, (k + 1) * tile)
        copies.append(pltpu.make_async_copy(w_down.at[0, :, part], wd.at[:, part], sems.at[k]))
    for copy in copies:
        copy.start()
    for k in range(wd.shape[1] // tile):
        part = slice(k * tile, (k + 1) * tile)
        copies[k].wait()
        for c in range(0, total, 512):
            end = min(c + 512, total)
            y = jnp.dot(act[c:end, :], wd[:, part], preferred_element_type=jnp.float32)
            for b in range(c // rows, end // rows):
                outs[b][:, part] = y[b * rows - c : (b + 1) * rows - c].astype(jnp.bfloat16)


def down(rows, act, wd):
    total, units = act.shape
    width = wd.shape[2]
    tile = tile_of(width, 512)
    blocks = total // rows
    in_hbm, in_vmem = pl.BlockSpec(memory_space=pltpu.HBM), pl.BlockSpec(memory_space=pltpu.VMEM)
    need = total * (2 * width + 2 * units) + 2 * width * units + 512 * tile * 8
    return pl.pallas_call(
        lambda *refs: down_kernel(rows, tile, *refs),
        in_specs=[in_vmem, in_hbm],
        out_specs=[in_vmem] * blocks,
        out_shape=[jax.ShapeDtypeStruct((rows, width), jnp.bfloat16)] * blocks,
        scratch_shapes=[
            pltpu.VMEM((units, width), jnp.bfloat16),
            pltpu.SemaphoreType.DMA((width // tile,)),
        ],
        compiler_params=pltpu.CompilerParams(vmem_limit_bytes=scoped(need)),
        cost_estimate=pl.CostEstimate(
            flops=2 * total * width * units,
            bytes_accessed=2 * width * units + 2 * total * width,
            transcendentals=0,
        ),
        name="down",
    )(act, wd)


def attention(q_abs, new_lat, owned_cache, row_lengths, latent):
    step_count, row_count, kv_width = new_lat.shape
    head_count = q_abs.shape[2] // kv_width
    context = owned_cache.shape[1]
    queries = q_abs.reshape(step_count, row_count, head_count, kv_width)
    cache_scores = (
        jnp.einsum("srhk,rpk->srhp", queries, owned_cache, preferred_element_type=jnp.float32)
        * qk_scale
    )
    visible = jnp.arange(context)[None, :] < row_lengths[:, None]
    cache_scores = jnp.where(visible[None, :, None, :], cache_scores, -1e30)
    fresh_scores = (
        jnp.einsum("srhk,trk->srht", queries, new_lat, preferred_element_type=jnp.float32)
        * qk_scale
    )
    causal = jnp.arange(step_count)[:, None] >= jnp.arange(step_count)[None, :]
    fresh_scores = jnp.where(causal[:, None, None, :], fresh_scores, -1e30)
    scores = jnp.concatenate([cache_scores, fresh_scores], axis=-1)
    weights = jax.nn.softmax(scores, axis=-1).astype(jnp.bfloat16)
    pooled = jnp.einsum(
        "srhp,rpl->srl",
        weights[..., :context],
        owned_cache[..., :latent],
        preferred_element_type=jnp.float32,
    )
    pooled = pooled + jnp.einsum(
        "srht,trl->srl",
        weights[..., context:],
        new_lat[..., :latent],
        preferred_element_type=jnp.float32,
    )
    return pooled.astype(jnp.bfloat16)


def local(
    q_abs,
    new_lat,
    latent_cache,
    lengths,
    owner,
    resid,
    routes,
    w_out,
    norm_gain,
    w_router,
    w_gate,
    w_up,
    w_down,
):
    devices = lax.axis_size("expert")
    device_index = lax.axis_index("expert")
    step_count, row_count, width = resid.shape
    rows = step_count * row_count
    experts_all = w_router.shape[1]
    sharers = devices // experts_all
    chips = devices // 2
    half = chips // 2
    cut = rows // 2
    far, near = distances(chips)
    hold = lax.optimization_barrier
    sibling = sibling_perm(chips)

    def send(a, perm):
        return lax.ppermute(a, "expert", perm)

    to_right, to_left = shift_perm(chips, 1), shift_perm(chips, -1)

    def around(to_the_right, to_the_left):
        return send(to_the_right, to_right), send(to_the_left, to_left)

    wanted = (owner[:, None] == jnp.arange(owner.shape[0], dtype=jnp.int32)).astype(jnp.bfloat16)
    ordered = jnp.einsum(
        "jr,rpk->jpk", wanted, latent_cache, preferred_element_type=jnp.float32
    ).astype(jnp.bfloat16)
    row_owner = lax.dynamic_slice_in_dim(owner, device_index * row_count, row_count)
    row_lengths = jnp.sum(
        jnp.where(
            row_owner[:, None] == jnp.arange(owner.shape[0], dtype=jnp.int32), lengths[None, :], 0
        ),
        axis=1,
    )
    routed = jnp.any(routes[..., None] == jnp.arange(LANES, dtype=jnp.int32), axis=2)
    routed = routed.astype(jnp.bfloat16)
    gain = norm_gain[None, :]
    pick = (device_index // sharers).astype(jnp.int32)[None]

    mine = resid.reshape(rows, width)
    held, sib = {0: mine}, {}
    held[-1], held[1] = around(mine, mine)
    ordered, held[-1], held[1] = hold((ordered, held[-1], held[1]))
    owned_cache = lax.all_to_all(ordered, "expert", split_axis=0, concat_axis=1, tiled=True)
    held[-2], held[2] = around(held[-1], held[1])
    sib[0] = send(mine, sibling)
    queries, held[-2], held[2], sib[0] = hold((q_abs, held[-2], held[2], sib[0]))
    for t in range(3, half):
        held[-t], held[t] = around(held[1 - t], held[t - 1])
    sib[-1], sib[1] = send(held[-1], sibling), send(held[1], sibling)
    owned_cache, row_lengths, routed, gain, pick, held[1 - half], held[half - 1], sib[-1], sib[1] = hold(
        (owned_cache, row_lengths, routed, gain, pick, held[1 - half], held[half - 1], sib[-1], sib[1])
    )
    last = around(held[1 - half][:cut], held[half - 1][cut:])
    for t in range(2, half):
        sib[-t], sib[t] = send(held[-t], sibling), send(held[t], sibling)
    pooled = attention(queries, new_lat, owned_cache, row_lengths, w_out.shape[0])
    packet = jnp.concatenate([pooled, routed], axis=2).reshape(rows, -1)
    packet, last, sib = hold((packet, last, sib))
    held[half] = jnp.concatenate(last, axis=0)
    sib[half] = send(held[half], sibling)

    packets, packets_sib = {0: packet}, {}
    for t in range(1, half):
        packets[-t], packets[t] = around(packets[1 - t], packets[t - 1])
        for d in {1 - t, t - 1}:
            packets_sib[d] = send(packets[d], sibling)
        packets, packets_sib, sib[half] = hold((packets, packets_sib, sib[half]))
    packets[half] = send(packets[1 - half], to_right)
    for d in (1 - half, half - 1, half):
        packets_sib[d] = send(packets[d], sibling)

    def laid(own, other):
        return [own[d] for d in far] + [other[d] for d in far] + (
            [own[d] for d in near] + [other[d] for d in near]
        )

    (x, scale, weight, hidden), outs = front(
        2 * len(far),
        pick,
        laid(packets, packets_sib),
        laid(held, sib),
        w_out,
        gain,
        w_router.T,
        w_gate,
        w_up,
        w_down,
    )

    f32 = jnp.float32
    own, got = {}, {}

    def swap(dists, results):
        for d, a, b in zip(dists, results[: len(dists)], results[len(dists) :]):
            own[d], got[d] = a, send(b, sibling)

    def part(d, lo=0, hi=rows):
        return own[d][lo:hi].astype(f32) + got[d][lo:hi].astype(f32)

    def both(right, left):
        return around(right.astype(jnp.bfloat16), left.astype(jnp.bfloat16))

    swap(far, outs)
    x, got = hold((x, got))
    right, left = both(part(half, 0, cut), part(half, cut, rows))
    act = gate_up(x, scale, weight, w_gate, w_up)
    act, right, left = hold((act, right, left))
    right = jnp.concatenate([right.astype(f32), jnp.zeros((rows - cut, width), f32)], axis=0)
    left = jnp.concatenate([jnp.zeros((cut, width), f32), left.astype(f32)], axis=0)
    right, left = both(part(half - 1) + right, part(1 - half) + left)
    outs = down(rows, act, w_down)
    outs, right, left = hold((outs, right, left))
    swap(near, outs)
    for t in range(half - 2, 0, -1):
        right, left = hold(both(part(t) + right.astype(f32), part(-t) + left.astype(f32)))
    mixed = hidden + part(0) + right.astype(f32) + left.astype(f32)
    return mixed.astype(jnp.bfloat16).reshape(step_count, row_count, width)


def solution(mesh):
    return jax.shard_map(
        local,
        mesh=mesh,
        in_specs=(
            P(None, ("group", "expert"), None),
            P(None, ("group", "expert"), None),
            P("group", "expert", None),
            P("group"),
            P("group"),
            P(None, ("group", "expert"), None),
            P(None, ("group", "expert"), None),
            P(),
            P(),
            P(),
            P("expert", None, None),
            P("expert", None, None),
            P("expert", None, None),
        ),
        out_specs=P(None, ("group", "expert"), None),
        check_vma=False,
    )
```

```python
import jax
import jax.numpy as jnp
from jax import lax
from jax.experimental import pallas as pl
from jax.experimental.pallas import tpu as pltpu
from jax.sharding import PartitionSpec as P

qk_scale = 192.0 ** (-0.5)
LANES = 128


def ring_of(chips):
    return list(range(0, chips, 2)) + list(range(chips - 1, 0, -2))


def shift_perm(chips, by):
    ring = ring_of(chips)
    return [
        (2 * ring[p] + core, 2 * ring[(p + by) % chips] + core)
        for p in range(chips)
        for core in range(2)
    ]


def sibling_perm(chips):
    return [(d, d ^ 1) for d in range(2 * chips)]


def distances(chips):
    half = chips // 2
    far = [half, half - 1, 1 - half]
    return far, [d for d in range(half - 1) for d in ((d, -d) if d else (0,))]


def gather_steps(chips):
    high = 4 if chips % 4 == 0 else 2
    return high, chips // high


def step_perm(chips, by_high, by_low):
    high, low = gather_steps(chips)
    return [
        (
            2 * (h * low + l) + core,
            2 * ((h - by_high) % high * low + (l - by_low) % low) + core,
        )
        for h in range(high)
        for l in range(low)
        for core in range(2)
    ]


def gathered_place(chips, parts):
    high, low = gather_steps(chips)
    ring = ring_of(chips)
    table = [[] for _ in range(chips)]
    for p, chip in enumerate(ring):
        for part in parts:
            for side in (0, chips):
                for d in part:
                    other = ring[(p + d) % chips]
                    by_high = (other // low - chip // low) % high
                    by_low = (other % low - chip % low) % low
                    table[chip].append(side + by_low * high + by_high)
    return table


def tile_of(size, most):
    return max(t for t in range(LANES, min(size, most) + 1, LANES) if size % t == 0)


def scoped(need):
    return max(52 << 20, (int(need) // (1 << 20) + 5) << 20)


def expert_rows(xs, r, gate, w_gu):
    both = jnp.dot(xs, w_gu, preferred_element_type=jnp.float32) * r
    half = both.shape[1] // 2
    return (jax.nn.silu(both[:, :half]) * both[:, half:] * gate).astype(jnp.bfloat16)


def stream_gate_up(tile, w_gate, w_up, wgu, sems):
    copies = []
    for k in range(w_gate.shape[2] // tile):
        part, at = slice(k * tile, (k + 1) * tile), 2 * k * tile
        copies.append(
            pltpu.make_async_copy(w_gate.at[0, :, part], wgu.at[:, at : at + tile], sems.at[2 * k])
        )
        copies.append(
            pltpu.make_async_copy(
                w_up.at[0, :, part], wgu.at[:, at + tile : at + 2 * tile], sems.at[2 * k + 1]
            )
        )
    return copies


def front_kernel(far, blocks, rows, latent, width, tile, down_tile, *refs):
    scalars = refs[0]
    pooled = refs[1:5]
    resid = refs[5 : 5 + blocks]
    w_out, gain, w_router, w_gate, w_up, w_down = refs[5 + blocks : 11 + blocks]
    x, scale, weight, hidden = refs[11 + blocks : 15 + blocks]
    outs = refs[15 + blocks : 15 + blocks + far]
    raw, joined, ssq, logits, x_far, act, wgu, wd, sems = refs[15 + blocks + far :]
    step = pl.program_id(0)
    cols = w_out.shape[1]
    tiles = width // cols
    total = blocks * rows
    far_rows = far * rows
    experts_all = w_router.shape[0]
    units = act.shape[1]
    chunk = min(512, total)

    copies = stream_gate_up(tile, w_gate, w_up, wgu, sems)
    gate_copies = len(copies)
    for k in range(width // down_tile):
        part = slice(k * down_tile, (k + 1) * down_tile)
        copies.append(
            pltpu.make_async_copy(w_down.at[0, :, part], wd.at[:, part], sems.at[gate_copies + k])
        )
    for j, copy in enumerate(copies):
        pl.when(step == min(j // 2, tiles - 1))(copy.start)

    @pl.when(step == 0)
    def _():
        start = 0
        for piece in pooled:
            raw[start : start + piece.shape[0], :] = piece[...]
            start += piece.shape[0]
        for b in range(blocks):
            place = pl.ds(pl.multiple_of(scalars[1 + b] * rows, rows), rows)
            joined[b * rows : (b + 1) * rows, :] = raw[place, :]
        ssq[...] = jnp.zeros_like(ssq)
        logits[...] = jnp.zeros_like(logits)

    @pl.when(step < tiles)
    def _():
        g = gain[...].astype(jnp.float32)
        here = pl.ds(pl.multiple_of(step * cols, cols), cols)
        for c in range(0, total, chunk):
            end = min(c + chunk, total)
            proj = jnp.dot(joined[c:end, :latent], w_out[...], preferred_element_type=jnp.float32)
            for b in range(c // rows, end // rows):
                at = slice(b * rows, (b + 1) * rows)
                h = proj[b * rows - c : (b + 1) * rows - c] + resid[b][...].astype(jnp.float32)
                if b == far:
                    hidden[...] = h
                scaled = (h * g).astype(jnp.bfloat16)
                if b < far:
                    x_far[at, here] = scaled
                else:
                    x[(b - far) * rows : (b - far + 1) * rows, :] = scaled
                sq = h * h
                part = sq[:, :LANES]
                for k in range(1, cols // LANES):
                    part = part + sq[:, k * LANES : (k + 1) * LANES]
                ssq[at, :] += part
        nt = (((1,), (1,)), ((), ()))
        logits[:far_rows, :] += lax.dot_general(
            x_far[:, here], w_router[...], nt, preferred_element_type=jnp.float32
        )
        logits[far_rows:, :] += lax.dot_general(
            x[...], w_router[...], nt, preferred_element_type=jnp.float32
        )

    @pl.when(step == tiles)
    def _():
        mean = jnp.sum(ssq[...], axis=1, keepdims=True) * (1.0 / width)
        r = lax.rsqrt(mean + 1e-06)
        mask = joined[:, latent : latent + experts_all].astype(jnp.float32)
        affinity = jax.nn.sigmoid(logits[...] * r) * mask
        lane = lax.broadcasted_iota(jnp.int32, affinity.shape, 1)
        mine = jnp.sum(jnp.where(lane == scalars[0], affinity, 0.0), axis=1, keepdims=True)
        gate = 2.5 * mine / jnp.sum(affinity, axis=1, keepdims=True)
        scale[...] = jnp.broadcast_to(r[far_rows:], (total - far_rows, LANES))
        weight[...] = jnp.broadcast_to(gate[far_rows:], (total - far_rows, LANES))
        for k in range(units // tile):
            copies[2 * k].wait()
            copies[2 * k + 1].wait()
            act[:, k * tile : (k + 1) * tile] = expert_rows(
                x_far[...], r[:far_rows], gate[:far_rows], wgu[:, 2 * k * tile : 2 * (k + 1) * tile]
            )
        for k in range(width // down_tile):
            copies[gate_copies + k].wait()
            part = slice(k * down_tile, (k + 1) * down_tile)
            y = jnp.dot(act[...], wd[:, part], preferred_element_type=jnp.float32)
            for b in range(far):
                outs[b][:, part] = y[b * rows : (b + 1) * rows].astype(jnp.bfloat16)


def front(far, scalars, pooled, resid_blocks, w_out, gain, w_router_t, wg, wu, wd):
    blocks = len(resid_blocks)
    rows, width = resid_blocks[0].shape
    latent = w_out.shape[0]
    total = blocks * rows
    rest = total - far * rows
    cols = tile_of(width, 512)
    tile_count = width // cols
    packed = pooled[0].shape[1]
    experts_all = w_router_t.shape[0]
    units = wg.shape[2]
    tile = tile_of(units, 256)
    down_tile = tile_of(width, 512)

    def whole(shape):
        return pl.BlockSpec(shape, lambda i: (0, 0), pipeline_mode=pl.Buffered(1))

    def tiles(height):
        return pl.BlockSpec((height, cols), lambda i: (0, jnp.minimum(i, tile_count - 1)))

    in_hbm = pl.BlockSpec(memory_space=pltpu.HBM)
    need = (
        total * (cols * 24 + packed * 6 + 8 * LANES * 4)
        + 4 * latent * cols
        + far * rows * (width * 8 + units * 16)
        + 6 * width * units
    )
    results = pl.pallas_call(
        lambda *refs: front_kernel(far, blocks, rows, latent, width, tile, down_tile, *refs),
        grid=(tile_count + 1,),
        in_specs=[pl.BlockSpec(memory_space=pltpu.SMEM)]
        + [whole(a.shape) for a in pooled]
        + [tiles(rows)] * blocks
        + [tiles(latent), tiles(1), tiles(experts_all)]
        + [in_hbm] * 3,
        out_shape=[
            jax.ShapeDtypeStruct((rest, width), jnp.bfloat16),
            jax.ShapeDtypeStruct((rest, LANES), jnp.float32),
            jax.ShapeDtypeStruct((rest, LANES), jnp.float32),
            jax.ShapeDtypeStruct((rows, width), jnp.float32),
        ]
        + [jax.ShapeDtypeStruct((rows, width), jnp.bfloat16)] * far,
        out_specs=[tiles(rest), whole((rest, LANES)), whole((rest, LANES)), tiles(rows)]
        + [whole((rows, width))] * far,
        scratch_shapes=[
            pltpu.VMEM((total, packed), jnp.bfloat16),
            pltpu.VMEM((total, packed), jnp.bfloat16),
            pltpu.VMEM((total, LANES), jnp.float32),
            pltpu.VMEM((total, experts_all), jnp.float32),
            pltpu.VMEM((far * rows, width), jnp.bfloat16),
            pltpu.VMEM((far * rows, units), jnp.bfloat16),
            pltpu.VMEM((width, 2 * units), jnp.bfloat16),
            pltpu.VMEM((units, width), jnp.bfloat16),
            pltpu.SemaphoreType.DMA((2 * (units // tile) + width // down_tile,)),
        ],
        compiler_params=pltpu.CompilerParams(
            dimension_semantics=("arbitrary",), vmem_limit_bytes=scoped(need)
        ),
        cost_estimate=pl.CostEstimate(
            flops=2 * total * width * latent + 6 * far * rows * width * units,
            bytes_accessed=2 * total * width * 2 + latent * width * 2 + 6 * width * units,
            transcendentals=total,
        ),
        name="front",
    )(scalars, *pooled, *resid_blocks, w_out, gain, w_router_t, wg, wu, wd)
    return results[:4], results[4:]


def gate_up_kernel(tile, x, scale, weight, w_gate, w_up, act, wgu, sems):
    total = x.shape[0]
    copies = stream_gate_up(tile, w_gate, w_up, wgu, sems)
    for copy in copies:
        copy.start()
    for k in range(w_gate.shape[2] // tile):
        copies[2 * k].wait()
        copies[2 * k + 1].wait()
        for c in range(0, total, 512):
            at = slice(c, min(c + 512, total))
            act[at, k * tile : (k + 1) * tile] = expert_rows(
                x[at, :], scale[at, :1], weight[at, :1], wgu[:, 2 * k * tile : 2 * (k + 1) * tile]
            )


def gate_up(x, scale, weight, wg, wu):
    total, width = x.shape
    units = wg.shape[2]
    tile = tile_of(units, 256)
    in_hbm, in_vmem = pl.BlockSpec(memory_space=pltpu.HBM), pl.BlockSpec(memory_space=pltpu.VMEM)
    need = total * (2 * width + 4 * units + 8 * LANES) + 4 * width * units + 512 * tile * 16
    return pl.pallas_call(
        lambda *refs: gate_up_kernel(tile, *refs),
        in_specs=[in_vmem] * 3 + [in_hbm] * 2,
        out_specs=in_vmem,
        out_shape=jax.ShapeDtypeStruct((total, units), jnp.bfloat16),
        scratch_shapes=[
            pltpu.VMEM((width, 2 * units), jnp.bfloat16),
            pltpu.SemaphoreType.DMA((2 * (units // tile),)),
        ],
        compiler_params=pltpu.CompilerParams(vmem_limit_bytes=scoped(need)),
        cost_estimate=pl.CostEstimate(
            flops=4 * total * width * units,
            bytes_accessed=4 * width * units + 2 * total * width,
            transcendentals=total * units,
        ),
        name="gate_up",
    )(x, scale, weight, wg, wu)


def down_kernel(rows, tile, act, w_down, *refs):
    outs, wd, sems = refs[:-2], refs[-2], refs[-1]
    total = act.shape[0]
    copies = []
    for k in range(wd.shape[1] // tile):
        part = slice(k * tile, (k + 1) * tile)
        copies.append(pltpu.make_async_copy(w_down.at[0, :, part], wd.at[:, part], sems.at[k]))
    for copy in copies:
        copy.start()
    for k in range(wd.shape[1] // tile):
        part = slice(k * tile, (k + 1) * tile)
        copies[k].wait()
        for c in range(0, total, 512):
            end = min(c + 512, total)
            y = jnp.dot(act[c:end, :], wd[:, part], preferred_element_type=jnp.float32)
            for b in range(c // rows, end // rows):
                outs[b][:, part] = y[b * rows - c : (b + 1) * rows - c].astype(jnp.bfloat16)


def down(rows, act, wd):
    total, units = act.shape
    width = wd.shape[2]
    tile = tile_of(width, 512)
    blocks = total // rows
    in_hbm, in_vmem = pl.BlockSpec(memory_space=pltpu.HBM), pl.BlockSpec(memory_space=pltpu.VMEM)
    need = total * (2 * width + 2 * units) + 2 * width * units + 512 * tile * 8
    return pl.pallas_call(
        lambda *refs: down_kernel(rows, tile, *refs),
        in_specs=[in_vmem, in_hbm],
        out_specs=[in_vmem] * blocks,
        out_shape=[jax.ShapeDtypeStruct((rows, width), jnp.bfloat16)] * blocks,
        scratch_shapes=[
            pltpu.VMEM((units, width), jnp.bfloat16),
            pltpu.SemaphoreType.DMA((width // tile,)),
        ],
        compiler_params=pltpu.CompilerParams(vmem_limit_bytes=scoped(need)),
        cost_estimate=pl.CostEstimate(
            flops=2 * total * width * units,
            bytes_accessed=2 * width * units + 2 * total * width,
            transcendentals=0,
        ),
        name="down",
    )(act, wd)


def attention(queries, new_lat, owned_cache, row_lengths, latent):
    step_count, row_count, kv_width = new_lat.shape
    context = owned_cache.shape[1]
    cache_scores = (
        jnp.einsum("srhk,rpk->srhp", queries, owned_cache, preferred_element_type=jnp.float32)
        * qk_scale
    )
    visible = jnp.arange(context)[None, :] < row_lengths[:, None]
    cache_scores = jnp.where(visible[None, :, None, :], cache_scores, -1e30)
    fresh_scores = (
        jnp.einsum("srhk,trk->srht", queries, new_lat, preferred_element_type=jnp.float32)
        * qk_scale
    )
    causal = jnp.arange(step_count)[:, None] >= jnp.arange(step_count)[None, :]
    fresh_scores = jnp.where(causal[:, None, None, :], fresh_scores, -1e30)
    scores = jnp.concatenate([cache_scores, fresh_scores], axis=-1)
    weights = jax.nn.softmax(scores, axis=-1).astype(jnp.bfloat16)
    pooled = jnp.einsum(
        "srhp,rpl->srl",
        weights[..., :context],
        owned_cache[..., :latent],
        preferred_element_type=jnp.float32,
    )
    pooled = pooled + jnp.einsum(
        "srht,trl->srl",
        weights[..., context:],
        new_lat[..., :latent],
        preferred_element_type=jnp.float32,
    )
    return pooled.astype(jnp.bfloat16)


def local(
    q_abs,
    new_lat,
    latent_cache,
    lengths,
    owner,
    resid,
    routes,
    w_out,
    norm_gain,
    w_router,
    w_gate,
    w_up,
    w_down,
):
    devices = lax.axis_size("expert")
    device_index = lax.axis_index("expert")
    step_count, row_count, width = resid.shape
    rows = step_count * row_count
    experts_all = w_router.shape[1]
    sharers = devices // experts_all
    chips = devices // 2
    half = chips // 2
    cut = rows // 2
    far, near = distances(chips)
    hold = lax.optimization_barrier
    sibling = sibling_perm(chips)

    def send(a, perm):
        return lax.ppermute(a, "expert", perm)

    to_right, to_left = shift_perm(chips, 1), shift_perm(chips, -1)

    def around(to_the_right, to_the_left):
        return send(to_the_right, to_right), send(to_the_left, to_left)

    wanted = (owner[:, None] == jnp.arange(owner.shape[0], dtype=jnp.int32)).astype(jnp.bfloat16)
    ordered = jnp.einsum(
        "jr,rpk->jpk", wanted, latent_cache, preferred_element_type=jnp.float32
    ).astype(jnp.bfloat16)
    owned_cache = lax.all_to_all(ordered, "expert", split_axis=0, concat_axis=1, tiled=True)

    mine = resid.reshape(rows, width)
    held, sib = {0: mine}, {}
    held[-1], held[1] = around(mine, mine)
    owner, lengths, routes, norm_gain, new_lat, held[-1], held[1] = hold(
        (owner, lengths, routes, norm_gain, new_lat, held[-1], held[1])
    )
    held[-2], held[2] = around(held[-1], held[1])
    sib[0] = send(mine, sibling)
    row_owner = lax.dynamic_slice_in_dim(owner, device_index * row_count, row_count)
    row_lengths = jnp.sum(
        jnp.where(
            row_owner[:, None] == jnp.arange(owner.shape[0], dtype=jnp.int32), lengths[None, :], 0
        ),
        axis=1,
    )
    routed = jnp.any(routes[..., None] == jnp.arange(LANES, dtype=jnp.int32), axis=2)
    routed = routed.astype(jnp.bfloat16)
    gain = norm_gain[None, :]
    scalars = jnp.array(
        [
            [device // sharers] + places
            for chip, places in enumerate(gathered_place(chips, (far, near)))
            for device in (2 * chip, 2 * chip + 1)
        ],
        jnp.int32,
    )[device_index]
    queries = q_abs.reshape(step_count, row_count, -1, new_lat.shape[2])
    queries, row_lengths, routed, gain, scalars, held[-2], held[2], sib[0] = hold(
        (queries, row_lengths, routed, gain, scalars, held[-2], held[2], sib[0])
    )
    for t in range(3, half):
        held[-t], held[t] = around(held[1 - t], held[t - 1])
    sib[-1], sib[1] = send(held[-1], sibling), send(held[1], sibling)
    pooled = attention(queries, new_lat, owned_cache, row_lengths, w_out.shape[0])
    packet = jnp.concatenate([pooled, routed], axis=2).reshape(rows, -1)
    packet, held, sib = hold((packet, held, sib))

    last = around(held[1 - half][:cut], held[half - 1][cut:])
    for t in range(2, half):
        sib[-t], sib[t] = send(held[-t], sibling), send(held[t], sibling)
    high, low = gather_steps(chips)
    along = hold([send(packet, step_perm(chips, i, 0)) for i in range(1, high)])
    along = jnp.concatenate([packet] + along, axis=0)
    across = [send(along, step_perm(chips, 0, i)) for i in range(1, low)]
    along_sib = send(along, sibling)
    across, last, sib = hold((across, last, sib))
    held[half] = jnp.concatenate(last, axis=0)
    sib[half] = send(held[half], sibling)
    across = across[0] if low == 2 else jnp.concatenate(across, axis=0)
    packets = [along, across, along_sib, send(across, sibling)]

    def laid(own, other):
        return [own[d] for d in far] + [other[d] for d in far] + (
            [own[d] for d in near] + [other[d] for d in near]
        )

    (x, scale, weight, hidden), outs = front(
        2 * len(far),
        scalars,
        packets,
        laid(held, sib),
        w_out,
        gain,
        w_router.T,
        w_gate,
        w_up,
        w_down,
    )

    f32 = jnp.float32
    own, got = {}, {}

    def swap(dists, results):
        for d, a, b in zip(dists, results[: len(dists)], results[len(dists) :]):
            own[d], got[d] = a, send(b, sibling)

    def part(d, lo=0, hi=rows):
        return own[d][lo:hi].astype(f32) + got[d][lo:hi].astype(f32)

    def both(right, left):
        return around(right.astype(jnp.bfloat16), left.astype(jnp.bfloat16))

    swap(far, outs)
    x, got = hold((x, got))
    right, left = both(part(half, 0, cut), part(half, cut, rows))
    act = gate_up(x, scale, weight, w_gate, w_up)
    act, right, left = hold((act, right, left))
    right = jnp.concatenate([right.astype(f32), jnp.zeros((rows - cut, width), f32)], axis=0)
    left = jnp.concatenate([jnp.zeros((cut, width), f32), left.astype(f32)], axis=0)
    right, left = both(part(half - 1) + right, part(1 - half) + left)
    outs = down(rows, act, w_down)
    outs, right, left = hold((outs, right, left))
    swap(near, outs)
    for t in range(half - 2, 0, -1):
        right, left = hold(both(part(t) + right.astype(f32), part(-t) + left.astype(f32)))
    mixed = hidden + part(0) + right.astype(f32) + left.astype(f32)
    return mixed.astype(jnp.bfloat16).reshape(step_count, row_count, width)


def solution(mesh):
    return jax.shard_map(
        local,
        mesh=mesh,
        in_specs=(
            P(None, ("group", "expert"), None),
            P(None, ("group", "expert"), None),
            P("group", "expert", None),
            P("group"),
            P("group"),
            P(None, ("group", "expert"), None),
            P(None, ("group", "expert"), None),
            P(),
            P(),
            P(),
            P("expert", None, None),
            P("expert", None, None),
            P("expert", None, None),
        ),
        out_specs=P(None, ("group", "expert"), None),
        check_vma=False,
    )
```

```python
import jax
import jax.numpy as jnp
from jax import lax
from jax.experimental import pallas as pl
from jax.experimental.pallas import tpu as pltpu
from jax.sharding import PartitionSpec as P

qk_scale = 192.0 ** (-0.5)
LANES = 128


def ring_of(chips):
    return list(range(0, chips, 2)) + list(range(chips - 1, 0, -2))


def shift_perm(chips, by):
    ring = ring_of(chips)
    return [
        (2 * ring[p] + core, 2 * ring[(p + by) % chips] + core)
        for p in range(chips)
        for core in range(2)
    ]


def sibling_perm(chips):
    return [(d, d ^ 1) for d in range(2 * chips)]


def distances(chips):
    half = chips // 2
    return [0] + [d for t in range(1, half) for d in (t, -t)] + [half]


def gather_steps(chips):
    high = 4 if chips % 4 == 0 else 2
    return high, chips // high


def step_perm(chips, by_high, by_low):
    high, low = gather_steps(chips)
    return [
        (
            2 * (h * low + l) + core,
            2 * ((h - by_high) % high * low + (l - by_low) % low) + core,
        )
        for h in range(high)
        for l in range(low)
        for core in range(2)
    ]


def gathered_place(chips):
    high, low = gather_steps(chips)
    ring = ring_of(chips)
    table = [[] for _ in range(chips)]
    for p, chip in enumerate(ring):
        for side in (0, chips):
            for d in distances(chips):
                other = ring[(p + d) % chips]
                by_high = (other // low - chip // low) % high
                by_low = (other % low - chip % low) % low
                table[chip].append(side + by_low * high + by_high)
    return table


def tile_of(size, most):
    return max(t for t in range(LANES, min(size, most) + 1, LANES) if size % t == 0)


def scoped(need):
    return max(52 << 20, (int(need) // (1 << 20) + 5) << 20)


def expert_kernel(blocks, rows, latent, width, gate_tile, *refs):
    scalars = refs[0]
    pooled = refs[1:5]
    resid = refs[5 : 5 + blocks]
    w_out, gain, w_router, w_gate, w_up, w_down = refs[5 + blocks : 11 + blocks]
    hidden = refs[11 + blocks]
    outs = refs[12 + blocks : 12 + 2 * blocks]
    raw, joined, ssq, logits, scale, weight, x, act, wg, wu, wd, sems = refs[12 + 2 * blocks :]
    step = pl.program_id(0)
    cols = w_out.shape[1]
    tiles = width // cols
    total = blocks * rows
    experts_all = w_router.shape[0]
    units = act.shape[1]
    chunk = min(512, total)
    gate_steps = units // gate_tile

    def rows_of(source, target, pieces, first):
        height = source.shape[1] // pieces
        return [
            pltpu.make_async_copy(
                source.at[0, k * height : (k + 1) * height, :],
                target.at[k * height : (k + 1) * height, :],
                sems.at[first + k],
            )
            for k in range(pieces)
        ]

    gates, ups, downs = rows_of(w_gate, wg, 4, 0), rows_of(w_up, wu, 4, 4), rows_of(w_down, wd, 4, 8)
    queue = [c for pair in zip(gates, ups) for c in pair] + downs
    for j, copy in enumerate(queue):
        pl.when(step == min(j // 2, tiles - 1))(copy.start)

    @pl.when(step == 0)
    def _():
        start = 0
        for piece in pooled:
            raw[start : start + piece.shape[0], :] = piece[...]
            start += piece.shape[0]
        for b in range(blocks):
            place = pl.ds(pl.multiple_of(scalars[1 + b] * rows, rows), rows)
            joined[b * rows : (b + 1) * rows, :] = raw[place, :]
        ssq[...] = jnp.zeros_like(ssq)
        logits[...] = jnp.zeros_like(logits)

    @pl.when(step < tiles)
    def _():
        g = gain[...].astype(jnp.float32)
        here = pl.ds(pl.multiple_of(step * cols, cols), cols)
        for c in range(0, total, chunk):
            end = min(c + chunk, total)
            proj = jnp.dot(joined[c:end, :latent], w_out[...], preferred_element_type=jnp.float32)
            for b in range(c // rows, end // rows):
                at = slice(b * rows, (b + 1) * rows)
                h = proj[b * rows - c : (b + 1) * rows - c] + resid[b][...].astype(jnp.float32)
                if b == 0:
                    hidden[...] = h
                x[at, here] = (h * g).astype(jnp.bfloat16)
                sq = h * h
                part = sq[:, :LANES]
                for k in range(1, cols // LANES):
                    part = part + sq[:, k * LANES : (k + 1) * LANES]
                ssq[at, :] += part
            logits[c:end, :] += lax.dot_general(
                x[c:end, here],
                w_router[...],
                (((1,), (1,)), ((), ())),
                preferred_element_type=jnp.float32,
            )

    @pl.when(step == tiles)
    def _():
        mean = jnp.sum(ssq[...], axis=1, keepdims=True) * (1.0 / width)
        r = lax.rsqrt(mean + 1e-06)
        mask = joined[:, latent : latent + experts_all].astype(jnp.float32)
        affinity = jax.nn.sigmoid(logits[...] * r) * mask
        lane = lax.broadcasted_iota(jnp.int32, affinity.shape, 1)
        mine = jnp.sum(jnp.where(lane == scalars[0], affinity, 0.0), axis=1, keepdims=True)
        gate = 2.5 * mine / jnp.sum(affinity, axis=1, keepdims=True)
        scale[...] = jnp.broadcast_to(r, scale.shape)
        weight[...] = jnp.broadcast_to(gate, weight.shape)
        for copy in gates + ups:
            copy.wait()

    @pl.when((step >= tiles) & (step < tiles + gate_steps))
    def _():
        part = pl.ds(pl.multiple_of((step - tiles) * gate_tile, gate_tile), gate_tile)
        for c in range(0, total, chunk):
            at = slice(c, min(c + chunk, total))
            r = scale[at, :1]
            a = jnp.dot(x[at, :], wg[:, part], preferred_element_type=jnp.float32) * r
            b = jnp.dot(x[at, :], wu[:, part], preferred_element_type=jnp.float32) * r
            act[at, part] = (jax.nn.silu(a) * b * weight[at, :1]).astype(jnp.bfloat16)

    @pl.when(step == tiles + gate_steps)
    def _():
        for copy in downs:
            copy.wait()

    @pl.when(step >= tiles + gate_steps)
    def _():
        here = pl.ds(pl.multiple_of((step - tiles - gate_steps) * cols, cols), cols)
        for c in range(0, total, chunk):
            end = min(c + chunk, total)
            y = jnp.dot(act[c:end, :], wd[:, here], preferred_element_type=jnp.float32)
            for b in range(c // rows, end // rows):
                outs[b][...] = y[b * rows - c : (b + 1) * rows - c].astype(jnp.bfloat16)


def experts(scalars, pooled, resid_blocks, w_out, gain, w_router_t, wg, wu, wd):
    blocks = len(resid_blocks)
    rows, width = resid_blocks[0].shape
    latent = w_out.shape[0]
    total = blocks * rows
    cols = tile_of(width, 512)
    tile_count = width // cols
    packed = pooled[0].shape[1]
    experts_all = w_router_t.shape[0]
    units = wg.shape[2]
    gate_tile = tile_of(units, 512)
    gate_steps = units // gate_tile

    def whole(shape):
        return pl.BlockSpec(shape, lambda i: (0, 0), pipeline_mode=pl.Buffered(1))

    def tiles(height):
        return pl.BlockSpec((height, cols), lambda i: (0, jnp.minimum(i, tile_count - 1)))

    out_tiles = pl.BlockSpec(
        (rows, cols), lambda i: (0, jnp.clip(i - tile_count - gate_steps, 0, tile_count - 1))
    )
    in_hbm = pl.BlockSpec(memory_space=pltpu.HBM)
    need = total * (2 * width + 2 * units + cols * 20 + packed * 6 + 8 * LANES * 4)
    need = need + 4 * latent * cols + 6 * width * units
    results = pl.pallas_call(
        lambda *refs: expert_kernel(blocks, rows, latent, width, gate_tile, *refs),
        grid=(2 * tile_count + gate_steps,),
        in_specs=[pl.BlockSpec(memory_space=pltpu.SMEM)]
        + [whole(a.shape) for a in pooled]
        + [tiles(rows)] * blocks
        + [tiles(latent), tiles(1), tiles(experts_all)]
        + [in_hbm] * 3,
        out_shape=[jax.ShapeDtypeStruct((rows, width), jnp.float32)]
        + [jax.ShapeDtypeStruct((rows, width), jnp.bfloat16)] * blocks,
        out_specs=[tiles(rows)] + [out_tiles] * blocks,
        scratch_shapes=[
            pltpu.VMEM((total, packed), jnp.bfloat16),
            pltpu.VMEM((total, packed), jnp.bfloat16),
            pltpu.VMEM((total, LANES), jnp.float32),
            pltpu.VMEM((total, experts_all), jnp.float32),
            pltpu.VMEM((total, LANES), jnp.float32),
            pltpu.VMEM((total, LANES), jnp.float32),
            pltpu.VMEM((total, width), jnp.bfloat16),
            pltpu.VMEM((total, units), jnp.bfloat16),
            pltpu.VMEM((width, units), jnp.bfloat16),
            pltpu.VMEM((width, units), jnp.bfloat16),
            pltpu.VMEM((units, width), jnp.bfloat16),
            pltpu.SemaphoreType.DMA((12,)),
        ],
        compiler_params=pltpu.CompilerParams(
            dimension_semantics=("arbitrary",), vmem_limit_bytes=scoped(need)
        ),
        cost_estimate=pl.CostEstimate(
            flops=2 * total * width * (latent + 3 * units),
            bytes_accessed=2 * total * width * 2 + latent * width * 2 + 6 * width * units,
            transcendentals=total * units,
        ),
        name="experts",
    )(scalars, *pooled, *resid_blocks, w_out, gain, w_router_t, wg, wu, wd)
    return results[0], results[1 : 1 + blocks // 2], results[1 + blocks // 2 :]


def attention(queries, new_lat, owned_cache, row_lengths, latent):
    step_count, row_count, kv_width = new_lat.shape
    context = owned_cache.shape[1]
    cache_scores = (
        jnp.einsum("srhk,rpk->srhp", queries, owned_cache, preferred_element_type=jnp.float32)
        * qk_scale
    )
    visible = jnp.arange(context)[None, :] < row_lengths[:, None]
    cache_scores = jnp.where(visible[None, :, None, :], cache_scores, -1e30)
    fresh_scores = (
        jnp.einsum("srhk,trk->srht", queries, new_lat, preferred_element_type=jnp.float32)
        * qk_scale
    )
    causal = jnp.arange(step_count)[:, None] >= jnp.arange(step_count)[None, :]
    fresh_scores = jnp.where(causal[:, None, None, :], fresh_scores, -1e30)
    scores = jnp.concatenate([cache_scores, fresh_scores], axis=-1)
    weights = jax.nn.softmax(scores, axis=-1).astype(jnp.bfloat16)
    pooled = jnp.einsum(
        "srhp,rpl->srl",
        weights[..., :context],
        owned_cache[..., :latent],
        preferred_element_type=jnp.float32,
    )
    pooled = pooled + jnp.einsum(
        "srht,trl->srl",
        weights[..., context:],
        new_lat[..., :latent],
        preferred_element_type=jnp.float32,
    )
    return pooled.astype(jnp.bfloat16)


def local(
    q_abs,
    new_lat,
    latent_cache,
    lengths,
    owner,
    resid,
    routes,
    w_out,
    norm_gain,
    w_router,
    w_gate,
    w_up,
    w_down,
):
    devices = lax.axis_size("expert")
    device_index = lax.axis_index("expert")
    step_count, row_count, width = resid.shape
    rows = step_count * row_count
    experts_all = w_router.shape[1]
    sharers = devices // experts_all
    chips = devices // 2
    half = chips // 2
    cut = rows // 2
    order = distances(chips)
    hold = lax.optimization_barrier
    sibling = sibling_perm(chips)

    def send(a, perm):
        return lax.ppermute(a, "expert", perm)

    to_right, to_left = shift_perm(chips, 1), shift_perm(chips, -1)

    def around(to_the_right, to_the_left):
        return send(to_the_right, to_right), send(to_the_left, to_left)

    wanted = (owner[:, None] == jnp.arange(owner.shape[0], dtype=jnp.int32)).astype(jnp.bfloat16)
    ordered = jnp.einsum(
        "jr,rpk->jpk", wanted, latent_cache, preferred_element_type=jnp.float32
    ).astype(jnp.bfloat16)
    owned_cache = lax.all_to_all(ordered, "expert", split_axis=0, concat_axis=1, tiled=True)

    mine = resid.reshape(rows, width)
    held, sib = {0: mine}, {}
    held[-1], held[1] = around(mine, mine)
    owner, lengths, routes, norm_gain, new_lat, held[-1], held[1] = hold(
        (owner, lengths, routes, norm_gain, new_lat, held[-1], held[1])
    )
    held[-2], held[2] = around(held[-1], held[1])
    sib[0] = send(mine, sibling)
    row_owner = lax.dynamic_slice_in_dim(owner, device_index * row_count, row_count)
    row_lengths = jnp.sum(
        jnp.where(
            row_owner[:, None] == jnp.arange(owner.shape[0], dtype=jnp.int32), lengths[None, :], 0
        ),
        axis=1,
    )
    routed = jnp.any(routes[..., None] == jnp.arange(LANES, dtype=jnp.int32), axis=2)
    routed = routed.astype(jnp.bfloat16)
    gain = norm_gain[None, :]
    scalars = jnp.array(
        [
            [device // sharers] + places
            for chip, places in enumerate(gathered_place(chips))
            for device in (2 * chip, 2 * chip + 1)
        ],
        jnp.int32,
    )[device_index]
    queries = q_abs.reshape(step_count, row_count, -1, new_lat.shape[2])
    owned_cache, queries, row_lengths, routed, gain, scalars, held[-2], held[2], sib[0] = hold(
        (owned_cache, queries, row_lengths, routed, gain, scalars, held[-2], held[2], sib[0])
    )
    for t in range(3, half):
        held[-t], held[t] = around(held[1 - t], held[t - 1])
    sib[-1], sib[1] = send(held[-1], sibling), send(held[1], sibling)
    pooled = attention(queries, new_lat, owned_cache, row_lengths, w_out.shape[0])
    packet = jnp.concatenate([pooled, routed], axis=2).reshape(rows, -1)
    packet, held, sib = hold((packet, held, sib))

    last = around(held[1 - half][:cut], held[half - 1][cut:])
    for t in range(2, half):
        sib[-t], sib[t] = send(held[-t], sibling), send(held[t], sibling)
    high, low = gather_steps(chips)
    along, last = hold(([send(packet, step_perm(chips, i, 0)) for i in range(1, high)], last))
    along = jnp.concatenate([packet] + along, axis=0)
    across = [send(along, step_perm(chips, 0, i)) for i in range(1, low)]
    held[half] = jnp.concatenate(last, axis=0)
    sib[half] = send(held[half], sibling)
    across, sib = hold((across, sib))
    across = across[0] if low == 2 else jnp.concatenate(across, axis=0)

    hidden, to_own, to_sib = experts(
        scalars,
        [along, across, send(along, sibling), send(across, sibling)],
        [held[d] for d in order] + [sib[d] for d in order],
        w_out,
        gain,
        w_router.T,
        w_gate,
        w_up,
        w_down,
    )

    f32 = jnp.float32
    own = dict(zip(order, to_own))
    got = {d: send(a, sibling) for d, a in reversed(list(zip(order, to_sib)))}
    halves = (slice(0, cut), slice(cut, rows))

    parts = {}
    for d in reversed(order):
        sums = [own[d][h].astype(f32) + got[d][h].astype(f32) for h in halves]
        parts[d] = hold(sums) if d else sums

    right, left = {}, {}
    for t, which in [(half, 0)] + [(t, w) for t in range(half - 1, 0, -1) for w in (1, 0)]:
        other = 1 - which
        to_r, to_l = parts[t][which], parts[-t if t < half else t][other]
        if which in right:
            to_r, to_l = to_r + right[which].astype(f32), to_l + left[other].astype(f32)
        right[which], left[other] = hold(around(to_r.astype(jnp.bfloat16), to_l.astype(jnp.bfloat16)))
    mixed = [
        hidden[halves[w]] + parts[0][w] + right[w].astype(f32) + left[w].astype(f32) for w in range(2)
    ]
    mixed = jnp.concatenate(mixed, axis=0)
    return mixed.astype(jnp.bfloat16).reshape(step_count, row_count, width)


def solution(mesh):
    return jax.shard_map(
        local,
        mesh=mesh,
        in_specs=(
            P(None, ("group", "expert"), None),
            P(None, ("group", "expert"), None),
            P("group", "expert", None),
            P("group"),
            P("group"),
            P(None, ("group", "expert"), None),
            P(None, ("group", "expert"), None),
            P(),
            P(),
            P(),
            P("expert", None, None),
            P("expert", None, None),
            P("expert", None, None),
        ),
        out_specs=P(None, ("group", "expert"), None),
        check_vma=False,
    )
```

```python
import jax
import jax.numpy as jnp
from jax import lax
from jax.experimental import pallas as pl
from jax.experimental.pallas import tpu as pltpu
from jax.sharding import PartitionSpec as P

qk_scale = 192.0 ** (-0.5)
LANES = 128


def ring_of(chips):
    return list(range(0, chips, 2)) + list(range(chips - 1, 0, -2))


def shift_perm(chips, by):
    ring = ring_of(chips)
    return [
        (2 * ring[p] + core, 2 * ring[(p + by) % chips] + core)
        for p in range(chips)
        for core in range(2)
    ]


def sibling_perm(chips):
    return [(d, d ^ 1) for d in range(2 * chips)]


def distances(chips):
    half = chips // 2
    far = [half, half - 1, 1 - half]
    return far, [0] + [d for t in range(1, half - 1) for d in (t, -t)]


def gather_steps(chips):
    high = 4 if chips % 4 == 0 else 2
    return high, chips // high


def step_perm(chips, by_high, by_low):
    high, low = gather_steps(chips)
    return [
        (
            2 * (h * low + l) + core,
            2 * ((h - by_high) % high * low + (l - by_low) % low) + core,
        )
        for h in range(high)
        for l in range(low)
        for core in range(2)
    ]


def gathered_place(chips):
    high, low = gather_steps(chips)
    ring = ring_of(chips)
    table = [[] for _ in range(chips)]
    for p, chip in enumerate(ring):
        for part in distances(chips):
            for side in (0, chips):
                for d in part:
                    other = ring[(p + d) % chips]
                    by_high = (other // low - chip // low) % high
                    by_low = (other % low - chip % low) % low
                    table[chip].append(side + by_low * high + by_high)
    return table


def tile_of(size, most):
    return max(t for t in range(LANES, min(size, most) + 1, LANES) if size % t == 0)


def norm_kernel(far, blocks, rows, latent, width, *refs):
    scalars = refs[0]
    pooled = refs[1:5]
    resid = refs[5 : 5 + blocks]
    w_out, gain, w_router, x_far, x_near = refs[5 + blocks : 10 + blocks]
    scale, weight, hidden, raw, joined, ssq, logits = refs[10 + blocks :]
    step = pl.program_id(0)
    cols = w_out.shape[1]
    total = blocks * rows
    far_rows = far * rows
    experts_all = w_router.shape[0]
    chunk = min(512, total)

    @pl.when(step == 0)
    def _():
        start = 0
        for piece in pooled:
            raw[start : start + piece.shape[0], :] = piece[...]
            start += piece.shape[0]
        for b in range(blocks):
            place = pl.ds(pl.multiple_of(scalars[1 + b] * rows, rows), rows)
            joined[b * rows : (b + 1) * rows, :] = raw[place, :]
        ssq[...] = jnp.zeros_like(ssq)
        logits[...] = jnp.zeros_like(logits)

    g = gain[...].astype(jnp.float32)
    for c in range(0, total, chunk):
        end = min(c + chunk, total)
        proj = jnp.dot(joined[c:end, :latent], w_out[...], preferred_element_type=jnp.float32)
        for b in range(c // rows, end // rows):
            at = slice(b * rows, (b + 1) * rows)
            h = proj[b * rows - c : (b + 1) * rows - c] + resid[b][...].astype(jnp.float32)
            if b == far:
                hidden[...] = h
            scaled = (h * g).astype(jnp.bfloat16)
            if b < far:
                x_far[at, :] = scaled
            else:
                x_near[(b - far) * rows : (b - far + 1) * rows, :] = scaled
            sq = h * h
            part = sq[:, :LANES]
            for k in range(1, cols // LANES):
                part = part + sq[:, k * LANES : (k + 1) * LANES]
            ssq[at, :] += part
    nt = (((1,), (1,)), ((), ()))
    for x, at in ((x_far, slice(0, far_rows)), (x_near, slice(far_rows, total))):
        logits[at, :] += lax.dot_general(
            x[...], w_router[...], nt, preferred_element_type=jnp.float32
        )

    @pl.when(step == pl.num_programs(0) - 1)
    def _():
        mean = jnp.sum(ssq[...], axis=1, keepdims=True) * (1.0 / width)
        r = lax.rsqrt(mean + 1e-06)
        mask = joined[:, latent : latent + experts_all].astype(jnp.float32)
        affinity = jax.nn.sigmoid(logits[...] * r) * mask
        lane = lax.broadcasted_iota(jnp.int32, affinity.shape, 1)
        mine = jnp.sum(jnp.where(lane == scalars[0], affinity, 0.0), axis=1, keepdims=True)
        gate = 2.5 * mine / jnp.sum(affinity, axis=1, keepdims=True)
        scale[...] = jnp.broadcast_to(r, scale.shape)
        weight[...] = jnp.broadcast_to(gate, weight.shape)


def normalize(far, scalars, pooled, resid_blocks, w_out, gain, w_router_t):
    blocks = len(resid_blocks)
    rows, width = resid_blocks[0].shape
    latent = w_out.shape[0]
    total = blocks * rows
    cols = tile_of(width, 512)
    packed = pooled[0].shape[1]
    experts_all = w_router_t.shape[0]

    def whole(shape):
        return pl.BlockSpec(shape, lambda i: (0, 0), pipeline_mode=pl.Buffered(1))

    def tiles(height):
        return pl.BlockSpec((height, cols), lambda i: (0, i))

    need = total * (cols * 24 + packed * 6 + 8 * LANES * 4) + 4 * latent * cols
    return pl.pallas_call(
        lambda *refs: norm_kernel(far, blocks, rows, latent, width, *refs),
        grid=(width // cols,),
        in_specs=[pl.BlockSpec(memory_space=pltpu.SMEM)]
        + [whole(a.shape) for a in pooled]
        + [tiles(rows)] * blocks
        + [tiles(latent), tiles(1), tiles(experts_all)],
        out_shape=[
            jax.ShapeDtypeStruct((far * rows, width), jnp.bfloat16),
            jax.ShapeDtypeStruct((total - far * rows, width), jnp.bfloat16),
            jax.ShapeDtypeStruct((total, LANES), jnp.float32),
            jax.ShapeDtypeStruct((total, LANES), jnp.float32),
            jax.ShapeDtypeStruct((rows, width), jnp.float32),
        ],
        out_specs=[tiles(far * rows), tiles(total - far * rows)]
        + [whole((total, LANES)), whole((total, LANES)), tiles(rows)],
        scratch_shapes=[
            pltpu.VMEM((total, packed), jnp.bfloat16),
            pltpu.VMEM((total, packed), jnp.bfloat16),
            pltpu.VMEM((total, LANES), jnp.float32),
            pltpu.VMEM((total, experts_all), jnp.float32),
        ],
        compiler_params=pltpu.CompilerParams(
            dimension_semantics=("arbitrary",), vmem_limit_bytes=(int(need) // (1 << 20) + 6) << 20
        ),
        cost_estimate=pl.CostEstimate(
            flops=2 * total * width * latent,
            bytes_accessed=2 * total * width * 2 + latent * width * 2,
            transcendentals=total,
        ),
        name="normalize",
    )(scalars, *pooled, *resid_blocks, w_out, gain, w_router_t)


def attention(queries, new_lat, owned_cache, row_lengths, latent):
    step_count, row_count, kv_width = new_lat.shape
    context = owned_cache.shape[1]
    cache_scores = (
        jnp.einsum("srhk,rpk->srhp", queries, owned_cache, preferred_element_type=jnp.float32)
        * qk_scale
    )
    visible = jnp.arange(context)[None, :] < row_lengths[:, None]
    cache_scores = jnp.where(visible[None, :, None, :], cache_scores, -1e30)
    fresh_scores = (
        jnp.einsum("srhk,trk->srht", queries, new_lat, preferred_element_type=jnp.float32)
        * qk_scale
    )
    causal = jnp.arange(step_count)[:, None] >= jnp.arange(step_count)[None, :]
    fresh_scores = jnp.where(causal[:, None, None, :], fresh_scores, -1e30)
    scores = jnp.concatenate([cache_scores, fresh_scores], axis=-1)
    weights = jax.nn.softmax(scores, axis=-1).astype(jnp.bfloat16)
    pooled = jnp.einsum(
        "srhp,rpl->srl",
        weights[..., :context],
        owned_cache[..., :latent],
        preferred_element_type=jnp.float32,
    )
    pooled = pooled + jnp.einsum(
        "srht,trl->srl",
        weights[..., context:],
        new_lat[..., :latent],
        preferred_element_type=jnp.float32,
    )
    return pooled.astype(jnp.bfloat16)


def local(
    q_abs,
    new_lat,
    latent_cache,
    lengths,
    owner,
    resid,
    routes,
    w_out,
    norm_gain,
    w_router,
    w_gate,
    w_up,
    w_down,
):
    devices = lax.axis_size("expert")
    device_index = lax.axis_index("expert")
    step_count, row_count, width = resid.shape
    rows = step_count * row_count
    experts_all = w_router.shape[1]
    sharers = devices // experts_all
    chips = devices // 2
    half = chips // 2
    cut = rows // 2
    far, near = distances(chips)
    hold = lax.optimization_barrier
    sibling = sibling_perm(chips)

    def send(a, perm):
        return lax.ppermute(a, "expert", perm)

    to_right, to_left = shift_perm(chips, 1), shift_perm(chips, -1)

    def around(to_the_right, to_the_left):
        return send(to_the_right, to_right), send(to_the_left, to_left)

    wanted = (owner[:, None] == jnp.arange(owner.shape[0], dtype=jnp.int32)).astype(jnp.bfloat16)
    ordered = jnp.einsum(
        "jr,rpk->jpk", wanted, latent_cache, preferred_element_type=jnp.float32
    ).astype(jnp.bfloat16)
    owned_cache = lax.all_to_all(ordered, "expert", split_axis=0, concat_axis=1, tiled=True)

    mine = resid.reshape(rows, width)
    held, sib = {0: mine}, {}
    held[-1], held[1] = around(mine, mine)
    owner, lengths, routes, norm_gain, new_lat, held[-1], held[1] = hold(
        (owner, lengths, routes, norm_gain, new_lat, held[-1], held[1])
    )
    held[-2], held[2] = around(held[-1], held[1])
    sib[0] = send(mine, sibling)
    row_owner = lax.dynamic_slice_in_dim(owner, device_index * row_count, row_count)
    row_lengths = jnp.sum(
        jnp.where(
            row_owner[:, None] == jnp.arange(owner.shape[0], dtype=jnp.int32), lengths[None, :], 0
        ),
        axis=1,
    )
    routed = jnp.any(routes[..., None] == jnp.arange(LANES, dtype=jnp.int32), axis=2)
    routed = routed.astype(jnp.bfloat16)
    gain = norm_gain[None, :]
    scalars = jnp.array(
        [
            [device // sharers] + places
            for chip, places in enumerate(gathered_place(chips))
            for device in (2 * chip, 2 * chip + 1)
        ],
        jnp.int32,
    )[device_index]
    queries = q_abs.reshape(step_count, row_count, -1, new_lat.shape[2])
    owned_cache, queries, row_lengths, routed, gain, scalars = hold(
        (owned_cache, queries, row_lengths, routed, gain, scalars)
    )
    pooled = attention(queries, new_lat, owned_cache, row_lengths, w_out.shape[0])
    packet = jnp.concatenate([pooled, routed], axis=2).reshape(rows, -1)
    packet, held[-2], held[2], sib[0] = hold((packet, held[-2], held[2], sib[0]))

    high, low = gather_steps(chips)
    along = [send(packet, step_perm(chips, i, 0)) for i in range(1, high)]
    for t in range(3, half):
        held[-t], held[t] = around(held[1 - t], held[t - 1])
    sib[-1], sib[1] = send(held[-1], sibling), send(held[1], sibling)
    along, held, sib = hold((along, held, sib))
    along = jnp.concatenate([packet] + along, axis=0)
    across = [send(along, step_perm(chips, 0, i)) for i in range(1, low)]
    last = around(held[1 - half][:cut], held[half - 1][cut:])
    for t in range(2, half):
        sib[-t], sib[t] = send(held[-t], sibling), send(held[t], sibling)
    along_sib = send(along, sibling)
    across, last, sib, along_sib = hold((across, last, sib, along_sib))
    held[half] = jnp.concatenate(last, axis=0)
    sib[half] = send(held[half], sibling)
    across = across[0] if low == 2 else jnp.concatenate(across, axis=0)

    f32 = jnp.float32
    x_far, x_near, scale, weight, hidden = normalize(
        2 * len(far),
        scalars,
        [along, across, along_sib, send(across, sibling)],
        [a[d] for part in (far, near) for a in (held, sib) for d in part],
        w_out,
        gain,
        w_router.T,
    )

    def product(a, w):
        return jnp.dot(a, w[0], preferred_element_type=f32)

    def activate(a, b, at):
        r, g = scale[at, :1], weight[at, :1]
        return (jax.nn.silu(a * r) * (b * r) * g).astype(jnp.bfloat16)

    cut_at = x_far.shape[0]
    sums = {}

    def swap(dists, y):
        return y, send(y[len(dists) * rows :], sibling)

    def add_up(dists, y, received):
        for i, d in enumerate(dists):
            at = slice(i * rows, (i + 1) * rows)
            sums[d] = y[at].astype(f32) + received[at].astype(f32)

    def both(right, left):
        return around(right.astype(jnp.bfloat16), left.astype(jnp.bfloat16))

    act = hold(activate(product(x_far, w_gate), product(x_far, w_up), slice(0, cut_at)))
    y, received = swap(far, product(act, w_down).astype(jnp.bfloat16))
    gated, y, received = hold((product(x_near, w_gate), y, received))
    add_up(far, y, received)
    right, left = both(sums[half][:cut], sums[half][cut:])
    act = activate(gated, product(x_near, w_up), slice(cut_at, None))
    act, right, left = hold((act, right, left))
    right = jnp.concatenate([right.astype(f32), jnp.zeros((rows - cut, width), f32)], axis=0)
    left = jnp.concatenate([jnp.zeros((cut, width), f32), left.astype(f32)], axis=0)
    right, left = both(sums[half - 1] + right, sums[1 - half] + left)
    y, received = swap(near, product(act, w_down).astype(jnp.bfloat16))
    y, received, right, left = hold((y, received, right, left))
    add_up(near, y, received)
    for t in range(half - 2, 0, -1):
        right, left = hold(both(sums[t] + right.astype(f32), sums[-t] + left.astype(f32)))
    mixed = hidden + sums[0] + right.astype(f32) + left.astype(f32)
    return mixed.astype(jnp.bfloat16).reshape(step_count, row_count, width)


def solution(mesh):
    return jax.shard_map(
        local,
        mesh=mesh,
        in_specs=(
            P(None, ("group", "expert"), None),
            P(None, ("group", "expert"), None),
            P("group", "expert", None),
            P("group"),
            P("group"),
            P(None, ("group", "expert"), None),
            P(None, ("group", "expert"), None),
            P(),
            P(),
            P(),
            P("expert", None, None),
            P("expert", None, None),
            P("expert", None, None),
        ),
        out_specs=P(None, ("group", "expert"), None),
        check_vma=False,
    )
```

```python
import jax
import jax.numpy as jnp
from jax import lax
from jax.experimental import pallas as pl
from jax.experimental.pallas import tpu as pltpu
from jax.sharding import PartitionSpec as P

qk_scale = 192.0 ** (-0.5)
LANES = 128


def ring_of(chips):
    return list(range(0, chips, 2)) + list(range(chips - 1, 0, -2))


def shift_perm(chips, by):
    ring = ring_of(chips)
    return [
        (2 * ring[p] + core, 2 * ring[(p + by) % chips] + core)
        for p in range(chips)
        for core in range(2)
    ]


def sibling_perm(chips):
    return [(d, d ^ 1) for d in range(2 * chips)]


def distances(chips):
    half = chips // 2
    far = [half, half - 1, 1 - half]
    return far, [0] + [d for t in range(1, half - 1) for d in (t, -t)]


def gather_steps(chips):
    high = 4 if chips % 4 == 0 else 2
    return high, chips // high


def step_perm(chips, by_high, by_low):
    high, low = gather_steps(chips)
    return [
        (
            2 * (h * low + l) + core,
            2 * ((h - by_high) % high * low + (l - by_low) % low) + core,
        )
        for h in range(high)
        for l in range(low)
        for core in range(2)
    ]


def gathered_place(chips):
    high, low = gather_steps(chips)
    ring = ring_of(chips)
    table = [[] for _ in range(chips)]
    for p, chip in enumerate(ring):
        for part in distances(chips):
            for side in (0, chips):
                for d in part:
                    other = ring[(p + d) % chips]
                    by_high = (other // low - chip // low) % high
                    by_low = (other % low - chip % low) % low
                    table[chip].append(side + by_low * high + by_high)
    return table


def tile_of(size, most):
    return max(t for t in range(LANES, min(size, most) + 1, LANES) if size % t == 0)


def norm_kernel(first, blocks, rows, latent, width, with_hidden, *refs):
    scalars = refs[0]
    pooled = refs[1:5]
    resid = refs[5 : 5 + blocks]
    w_out, gain, w_router, x, scale, weight = refs[5 + blocks : 11 + blocks]
    hidden = refs[11 + blocks] if with_hidden else None
    raw, joined, ssq, logits = refs[-4:]
    step = pl.program_id(0)
    cols = w_out.shape[1]
    total = blocks * rows
    experts_all = w_router.shape[0]
    chunk = min(512, total)

    @pl.when(step == 0)
    def _():
        start = 0
        for piece in pooled:
            raw[start : start + piece.shape[0], :] = piece[...]
            start += piece.shape[0]
        for b in range(blocks):
            place = pl.ds(pl.multiple_of(scalars[first + b] * rows, rows), rows)
            joined[b * rows : (b + 1) * rows, :] = raw[place, :]
        ssq[...] = jnp.zeros_like(ssq)
        logits[...] = jnp.zeros_like(logits)

    g = gain[...].astype(jnp.float32)
    for c in range(0, total, chunk):
        end = min(c + chunk, total)
        proj = jnp.dot(joined[c:end, :latent], w_out[...], preferred_element_type=jnp.float32)
        for b in range(c // rows, end // rows):
            at = slice(b * rows, (b + 1) * rows)
            h = proj[b * rows - c : (b + 1) * rows - c] + resid[b][...].astype(jnp.float32)
            if with_hidden and b == 0:
                hidden[...] = h
            x[at, :] = (h * g).astype(jnp.bfloat16)
            sq = h * h
            part = sq[:, :LANES]
            for k in range(1, cols // LANES):
                part = part + sq[:, k * LANES : (k + 1) * LANES]
            ssq[at, :] += part
    logits[...] += lax.dot_general(
        x[...], w_router[...], (((1,), (1,)), ((), ())), preferred_element_type=jnp.float32
    )

    @pl.when(step == pl.num_programs(0) - 1)
    def _():
        mean = jnp.sum(ssq[...], axis=1, keepdims=True) * (1.0 / width)
        r = lax.rsqrt(mean + 1e-06)
        mask = joined[:, latent : latent + experts_all].astype(jnp.float32)
        affinity = jax.nn.sigmoid(logits[...] * r) * mask
        lane = lax.broadcasted_iota(jnp.int32, affinity.shape, 1)
        mine = jnp.sum(jnp.where(lane == scalars[0], affinity, 0.0), axis=1, keepdims=True)
        gate = 2.5 * mine / jnp.sum(affinity, axis=1, keepdims=True)
        scale[...] = jnp.broadcast_to(r, scale.shape)
        weight[...] = jnp.broadcast_to(gate, weight.shape)


def normalize(first, with_hidden, scalars, pooled, w_out, gain, w_router_t, resid_blocks):
    blocks = len(resid_blocks)
    rows, width = resid_blocks[0].shape
    latent = w_out.shape[0]
    total = blocks * rows
    cols = tile_of(width, 512)
    packed = pooled[0].shape[1]
    experts_all = w_router_t.shape[0]

    def whole(shape):
        return pl.BlockSpec(shape, lambda i: (0, 0), pipeline_mode=pl.Buffered(1))

    def tiles(height):
        return pl.BlockSpec((height, cols), lambda i: (0, i))

    gathered = sum(a.shape[0] for a in pooled)
    need = total * (cols * 24 + packed * 2 + 8 * LANES * 4) + gathered * packed * 4 + 4 * latent * cols
    return pl.pallas_call(
        lambda *refs: norm_kernel(first, blocks, rows, latent, width, with_hidden, *refs),
        grid=(width // cols,),
        in_specs=[pl.BlockSpec(memory_space=pltpu.SMEM)]
        + [whole(a.shape) for a in pooled]
        + [tiles(rows)] * blocks
        + [tiles(latent), tiles(1), tiles(experts_all)],
        out_shape=[
            jax.ShapeDtypeStruct((total, width), jnp.bfloat16),
            jax.ShapeDtypeStruct((total, LANES), jnp.float32),
            jax.ShapeDtypeStruct((total, LANES), jnp.float32),
        ]
        + [jax.ShapeDtypeStruct((rows, width), jnp.float32)] * with_hidden,
        out_specs=[tiles(total), whole((total, LANES)), whole((total, LANES))]
        + [tiles(rows)] * with_hidden,
        scratch_shapes=[
            pltpu.VMEM((gathered, packed), jnp.bfloat16),
            pltpu.VMEM((total, packed), jnp.bfloat16),
            pltpu.VMEM((total, LANES), jnp.float32),
            pltpu.VMEM((total, experts_all), jnp.float32),
        ],
        compiler_params=pltpu.CompilerParams(
            dimension_semantics=("arbitrary",), vmem_limit_bytes=(int(need) // (1 << 20) + 6) << 20
        ),
        cost_estimate=pl.CostEstimate(
            flops=2 * total * width * latent,
            bytes_accessed=2 * total * width * 2 + latent * width * 2,
            transcendentals=total,
        ),
        name="normalize",
    )(scalars, *pooled, *resid_blocks, w_out, gain, w_router_t)


def attention_kernel(context, latent, q, cache, fresh, lengths, routes, packet, keys_a, keys_b, total):
    step = pl.program_id(0)
    rows, kv_width = q.shape[1], cache.shape[1]
    wide = keys_a.shape[1]
    pairs = q.shape[2] // (2 * kv_width)
    keys = keys_a.shape[0]
    cached = cache.shape[0]

    @pl.when(step == 0)
    def _():
        keys_a[...] = jnp.zeros_like(keys_a)
        keys_a[:cached, :kv_width] = cache[...]
        keys_a[cached:, :kv_width] = fresh[...]
        shifted = pltpu.roll(keys_a[...].astype(jnp.float32), wide - kv_width, 1)
        keys_b[...] = shifted.astype(jnp.bfloat16)

    row = lax.broadcasted_iota(jnp.int32, (rows, keys), 0)
    key = lax.broadcasted_iota(jnp.int32, (rows, keys), 1)
    place = key // rows
    seen = (place < lengths[:, :1]) & (place < context)
    seen = seen | ((place >= context) & (place <= context + step))
    bias = jnp.where(seen & (key % rows == row), 0.0, -1e30)
    summed = jnp.zeros((rows, keys), jnp.float32)
    for held, first in ((keys_a, 0), (keys_b, 2 * kv_width - wide)):
        heads = [
            q[0, :, 2 * kv_width * i + first : 2 * kv_width * i + first + wide].astype(jnp.float32)
            for i in range(pairs)
        ]
        scores = lax.dot_general(
            jnp.concatenate(heads, axis=0).astype(jnp.bfloat16),
            held[...],
            (((1,), (1,)), ((), ())),
            preferred_element_type=jnp.float32,
        )
        scores = (scores * qk_scale).reshape(pairs, rows, keys) + bias[None]
        e = jnp.exp(scores - jnp.max(scores, axis=2, keepdims=True))
        weights = e / jnp.sum(e, axis=2, keepdims=True)
        summed = summed + jnp.sum(weights.astype(jnp.bfloat16).astype(jnp.float32), axis=0)
    total[pl.ds(pl.multiple_of(step * rows, rows), rows), :] = summed

    @pl.when(step == pl.num_programs(0) - 1)
    def _():
        high = total[...].astype(jnp.bfloat16)
        low = (total[...] - high.astype(jnp.float32)).astype(jnp.bfloat16)
        values = keys_a[:, :latent]
        pooled = jnp.dot(high, values, preferred_element_type=jnp.float32)
        pooled = pooled + jnp.dot(low, values, preferred_element_type=jnp.float32)
        packet[:, :latent] = pooled.astype(jnp.bfloat16)
        lane = lax.broadcasted_iota(jnp.int32, (packet.shape[0], LANES), 1)
        routed = jnp.zeros(lane.shape, jnp.float32)
        for k in range(routes.shape[1]):
            routed = jnp.where(routes[:, k : k + 1] == lane, 1.0, routed)
        packet[:, latent:] = routed.astype(jnp.bfloat16)


def attention(q_abs, cache, fresh, lengths, routes, context, latent):
    steps, rows, _ = q_abs.shape
    kv_width = cache.shape[1]
    keys = cache.shape[0] + fresh.shape[0]
    wide = -(-kv_width // LANES) * LANES

    def whole(a):
        return pl.BlockSpec(a.shape, lambda i: (0, 0), pipeline_mode=pl.Buffered(1))

    heads = q_abs.shape[2] // kv_width
    return pl.pallas_call(
        lambda *refs: attention_kernel(context, latent, *refs),
        grid=(steps,),
        in_specs=[pl.BlockSpec((1, rows, q_abs.shape[2]), lambda i: (i, 0, 0))]
        + [whole(a) for a in (cache, fresh, lengths, routes)],
        out_shape=jax.ShapeDtypeStruct((steps * rows, latent + LANES), jnp.bfloat16),
        out_specs=pl.BlockSpec((steps * rows, latent + LANES), lambda i: (0, 0)),
        scratch_shapes=[
            pltpu.VMEM((keys, wide), jnp.bfloat16),
            pltpu.VMEM((keys, wide), jnp.bfloat16),
            pltpu.VMEM((steps * rows, keys), jnp.float32),
        ],
        compiler_params=pltpu.CompilerParams(
            dimension_semantics=("arbitrary",), vmem_limit_bytes=24 << 20
        ),
        cost_estimate=pl.CostEstimate(
            flops=2 * steps * rows * heads * wide * keys,
            bytes_accessed=2 * q_abs.size,
            transcendentals=steps * rows * heads * keys,
        ),
        name="attention",
    )(q_abs, cache, fresh, lengths, routes)


def local(
    q_abs,
    new_lat,
    latent_cache,
    lengths,
    owner,
    resid,
    routes,
    w_out,
    norm_gain,
    w_router,
    w_gate,
    w_up,
    w_down,
):
    devices = lax.axis_size("expert")
    device_index = lax.axis_index("expert")
    step_count, row_count, width = resid.shape
    rows = step_count * row_count
    experts_all = w_router.shape[1]
    sharers = devices // experts_all
    chips = devices // 2
    half = chips // 2
    cut = rows // 2
    far, near = distances(chips)
    hold = lax.optimization_barrier
    sibling = sibling_perm(chips)

    def send(a, perm):
        return lax.ppermute(a, "expert", perm)

    to_right, to_left = shift_perm(chips, 1), shift_perm(chips, -1)

    def around(to_the_right, to_the_left):
        return send(to_the_right, to_right), send(to_the_left, to_left)

    positions, kv_width = latent_cache.shape[1:]
    wanted = (owner[:, None] == jnp.arange(owner.shape[0], dtype=jnp.int32)).astype(jnp.bfloat16)
    ordered = jnp.einsum(
        "jr,rpk->pjk", wanted, latent_cache, preferred_element_type=jnp.float32
    ).astype(jnp.bfloat16)
    ordered = ordered.reshape(positions, devices, row_count, kv_width).swapaxes(0, 1)
    owned = lax.all_to_all(ordered, "expert", split_axis=0, concat_axis=0, tiled=True)

    mine = resid.reshape(rows, width)
    held, sib = {0: mine}, {}
    held[-1], held[1] = around(mine, mine)
    owner, lengths, held[-1], held[1] = hold((owner, lengths, held[-1], held[1]))
    held[-2], held[2] = around(held[-1], held[1])
    sib[0] = send(mine, sibling)
    row_owner = lax.dynamic_slice_in_dim(owner, device_index * row_count, row_count)
    row_lengths = jnp.sum(
        jnp.where(
            row_owner[:, None] == jnp.arange(owner.shape[0], dtype=jnp.int32), lengths[None, :], 0
        ),
        axis=1,
        keepdims=True,
    )
    row_lengths = jnp.broadcast_to(row_lengths, (row_count, LANES))
    gain = norm_gain[None, :]
    scalars = jnp.array(
        [
            [device // sharers] + places
            for chip, places in enumerate(gathered_place(chips))
            for device in (2 * chip, 2 * chip + 1)
        ],
        jnp.int32,
    )[device_index]
    owned, row_lengths, gain, scalars, held[-2], held[2], sib[0] = hold(
        (owned, row_lengths, gain, scalars, held[-2], held[2], sib[0])
    )
    for t in range(3, half):
        held[-t], held[t] = around(held[1 - t], held[t - 1])
    sib[-1], sib[1] = send(held[-1], sibling), send(held[1], sibling)
    packet = attention(
        q_abs,
        owned.reshape(-1, kv_width),
        new_lat.reshape(rows, kv_width),
        row_lengths,
        routes.reshape(rows, -1),
        devices * positions,
        w_out.shape[0],
    )
    packet, held, sib = hold((packet, held, sib))

    high, low = gather_steps(chips)
    along = [send(packet, step_perm(chips, i, 0)) for i in range(1, high)]
    last = around(held[1 - half][:cut], held[half - 1][cut:])
    for t in range(2, half - 1):
        sib[-t], sib[t] = send(held[-t], sibling), send(held[t], sibling)
    along, last, sib = hold((along, last, sib))
    along = jnp.concatenate([packet] + along, axis=0)
    across = [send(along, step_perm(chips, 0, i)) for i in range(1, low)]
    held[half] = jnp.concatenate(last, axis=0)
    for d in (1 - half, half - 1, half):
        sib[d] = send(held[d], sibling)
    across, sib = hold((across, sib))
    across = across[0] if low == 2 else jnp.concatenate(across, axis=0)
    gathered = [along, across, send(along, sibling), send(across, sibling)]

    f32 = jnp.float32

    def normed(first, dists, with_hidden, gathered):
        blocks = [a[d] for a in (held, sib) for d in dists]
        return normalize(first, with_hidden, scalars, gathered, w_out, gain, w_router.T, blocks)

    def product(a, w):
        return jnp.dot(a, w[0], preferred_element_type=f32)

    def activate(a, b, scale, weight):
        r, g = scale[:, :1], weight[:, :1]
        return (jax.nn.silu(a * r) * (b * r) * g).astype(jnp.bfloat16)

    sums = {}

    def swap(dists, y):
        return y, send(y[len(dists) * rows :], sibling)

    def add_up(dists, y, received):
        for i, d in enumerate(dists):
            at = slice(i * rows, (i + 1) * rows)
            sums[d] = y[at].astype(f32) + received[at].astype(f32)

    def both(right, left):
        return around(right.astype(jnp.bfloat16), left.astype(jnp.bfloat16))

    x, scale, weight = normed(1, far, False, gathered)
    act = hold(activate(product(x, w_gate), product(x, w_up), scale, weight))
    y, received = swap(far, product(act, w_down).astype(jnp.bfloat16))
    y, gathered = hold((y, gathered))
    x, scale, weight, hidden = normed(1 + 2 * len(far), near, True, gathered)
    x, y, received = hold((x, y, received))
    add_up(far, y, received)
    right, left = both(sums[half][:cut], sums[half][cut:])
    act = activate(product(x, w_gate), product(x, w_up), scale, weight)
    act, right, left = hold((act, right, left))
    right = jnp.concatenate([right.astype(f32), jnp.zeros((rows - cut, width), f32)], axis=0)
    left = jnp.concatenate([jnp.zeros((cut, width), f32), left.astype(f32)], axis=0)
    right, left = both(sums[half - 1] + right, sums[1 - half] + left)
    y, received = swap(near, product(act, w_down).astype(jnp.bfloat16))
    y, received, right, left = hold((y, received, right, left))
    add_up(near, y, received)
    for t in range(half - 2, 0, -1):
        right, left = hold(both(sums[t] + right.astype(f32), sums[-t] + left.astype(f32)))
    mixed = hidden + sums[0] + right.astype(f32) + left.astype(f32)
    return mixed.astype(jnp.bfloat16).reshape(step_count, row_count, width)


def solution(mesh):
    return jax.shard_map(
        local,
        mesh=mesh,
        in_specs=(
            P(None, ("group", "expert"), None),
            P(None, ("group", "expert"), None),
            P("group", "expert", None),
            P("group"),
            P("group"),
            P(None, ("group", "expert"), None),
            P(None, ("group", "expert"), None),
            P(),
            P(),
            P(),
            P("expert", None, None),
            P("expert", None, None),
            P("expert", None, None),
        ),
        out_specs=P(None, ("group", "expert"), None),
        check_vma=False,
    )
```

```python
import jax
import jax.numpy as jnp
from jax import lax
from jax.experimental import pallas as pl
from jax.experimental.pallas import tpu as pltpu
from jax.sharding import PartitionSpec as P

qk_scale = 192.0 ** (-0.5)
LANES = 128


def ring_of(chips):
    return list(range(0, chips, 2)) + list(range(chips - 1, 0, -2))


def shift_perm(chips, by):
    ring = ring_of(chips)
    return [
        (2 * ring[p] + core, 2 * ring[(p + by) % chips] + core)
        for p in range(chips)
        for core in range(2)
    ]


def sibling_perm(chips):
    return [(d, d ^ 1) for d in range(2 * chips)]


def distances(chips):
    half = chips // 2
    far = [half, half - 1, 1 - half]
    return far, [0] + [d for t in range(1, half - 1) for d in (t, -t)]


def gather_steps(chips):
    high = 4 if chips % 4 == 0 else 2
    return high, chips // high


def step_perm(chips, by_high, by_low):
    high, low = gather_steps(chips)
    return [
        (
            2 * (h * low + l) + core,
            2 * ((h - by_high) % high * low + (l - by_low) % low) + core,
        )
        for h in range(high)
        for l in range(low)
        for core in range(2)
    ]


def gathered_place(chips):
    high, low = gather_steps(chips)
    ring = ring_of(chips)
    table = [[] for _ in range(chips)]
    for p, chip in enumerate(ring):
        for part in distances(chips):
            for side in (0, chips):
                for d in part:
                    other = ring[(p + d) % chips]
                    by_high = (other // low - chip // low) % high
                    by_low = (other % low - chip % low) % low
                    table[chip].append(side + by_low * high + by_high)
    return table


def tile_of(size, most):
    return max(t for t in range(LANES, min(size, most) + 1, LANES) if size % t == 0)


def norm_kernel(first, blocks, rows, latent, width, with_hidden, *refs):
    scalars = refs[0]
    pooled = refs[1:5]
    resid = refs[5 : 5 + blocks]
    w_out, gain, w_router, x, scale, weight = refs[5 + blocks : 11 + blocks]
    hidden = refs[11 + blocks] if with_hidden else None
    raw, joined, ssq, logits = refs[-4:]
    step = pl.program_id(0)
    cols = w_out.shape[1]
    total = blocks * rows
    experts_all = w_router.shape[0]
    chunk = min(512, total)

    @pl.when(step == 0)
    def _():
        start = 0
        for piece in pooled:
            raw[start : start + piece.shape[0], :] = piece[...]
            start += piece.shape[0]
        for b in range(blocks):
            place = pl.ds(pl.multiple_of(scalars[first + b] * rows, rows), rows)
            joined[b * rows : (b + 1) * rows, :] = raw[place, :]
        ssq[...] = jnp.zeros_like(ssq)
        logits[...] = jnp.zeros_like(logits)

    g = gain[...].astype(jnp.float32)
    for c in range(0, total, chunk):
        end = min(c + chunk, total)
        proj = jnp.dot(joined[c:end, :latent], w_out[...], preferred_element_type=jnp.float32)
        for b in range(c // rows, end // rows):
            at = slice(b * rows, (b + 1) * rows)
            h = proj[b * rows - c : (b + 1) * rows - c] + resid[b][...].astype(jnp.float32)
            if with_hidden and b == 0:
                hidden[...] = h
            x[at, :] = (h * g).astype(jnp.bfloat16)
            sq = h * h
            part = sq[:, :LANES]
            for k in range(1, cols // LANES):
                part = part + sq[:, k * LANES : (k + 1) * LANES]
            ssq[at, :] += part
    logits[...] += lax.dot_general(
        x[...], w_router[...], (((1,), (1,)), ((), ())), preferred_element_type=jnp.float32
    )

    @pl.when(step == pl.num_programs(0) - 1)
    def _():
        mean = jnp.sum(ssq[...], axis=1, keepdims=True) * (1.0 / width)
        r = lax.rsqrt(mean + 1e-06)
        mask = joined[:, latent : latent + experts_all].astype(jnp.float32)
        affinity = jax.nn.sigmoid(logits[...] * r) * mask
        lane = lax.broadcasted_iota(jnp.int32, affinity.shape, 1)
        mine = jnp.sum(jnp.where(lane == scalars[0], affinity, 0.0), axis=1, keepdims=True)
        gate = 2.5 * mine / jnp.sum(affinity, axis=1, keepdims=True)
        scale[...] = jnp.broadcast_to(r, scale.shape)
        weight[...] = jnp.broadcast_to(gate, weight.shape)


def normalize(first, with_hidden, scalars, pooled, w_out, gain, w_router_t, resid_blocks):
    blocks = len(resid_blocks)
    rows, width = resid_blocks[0].shape
    latent = w_out.shape[0]
    total = blocks * rows
    cols = tile_of(width, 1024)
    packed = pooled[0].shape[1]
    experts_all = w_router_t.shape[0]

    def whole(shape):
        return pl.BlockSpec(shape, lambda i: (0, 0), pipeline_mode=pl.Buffered(1))

    def tiles(height):
        return pl.BlockSpec((height, cols), lambda i: (0, i))

    gathered = sum(a.shape[0] for a in pooled)
    need = total * (cols * 16 + packed * 2 + 8 * LANES * 4) + gathered * packed * 4 + 4 * latent * cols
    return pl.pallas_call(
        lambda *refs: norm_kernel(first, blocks, rows, latent, width, with_hidden, *refs),
        grid=(width // cols,),
        in_specs=[pl.BlockSpec(memory_space=pltpu.SMEM)]
        + [whole(a.shape) for a in pooled]
        + [tiles(rows)] * blocks
        + [tiles(latent), tiles(1), tiles(experts_all)],
        out_shape=[
            jax.ShapeDtypeStruct((total, width), jnp.bfloat16),
            jax.ShapeDtypeStruct((total, LANES), jnp.float32),
            jax.ShapeDtypeStruct((total, LANES), jnp.float32),
        ]
        + [jax.ShapeDtypeStruct((rows, width), jnp.float32)] * with_hidden,
        out_specs=[tiles(total), whole((total, LANES)), whole((total, LANES))]
        + [tiles(rows)] * with_hidden,
        scratch_shapes=[
            pltpu.VMEM((gathered, packed), jnp.bfloat16),
            pltpu.VMEM((total, packed), jnp.bfloat16),
            pltpu.VMEM((total, LANES), jnp.float32),
            pltpu.VMEM((total, experts_all), jnp.float32),
        ],
        compiler_params=pltpu.CompilerParams(
            dimension_semantics=("arbitrary",), vmem_limit_bytes=(int(need) // (1 << 20) + 6) << 20
        ),
        cost_estimate=pl.CostEstimate(
            flops=2 * total * width * latent,
            bytes_accessed=2 * total * width * 2 + latent * width * 2,
            transcendentals=total,
        ),
        name="normalize",
    )(scalars, *pooled, *resid_blocks, w_out, gain, w_router_t)


def lengths_kernel(owner, lengths, device, out):
    rows = out.shape[0]
    for j in range(rows):
        length = lengths[owner[device[0] * rows + j]]
        out[j : j + 1, :] = jnp.full((1, LANES), length, jnp.int32)


def lengths_of(owner, lengths, device_index, rows):
    scalar = pl.BlockSpec(memory_space=pltpu.SMEM)
    return pl.pallas_call(
        lengths_kernel,
        in_specs=[scalar] * 3,
        out_shape=jax.ShapeDtypeStruct((rows, LANES), jnp.int32),
        cost_estimate=pl.CostEstimate(flops=10**10, bytes_accessed=10**8, transcendentals=0),
        name="lengths",
    )(owner, lengths, device_index[None])


def attention_kernel(context, latent, q, cache, fresh, lengths, routes, packet, keys_a, keys_b, total):
    step = pl.program_id(0)
    rows, kv_width = q.shape[1], cache.shape[1]
    wide = keys_a.shape[1]
    pairs = q.shape[2] // (2 * kv_width)
    keys = keys_a.shape[0]
    cached = cache.shape[0]

    @pl.when(step == 0)
    def _():
        keys_a[...] = jnp.zeros_like(keys_a)
        keys_a[:cached, :kv_width] = cache[...]
        keys_a[cached:, :kv_width] = fresh[...]
        shifted = pltpu.roll(keys_a[...].astype(jnp.float32), wide - kv_width, 1)
        keys_b[...] = shifted.astype(jnp.bfloat16)

    row = lax.broadcasted_iota(jnp.int32, (rows, keys), 0)
    key = lax.broadcasted_iota(jnp.int32, (rows, keys), 1)
    place = key // rows
    seen = (place < lengths[:, :1]) & (place < context)
    seen = seen | ((place >= context) & (place <= context + step))
    bias = jnp.where(seen & (key % rows == row), 0.0, -1e30)
    summed = jnp.zeros((rows, keys), jnp.float32)
    for held, first in ((keys_a, 0), (keys_b, 2 * kv_width - wide)):
        heads = [
            q[0, :, 2 * kv_width * i + first : 2 * kv_width * i + first + wide].astype(jnp.float32)
            for i in range(pairs)
        ]
        scores = lax.dot_general(
            jnp.concatenate(heads, axis=0).astype(jnp.bfloat16),
            held[...],
            (((1,), (1,)), ((), ())),
            preferred_element_type=jnp.float32,
        )
        scores = (scores * qk_scale).reshape(pairs, rows, keys) + bias[None]
        e = jnp.exp(scores - jnp.max(scores, axis=2, keepdims=True))
        weights = e / jnp.sum(e, axis=2, keepdims=True)
        summed = summed + jnp.sum(weights.astype(jnp.bfloat16).astype(jnp.float32), axis=0)
    total[pl.ds(pl.multiple_of(step * rows, rows), rows), :] = summed

    @pl.when(step == pl.num_programs(0) - 1)
    def _():
        high = total[...].astype(jnp.bfloat16)
        low = (total[...] - high.astype(jnp.float32)).astype(jnp.bfloat16)
        values = keys_a[:, :latent]
        pooled = jnp.dot(high, values, preferred_element_type=jnp.float32)
        pooled = pooled + jnp.dot(low, values, preferred_element_type=jnp.float32)
        packet[:, :latent] = pooled.astype(jnp.bfloat16)
        lane = lax.broadcasted_iota(jnp.int32, (packet.shape[0], LANES), 1)
        routed = jnp.zeros(lane.shape, jnp.float32)
        for k in range(routes.shape[1]):
            routed = jnp.where(routes[:, k : k + 1] == lane, 1.0, routed)
        packet[:, latent:] = routed.astype(jnp.bfloat16)


def attention(q_abs, cache, fresh, lengths, routes, context, latent):
    steps, rows, _ = q_abs.shape
    kv_width = cache.shape[1]
    keys = cache.shape[0] + fresh.shape[0]
    wide = -(-kv_width // LANES) * LANES

    def whole(a):
        return pl.BlockSpec(a.shape, lambda i: (0, 0), pipeline_mode=pl.Buffered(1))

    heads = q_abs.shape[2] // kv_width
    return pl.pallas_call(
        lambda *refs: attention_kernel(context, latent, *refs),
        grid=(steps,),
        in_specs=[pl.BlockSpec((1, rows, q_abs.shape[2]), lambda i: (i, 0, 0))]
        + [whole(a) for a in (cache, fresh, lengths, routes)],
        out_shape=jax.ShapeDtypeStruct((steps * rows, latent + LANES), jnp.bfloat16),
        out_specs=pl.BlockSpec((steps * rows, latent + LANES), lambda i: (0, 0)),
        scratch_shapes=[
            pltpu.VMEM((keys, wide), jnp.bfloat16),
            pltpu.VMEM((keys, wide), jnp.bfloat16),
            pltpu.VMEM((steps * rows, keys), jnp.float32),
        ],
        compiler_params=pltpu.CompilerParams(
            dimension_semantics=("arbitrary",), vmem_limit_bytes=(10 << 20) + 10240 * keys
        ),
        cost_estimate=pl.CostEstimate(
            flops=2 * steps * rows * heads * wide * keys,
            bytes_accessed=2 * q_abs.size,
            transcendentals=steps * rows * heads * keys,
        ),
        name="attention",
    )(q_abs, cache, fresh, lengths, routes)


def local(
    q_abs,
    new_lat,
    latent_cache,
    lengths,
    owner,
    resid,
    routes,
    w_out,
    norm_gain,
    w_router,
    w_gate,
    w_up,
    w_down,
):
    devices = lax.axis_size("expert")
    device_index = lax.axis_index("expert")
    step_count, row_count, width = resid.shape
    rows = step_count * row_count
    experts_all = w_router.shape[1]
    sharers = devices // experts_all
    chips = devices // 2
    half = chips // 2
    cut = rows // 2
    far, near = distances(chips)
    hold = lax.optimization_barrier
    sibling = sibling_perm(chips)

    def send(a, perm):
        return lax.ppermute(a, "expert", perm)

    to_right, to_left = shift_perm(chips, 1), shift_perm(chips, -1)

    def around(to_the_right, to_the_left):
        return send(to_the_right, to_right), send(to_the_left, to_left)

    positions, kv_width = latent_cache.shape[1:]
    wanted = (owner[:, None] == jnp.arange(owner.shape[0], dtype=jnp.int32)).astype(jnp.bfloat16)
    ordered = jnp.einsum(
        "jr,rpk->pjk", wanted, latent_cache, preferred_element_type=jnp.float32
    ).astype(jnp.bfloat16)
    ordered = ordered.reshape(positions, devices, row_count, kv_width).swapaxes(0, 1)
    owned = lax.all_to_all(ordered, "expert", split_axis=0, concat_axis=0, tiled=True)

    mine = resid.reshape(rows, width)
    held, sib = {0: mine}, {}
    held[-1], held[1] = around(mine, mine)
    row_lengths = lengths_of(owner, lengths, device_index, row_count)
    row_lengths, held[-1], held[1] = hold((row_lengths, held[-1], held[1]))
    held[-2], held[2] = around(held[-1], held[1])
    sib[0] = send(mine, sibling)
    gain = norm_gain[None, :]
    scalars = jnp.array(
        [
            [device // sharers] + places
            for chip, places in enumerate(gathered_place(chips))
            for device in (2 * chip, 2 * chip + 1)
        ],
        jnp.int32,
    )[device_index]
    owned, row_lengths, gain, scalars, held[-2], held[2], sib[0] = hold(
        (owned, row_lengths, gain, scalars, held[-2], held[2], sib[0])
    )
    for t in range(3, half):
        held[-t], held[t] = around(held[1 - t], held[t - 1])
    sib[-1], sib[1] = send(held[-1], sibling), send(held[1], sibling)
    packet = attention(
        q_abs,
        owned.reshape(-1, kv_width),
        new_lat.reshape(rows, kv_width),
        row_lengths,
        routes.reshape(rows, -1),
        devices * positions,
        w_out.shape[0],
    )
    packet, held, sib = hold((packet, held, sib))

    high, low = gather_steps(chips)
    along = [send(packet, step_perm(chips, i, 0)) for i in range(1, high)]
    last = around(held[1 - half][:cut], held[half - 1][cut:])
    for t in range(2, half - 1):
        sib[-t], sib[t] = send(held[-t], sibling), send(held[t], sibling)
    along, last, sib = hold((along, last, sib))
    along = jnp.concatenate([packet] + along, axis=0)
    across = [send(along, step_perm(chips, 0, i)) for i in range(1, low)]
    held[half] = jnp.concatenate(last, axis=0)
    for d in (1 - half, half - 1, half):
        sib[d] = send(held[d], sibling)
    across, sib = hold((across, sib))
    across = across[0] if low == 2 else jnp.concatenate(across, axis=0)
    gathered = [along, across, send(along, sibling), send(across, sibling)]

    f32 = jnp.float32

    def normed(first, dists, with_hidden, gathered):
        blocks = [a[d] for a in (held, sib) for d in dists]
        return normalize(first, with_hidden, scalars, gathered, w_out, gain, w_router.T, blocks)

    def product(a, w):
        return jnp.dot(a, w[0], preferred_element_type=f32)

    def activate(a, b, scale, weight):
        r, g = scale[:, :1], weight[:, :1]
        return (jax.nn.silu(a * r) * (b * r) * g).astype(jnp.bfloat16)

    sums = {}

    def swap(dists, y):
        return y, send(y[len(dists) * rows :], sibling)

    def add_up(dists, y, received):
        for i, d in enumerate(dists):
            at = slice(i * rows, (i + 1) * rows)
            sums[d] = y[at].astype(f32) + received[at].astype(f32)

    def both(right, left):
        return around(right.astype(jnp.bfloat16), left.astype(jnp.bfloat16))

    x, scale, weight = normed(1, far, False, gathered)
    act = hold(activate(product(x, w_gate), product(x, w_up), scale, weight))
    y, received = swap(far, product(act, w_down).astype(jnp.bfloat16))
    y, gathered = hold((y, gathered))
    x, scale, weight, hidden = normed(1 + 2 * len(far), near, True, gathered)
    x, y, received = hold((x, y, received))
    add_up(far, y, received)
    right, left = both(sums[half][:cut], sums[half][cut:])
    act = activate(product(x, w_gate), product(x, w_up), scale, weight)
    act, right, left = hold((act, right, left))
    right = jnp.concatenate([right.astype(f32), jnp.zeros((rows - cut, width), f32)], axis=0)
    left = jnp.concatenate([jnp.zeros((cut, width), f32), left.astype(f32)], axis=0)
    right, left = both(sums[half - 1] + right, sums[1 - half] + left)
    y, received = swap(near, product(act, w_down).astype(jnp.bfloat16))
    y, received, right, left = hold((y, received, right, left))
    add_up(near, y, received)
    for t in range(half - 2, 0, -1):
        right, left = hold(both(sums[t] + right.astype(f32), sums[-t] + left.astype(f32)))
    mixed = hidden + sums[0] + right.astype(f32) + left.astype(f32)
    return mixed.astype(jnp.bfloat16).reshape(step_count, row_count, width)


def solution(mesh):
    return jax.shard_map(
        local,
        mesh=mesh,
        in_specs=(
            P(None, ("group", "expert"), None),
            P(None, ("group", "expert"), None),
            P("group", "expert", None),
            P("group"),
            P("group"),
            P(None, ("group", "expert"), None),
            P(None, ("group", "expert"), None),
            P(),
            P(),
            P(),
            P("expert", None, None),
            P("expert", None, None),
            P("expert", None, None),
        ),
        out_specs=P(None, ("group", "expert"), None),
        check_vma=False,
    )
```

```python
import jax
import jax.numpy as jnp
from jax import lax
from jax.experimental import pallas as pl
from jax.experimental.pallas import tpu as pltpu
from jax.sharding import PartitionSpec as P

qk_scale = 192.0 ** (-0.5)
LANES = 128


def ring_of(chips):
    return list(range(0, chips, 2)) + list(range(chips - 1, 0, -2))


def shift_perm(chips, by):
    ring = ring_of(chips)
    return [
        (2 * ring[p] + core, 2 * ring[(p + by) % chips] + core)
        for p in range(chips)
        for core in range(2)
    ]


def sibling_perm(chips):
    return [(d, d ^ 1) for d in range(2 * chips)]


def distances(chips):
    half = chips // 2
    far = [half, half - 1, 1 - half]
    return far, [0] + [d for t in range(1, half - 1) for d in (t, -t)]


def gather_steps(chips):
    high = 4 if chips % 4 == 0 else 2
    return high, chips // high


def step_perm(chips, by_high, by_low):
    high, low = gather_steps(chips)
    return [
        (
            2 * (h * low + l) + core,
            2 * ((h - by_high) % high * low + (l - by_low) % low) + core,
        )
        for h in range(high)
        for l in range(low)
        for core in range(2)
    ]


def gathered_place(chips):
    high, low = gather_steps(chips)
    ring = ring_of(chips)
    table = [[] for _ in range(chips)]
    for p, chip in enumerate(ring):
        for part in distances(chips):
            for side in (0, chips):
                for d in part:
                    other = ring[(p + d) % chips]
                    by_high = (other // low - chip // low) % high
                    by_low = (other % low - chip % low) % low
                    table[chip].append(side + by_low * high + by_high)
    return table


def tile_of(size, most):
    return max(t for t in range(LANES, min(size, most) + 1, LANES) if size % t == 0)


def norm_kernel(far, blocks, rows, latent, width, *refs):
    scalars = refs[0]
    pooled = refs[1:5]
    resid = refs[5 : 5 + blocks]
    w_out, gain, w_router, x_far, x_near = refs[5 + blocks : 10 + blocks]
    scale, weight, hidden, raw, joined, ssq, logits = refs[10 + blocks :]
    step = pl.program_id(0)
    cols = w_out.shape[1]
    total = blocks * rows
    far_rows = far * rows
    experts_all = w_router.shape[0]
    chunk = min(512, total)

    @pl.when(step == 0)
    def _():
        start = 0
        for piece in pooled:
            raw[start : start + piece.shape[0], :] = piece[...]
            start += piece.shape[0]
        for b in range(blocks):
            place = pl.ds(pl.multiple_of(scalars[1 + b] * rows, rows), rows)
            joined[b * rows : (b + 1) * rows, :] = raw[place, :]
        ssq[...] = jnp.zeros_like(ssq)
        logits[...] = jnp.zeros_like(logits)

    g = gain[...].astype(jnp.float32)
    for c in range(0, total, chunk):
        end = min(c + chunk, total)
        proj = jnp.dot(joined[c:end, :latent], w_out[...], preferred_element_type=jnp.float32)
        for b in range(c // rows, end // rows):
            at = slice(b * rows, (b + 1) * rows)
            h = proj[b * rows - c : (b + 1) * rows - c] + resid[b][...].astype(jnp.float32)
            if b == far:
                hidden[...] = h
            scaled = (h * g).astype(jnp.bfloat16)
            if b < far:
                x_far[at, :] = scaled
            else:
                x_near[(b - far) * rows : (b - far + 1) * rows, :] = scaled
            sq = h * h
            part = sq[:, :LANES]
            for k in range(1, cols // LANES):
                part = part + sq[:, k * LANES : (k + 1) * LANES]
            ssq[at, :] += part
    nt = (((1,), (1,)), ((), ()))
    for x, at in ((x_far, slice(0, far_rows)), (x_near, slice(far_rows, total))):
        logits[at, :] += lax.dot_general(
            x[...], w_router[...], nt, preferred_element_type=jnp.float32
        )

    @pl.when(step == pl.num_programs(0) - 1)
    def _():
        mean = jnp.sum(ssq[...], axis=1, keepdims=True) * (1.0 / width)
        r = lax.rsqrt(mean + 1e-06)
        mask = joined[:, latent : latent + experts_all].astype(jnp.float32)
        affinity = jax.nn.sigmoid(logits[...] * r) * mask
        lane = lax.broadcasted_iota(jnp.int32, affinity.shape, 1)
        mine = jnp.sum(jnp.where(lane == scalars[0], affinity, 0.0), axis=1, keepdims=True)
        gate = 2.5 * mine / jnp.sum(affinity, axis=1, keepdims=True)
        scale[...] = jnp.broadcast_to(r, scale.shape)
        weight[...] = jnp.broadcast_to(gate, weight.shape)


def normalize(far, scalars, pooled, resid_blocks, w_out, gain, w_router_t):
    blocks = len(resid_blocks)
    rows, width = resid_blocks[0].shape
    latent = w_out.shape[0]
    total = blocks * rows
    cols = tile_of(width, 1024)
    packed = pooled[0].shape[1]
    experts_all = w_router_t.shape[0]

    def whole(shape):
        return pl.BlockSpec(shape, lambda i: (0, 0), pipeline_mode=pl.Buffered(1))

    def tiles(height):
        return pl.BlockSpec((height, cols), lambda i: (0, i))

    need = total * (cols * 16 + packed * 6 + 8 * LANES * 4) + 4 * latent * cols
    return pl.pallas_call(
        lambda *refs: norm_kernel(far, blocks, rows, latent, width, *refs),
        grid=(width // cols,),
        in_specs=[pl.BlockSpec(memory_space=pltpu.SMEM)]
        + [whole(a.shape) for a in pooled]
        + [tiles(rows)] * blocks
        + [tiles(latent), tiles(1), tiles(experts_all)],
        out_shape=[
            jax.ShapeDtypeStruct((far * rows, width), jnp.bfloat16),
            jax.ShapeDtypeStruct((total - far * rows, width), jnp.bfloat16),
            jax.ShapeDtypeStruct((total, LANES), jnp.float32),
            jax.ShapeDtypeStruct((total, LANES), jnp.float32),
            jax.ShapeDtypeStruct((rows, width), jnp.float32),
        ],
        out_specs=[tiles(far * rows), tiles(total - far * rows)]
        + [whole((total, LANES)), whole((total, LANES)), tiles(rows)],
        scratch_shapes=[
            pltpu.VMEM((total, packed), jnp.bfloat16),
            pltpu.VMEM((total, packed), jnp.bfloat16),
            pltpu.VMEM((total, LANES), jnp.float32),
            pltpu.VMEM((total, experts_all), jnp.float32),
        ],
        compiler_params=pltpu.CompilerParams(
            dimension_semantics=("arbitrary",), vmem_limit_bytes=(int(need) // (1 << 20) + 6) << 20
        ),
        cost_estimate=pl.CostEstimate(
            flops=2 * total * width * latent,
            bytes_accessed=2 * total * width * 2 + latent * width * 2,
            transcendentals=total,
        ),
        name="normalize",
    )(scalars, *pooled, *resid_blocks, w_out, gain, w_router_t)


def lengths_kernel(owner, lengths, device, out):
    rows = out.shape[0]
    for j in range(rows):
        length = lengths[owner[device[0] * rows + j]]
        out[j : j + 1, :] = jnp.full((1, LANES), length, jnp.int32)


LONG = dict(flops=10**10, bytes_accessed=10**8, transcendentals=0)


def lengths_of(owner, lengths, device_index, rows):
    scalar = pl.BlockSpec(memory_space=pltpu.SMEM)
    return pl.pallas_call(
        lengths_kernel,
        in_specs=[scalar] * 3,
        out_shape=jax.ShapeDtypeStruct((rows, LANES), jnp.int32),
        cost_estimate=pl.CostEstimate(**LONG),
        name="lengths",
    )(owner, lengths, device_index[None])


def attention_kernel(context, latent, q, cache, fresh, lengths, routes, packet, keys_a, keys_b, total):
    step = pl.program_id(0)
    rows, kv_width = q.shape[1], cache.shape[1]
    wide = keys_a.shape[1]
    pairs = q.shape[2] // (2 * kv_width)
    keys = keys_a.shape[0]
    cached = cache.shape[0]

    @pl.when(step == 0)
    def _():
        keys_a[...] = jnp.zeros_like(keys_a)
        keys_a[:cached, :kv_width] = cache[...]
        keys_a[cached:, :kv_width] = fresh[...]
        shifted = pltpu.roll(keys_a[...].astype(jnp.float32), wide - kv_width, 1)
        keys_b[...] = shifted.astype(jnp.bfloat16)

    row = lax.broadcasted_iota(jnp.int32, (rows, keys), 0)
    key = lax.broadcasted_iota(jnp.int32, (rows, keys), 1)
    place = key // rows
    seen = (place < lengths[:, :1]) & (place < context)
    seen = seen | ((place >= context) & (place <= context + step))
    bias = jnp.where(seen & (key % rows == row), 0.0, -1e30)
    summed = jnp.zeros((rows, keys), jnp.float32)
    for held, first in ((keys_a, 0), (keys_b, 2 * kv_width - wide)):
        heads = [
            q[0, :, 2 * kv_width * i + first : 2 * kv_width * i + first + wide].astype(jnp.float32)
            for i in range(pairs)
        ]
        scores = lax.dot_general(
            jnp.concatenate(heads, axis=0).astype(jnp.bfloat16),
            held[...],
            (((1,), (1,)), ((), ())),
            preferred_element_type=jnp.float32,
        )
        scores = (scores * qk_scale).reshape(pairs, rows, keys) + bias[None]
        e = jnp.exp(scores - jnp.max(scores, axis=2, keepdims=True))
        weights = e / jnp.sum(e, axis=2, keepdims=True)
        summed = summed + jnp.sum(weights.astype(jnp.bfloat16).astype(jnp.float32), axis=0)
    total[pl.ds(pl.multiple_of(step * rows, rows), rows), :] = summed

    @pl.when(step == pl.num_programs(0) - 1)
    def _():
        high = total[...].astype(jnp.bfloat16)
        low = (total[...] - high.astype(jnp.float32)).astype(jnp.bfloat16)
        values = keys_a[:, :latent]
        pooled = jnp.dot(high, values, preferred_element_type=jnp.float32)
        pooled = pooled + jnp.dot(low, values, preferred_element_type=jnp.float32)
        packet[:, :latent] = pooled.astype(jnp.bfloat16)
        lane = lax.broadcasted_iota(jnp.int32, (packet.shape[0], LANES), 1)
        routed = jnp.zeros(lane.shape, jnp.float32)
        for k in range(routes.shape[1]):
            routed = jnp.where(routes[:, k : k + 1] == lane, 1.0, routed)
        packet[:, latent:] = routed.astype(jnp.bfloat16)


def attention(q_abs, cache, fresh, lengths, routes, context, latent):
    steps, rows, _ = q_abs.shape
    kv_width = cache.shape[1]
    keys = cache.shape[0] + fresh.shape[0]
    wide = -(-kv_width // LANES) * LANES

    def whole(a):
        return pl.BlockSpec(a.shape, lambda i: (0, 0), pipeline_mode=pl.Buffered(1))

    return pl.pallas_call(
        lambda *refs: attention_kernel(context, latent, *refs),
        grid=(steps,),
        in_specs=[pl.BlockSpec((1, rows, q_abs.shape[2]), lambda i: (i, 0, 0))]
        + [whole(a) for a in (cache, fresh, lengths, routes)],
        out_shape=jax.ShapeDtypeStruct((steps * rows, latent + LANES), jnp.bfloat16),
        out_specs=pl.BlockSpec((steps * rows, latent + LANES), lambda i: (0, 0)),
        scratch_shapes=[
            pltpu.VMEM((keys, wide), jnp.bfloat16),
            pltpu.VMEM((keys, wide), jnp.bfloat16),
            pltpu.VMEM((steps * rows, keys), jnp.float32),
        ],
        compiler_params=pltpu.CompilerParams(
            dimension_semantics=("arbitrary",), vmem_limit_bytes=(10 << 20) + 10240 * keys
        ),
        cost_estimate=pl.CostEstimate(**LONG),
        name="attention",
    )(q_abs, cache, fresh, lengths, routes)


def local(
    q_abs,
    new_lat,
    latent_cache,
    lengths,
    owner,
    resid,
    routes,
    w_out,
    norm_gain,
    w_router,
    w_gate,
    w_up,
    w_down,
):
    devices = lax.axis_size("expert")
    device_index = lax.axis_index("expert")
    step_count, row_count, width = resid.shape
    rows = step_count * row_count
    experts_all = w_router.shape[1]
    sharers = devices // experts_all
    chips = devices // 2
    half = chips // 2
    cut = rows // 2
    far, near = distances(chips)
    hold = lax.optimization_barrier
    sibling = sibling_perm(chips)

    def send(a, perm):
        return lax.ppermute(a, "expert", perm)

    shifts = [(shift_perm(chips, by), shift_perm(chips, -by)) for by in (1, 2)]

    def around(to_the_right, to_the_left, by=1):
        right, left = shifts[by - 1]
        return send(to_the_right, right), send(to_the_left, left)

    positions, kv_width = latent_cache.shape[1:]
    wanted = (owner[:, None] == jnp.arange(owner.shape[0], dtype=jnp.int32)).astype(jnp.bfloat16)
    ordered = jnp.einsum(
        "jr,rpk->pjk", wanted, latent_cache, preferred_element_type=jnp.float32
    ).astype(jnp.bfloat16)
    ordered = ordered.reshape(positions, devices, row_count, kv_width).swapaxes(0, 1)
    owned = lax.all_to_all(ordered, "expert", split_axis=0, concat_axis=0, tiled=True)

    mine = resid.reshape(rows, width)
    held, sib = {0: mine}, {}
    held[-1], held[1] = around(mine, mine)
    held[-2], held[2] = around(mine, mine, 2)
    row_lengths = lengths_of(owner, lengths, device_index, row_count)
    row_lengths, held = hold((row_lengths, held))
    for t in range(3, half):
        held[-t], held[t] = around(held[1 - t], held[t - 1])
    last = around(held[2 - half][:cut], held[half - 2][cut:], 2)
    for d in (0, -1, 1, -2, 2):
        sib[d] = send(held[d], sibling)
    gain = norm_gain[None, :]
    scalars = jnp.array(
        [
            [device // sharers] + places
            for chip, places in enumerate(gathered_place(chips))
            for device in (2 * chip, 2 * chip + 1)
        ],
        jnp.int32,
    )[device_index]
    packet = attention(
        q_abs,
        owned.reshape(-1, kv_width),
        new_lat.reshape(rows, kv_width),
        row_lengths,
        routes.reshape(rows, -1),
        devices * positions,
        w_out.shape[0],
    )
    packet, gain, scalars, held, last, sib = hold((packet, gain, scalars, held, last, sib))

    high, low = gather_steps(chips)
    along = [send(packet, step_perm(chips, i, 0)) for i in range(1, high)]
    along = hold(along)
    along = jnp.concatenate([packet] + along, axis=0)
    across = [send(along, step_perm(chips, 0, i)) for i in range(1, low)]
    held[half] = jnp.concatenate(last, axis=0)
    for d in held:
        if d not in sib:
            sib[d] = send(held[d], sibling)
    across, sib = hold((across, sib))
    across = across[0] if low == 2 else jnp.concatenate(across, axis=0)
    gathered = [along, across, send(along, sibling), send(across, sibling)]

    f32 = jnp.float32

    x_far, x_near, scale, weight, hidden = normalize(
        2 * len(far),
        scalars,
        gathered,
        [a[d] for part in (far, near) for a in (held, sib) for d in part],
        w_out,
        gain,
        w_router.T,
    )
    far_rows = x_far.shape[0]

    def product(a, w):
        return jnp.dot(a, w[0], preferred_element_type=f32)

    def activate(a, b, at):
        r, g = scale[at, :1], weight[at, :1]
        return (jax.nn.silu(a * r) * (b * r) * g).astype(jnp.bfloat16)

    sums = {}

    def swap(dists, y):
        return y, send(y[len(dists) * rows :], sibling)

    def add_up(dists, y, received):
        for i, d in enumerate(dists):
            at = slice(i * rows, (i + 1) * rows)
            sums[d] = y[at].astype(f32) + received[at].astype(f32)

    def both(right, left, by=1):
        return around(right.astype(jnp.bfloat16), left.astype(jnp.bfloat16), by)

    act = hold(activate(product(x_far, w_gate), product(x_far, w_up), slice(0, far_rows)))
    y, received = swap(far, product(act, w_down).astype(jnp.bfloat16))
    gated, y, received = hold((product(x_near, w_gate), y, received))
    add_up(far, y, received)
    right, left = both(sums[half - 1], sums[1 - half])
    right2, left2 = both(sums[half][:cut], sums[half][cut:], 2)
    act = activate(gated, product(x_near, w_up), slice(far_rows, None))
    y = product(act, w_down).astype(jnp.bfloat16)
    y, right, left, right2, left2 = hold((y, right, left, right2, left2))
    y, received = swap(near, y)
    add_up(near, y, received)
    right = right.astype(f32) + jnp.pad(right2.astype(f32), ((0, rows - cut), (0, 0)))
    left = left.astype(f32) + jnp.pad(left2.astype(f32), ((cut, 0), (0, 0)))
    for t in range(half - 2, 0, -1):
        right, left = hold(both(sums[t] + right.astype(f32), sums[-t] + left.astype(f32)))
    mixed = hidden + sums[0] + right.astype(f32) + left.astype(f32)
    return mixed.astype(jnp.bfloat16).reshape(step_count, row_count, width)


def solution(mesh):
    return jax.shard_map(
        local,
        mesh=mesh,
        in_specs=(
            P(None, ("group", "expert"), None),
            P(None, ("group", "expert"), None),
            P("group", "expert", None),
            P("group"),
            P("group"),
            P(None, ("group", "expert"), None),
            P(None, ("group", "expert"), None),
            P(),
            P(),
            P(),
            P("expert", None, None),
            P("expert", None, None),
            P("expert", None, None),
        ),
        out_specs=P(None, ("group", "expert"), None),
        check_vma=False,
    )
```

```python
import jax
import jax.numpy as jnp
from jax import lax
from jax.experimental import pallas as pl
from jax.experimental.pallas import tpu as pltpu
from jax.sharding import PartitionSpec as P

qk_scale = 192.0 ** (-0.5)
LANES = 128


def ring_of(chips):
    return list(range(0, chips, 2)) + list(range(chips - 1, 0, -2))


def shift_perm(chips, by):
    ring = ring_of(chips)
    return [
        (2 * ring[p] + core, 2 * ring[(p + by) % chips] + core)
        for p in range(chips)
        for core in range(2)
    ]


def sibling_perm(chips):
    return [(d, d ^ 1) for d in range(2 * chips)]


def distances(chips):
    half = chips // 2
    far = [half, half - 1, 1 - half]
    return far, [0] + [d for t in range(1, half - 1) for d in (t, -t)]


def gather_steps(chips):
    high = 4 if chips % 4 == 0 else 2
    return high, chips // high


def step_perm(chips, by_high, by_low):
    high, low = gather_steps(chips)
    return [
        (
            2 * (h * low + l) + core,
            2 * ((h - by_high) % high * low + (l - by_low) % low) + core,
        )
        for h in range(high)
        for l in range(low)
        for core in range(2)
    ]


def gathered_place(chips):
    high, low = gather_steps(chips)
    ring = ring_of(chips)
    table = [[] for _ in range(chips)]
    for p, chip in enumerate(ring):
        for part in distances(chips):
            for side in (0, chips):
                for d in part:
                    other = ring[(p + d) % chips]
                    by_high = (other // low - chip // low) % high
                    by_low = (other % low - chip % low) % low
                    table[chip].append(side + by_low * high + by_high)
    return table


def tile_of(size, most):
    return max(t for t in range(LANES, min(size, most) + 1, LANES) if size % t == 0)


def norm_kernel(far, blocks, rows, latent, width, *refs):
    scalars = refs[0]
    pooled = refs[1:5]
    resid = refs[5 : 5 + blocks]
    w_out, gain, w_router, x_far, x_near = refs[5 + blocks : 10 + blocks]
    scale, weight, hidden, raw, joined, ssq, logits = refs[10 + blocks :]
    step = pl.program_id(0)
    cols = w_out.shape[1]
    total = blocks * rows
    far_rows = far * rows
    experts_all = w_router.shape[0]
    chunk = min(512, total)

    @pl.when(step == 0)
    def _():
        start = 0
        for piece in pooled:
            raw[start : start + piece.shape[0], :] = piece[...]
            start += piece.shape[0]
        for b in range(blocks):
            place = pl.ds(pl.multiple_of(scalars[1 + b] * rows, rows), rows)
            joined[b * rows : (b + 1) * rows, :] = raw[place, :]
        ssq[...] = jnp.zeros_like(ssq)
        logits[...] = jnp.zeros_like(logits)

    g = gain[...].astype(jnp.float32)
    for c in range(0, total, chunk):
        end = min(c + chunk, total)
        proj = jnp.dot(joined[c:end, :latent], w_out[...], preferred_element_type=jnp.float32)
        for b in range(c // rows, end // rows):
            at = slice(b * rows, (b + 1) * rows)
            h = proj[b * rows - c : (b + 1) * rows - c] + resid[b][...].astype(jnp.float32)
            if b == far:
                hidden[...] = h
            scaled = (h * g).astype(jnp.bfloat16)
            if b < far:
                x_far[at, :] = scaled
            else:
                x_near[(b - far) * rows : (b - far + 1) * rows, :] = scaled
            sq = h * h
            part = sq[:, :LANES]
            for k in range(1, cols // LANES):
                part = part + sq[:, k * LANES : (k + 1) * LANES]
            ssq[at, :] += part
    nt = (((1,), (1,)), ((), ()))
    for x, at in ((x_far, slice(0, far_rows)), (x_near, slice(far_rows, total))):
        logits[at, :] += lax.dot_general(
            x[...], w_router[...], nt, preferred_element_type=jnp.float32
        )

    @pl.when(step == pl.num_programs(0) - 1)
    def _():
        mean = jnp.sum(ssq[...], axis=1, keepdims=True) * (1.0 / width)
        r = lax.rsqrt(mean + 1e-06)
        mask = joined[:, latent : latent + experts_all].astype(jnp.float32)
        affinity = jax.nn.sigmoid(logits[...] * r) * mask
        lane = lax.broadcasted_iota(jnp.int32, affinity.shape, 1)
        mine = jnp.sum(jnp.where(lane == scalars[0], affinity, 0.0), axis=1, keepdims=True)
        gate = 2.5 * mine / jnp.sum(affinity, axis=1, keepdims=True)
        scale[...] = jnp.broadcast_to(r, scale.shape)
        weight[...] = jnp.broadcast_to(gate, weight.shape)


def normalize(far, scalars, pooled, resid_blocks, w_out, gain, w_router_t):
    blocks = len(resid_blocks)
    rows, width = resid_blocks[0].shape
    latent = w_out.shape[0]
    total = blocks * rows
    cols = tile_of(width, 1024)
    packed = pooled[0].shape[1]
    experts_all = w_router_t.shape[0]

    def whole(shape):
        return pl.BlockSpec(shape, lambda i: (0, 0), pipeline_mode=pl.Buffered(1))

    def tiles(height):
        return pl.BlockSpec((height, cols), lambda i: (0, i))

    need = total * (cols * 14 + packed * 6 + 6 * LANES * 4) + 4 * latent * cols
    return pl.pallas_call(
        lambda *refs: norm_kernel(far, blocks, rows, latent, width, *refs),
        grid=(width // cols,),
        in_specs=[pl.BlockSpec(memory_space=pltpu.SMEM)]
        + [whole(a.shape) for a in pooled]
        + [tiles(rows)] * blocks
        + [tiles(latent), tiles(1), tiles(experts_all)],
        out_shape=[
            jax.ShapeDtypeStruct((far * rows, width), jnp.bfloat16),
            jax.ShapeDtypeStruct((total - far * rows, width), jnp.bfloat16),
            jax.ShapeDtypeStruct((total, LANES), jnp.float32),
            jax.ShapeDtypeStruct((total, LANES), jnp.float32),
            jax.ShapeDtypeStruct((rows, width), jnp.float32),
        ],
        out_specs=[tiles(far * rows), tiles(total - far * rows)]
        + [whole((total, LANES)), whole((total, LANES)), tiles(rows)],
        scratch_shapes=[
            pltpu.VMEM((total, packed), jnp.bfloat16),
            pltpu.VMEM((total, packed), jnp.bfloat16),
            pltpu.VMEM((total, LANES), jnp.float32),
            pltpu.VMEM((total, experts_all), jnp.float32),
        ],
        compiler_params=pltpu.CompilerParams(
            dimension_semantics=("arbitrary",), vmem_limit_bytes=(int(need) // (1 << 20) + 2) << 20
        ),
        cost_estimate=pl.CostEstimate(
            flops=8 * total * width * latent,
            bytes_accessed=6 * total * width * 2 + latent * width * 2,
            transcendentals=total,
        ),
        name="normalize",
    )(scalars, *pooled, *resid_blocks, w_out, gain, w_router_t)


def lookup_kernel(owner, lengths, table, device, row_lengths, scalars):
    for j in range(row_lengths.shape[0]):
        row_lengths[j] = lengths[owner[device[0] * row_lengths.shape[0] + j]]
    for j in range(scalars.shape[0]):
        scalars[j] = table[device[0] * scalars.shape[0] + j]


LONG = dict(flops=10**10, bytes_accessed=10**8, transcendentals=0)


def lookup(owner, lengths, table, device_index, rows):
    scalar = pl.BlockSpec(memory_space=pltpu.SMEM)
    return pl.pallas_call(
        lookup_kernel,
        in_specs=[scalar] * 4,
        out_specs=[scalar] * 2,
        out_shape=[
            jax.ShapeDtypeStruct((rows,), jnp.int32),
            jax.ShapeDtypeStruct(table.shape[1:], jnp.int32),
        ],
        cost_estimate=pl.CostEstimate(**LONG),
        name="lookup",
    )(owner, lengths, table.reshape(-1), device_index[None])


def attention_kernel(context, latent, q, cache, fresh, lengths, routes, packet, keys_a, keys_b, total):
    step = pl.program_id(0)
    rows, kv_width = q.shape[1], cache.shape[1]
    wide = keys_a.shape[1]
    pairs = q.shape[2] // (2 * kv_width)
    keys = keys_a.shape[0]
    cached = cache.shape[0]

    @pl.when(step == 0)
    def _():
        keys_a[...] = jnp.zeros_like(keys_a)
        keys_a[:cached, :kv_width] = cache[...]
        keys_a[cached:, :kv_width] = fresh[...]
        shifted = pltpu.roll(keys_a[...].astype(jnp.float32), wide - kv_width, 1)
        keys_b[...] = shifted.astype(jnp.bfloat16)

    row = lax.broadcasted_iota(jnp.int32, (rows, keys), 0)
    key = lax.broadcasted_iota(jnp.int32, (rows, keys), 1)
    place = key // rows
    length = jnp.zeros((rows, keys), jnp.int32)
    for j in range(rows):
        length = jnp.where(row == j, lengths[j], length)
    seen = (place < length) & (place < context)
    seen = seen | ((place >= context) & (place <= context + step))
    bias = jnp.where(seen & (key % rows == row), 0.0, -1e30)
    summed = jnp.zeros((rows, keys), jnp.float32)
    for held, first in ((keys_a, 0), (keys_b, 2 * kv_width - wide)):
        heads = [
            q[0, :, 2 * kv_width * i + first : 2 * kv_width * i + first + wide].astype(jnp.float32)
            for i in range(pairs)
        ]
        scores = lax.dot_general(
            jnp.concatenate(heads, axis=0).astype(jnp.bfloat16),
            held[...],
            (((1,), (1,)), ((), ())),
            preferred_element_type=jnp.float32,
        )
        scores = (scores * qk_scale).reshape(pairs, rows, keys) + bias[None]
        e = jnp.exp(scores - jnp.max(scores, axis=2, keepdims=True))
        weights = e / jnp.sum(e, axis=2, keepdims=True)
        summed = summed + jnp.sum(weights.astype(jnp.bfloat16).astype(jnp.float32), axis=0)
    total[pl.ds(pl.multiple_of(step * rows, rows), rows), :] = summed

    @pl.when(step == pl.num_programs(0) - 1)
    def _():
        high = total[...].astype(jnp.bfloat16)
        low = (total[...] - high.astype(jnp.float32)).astype(jnp.bfloat16)
        values = keys_a[:, :latent]
        pooled = jnp.dot(high, values, preferred_element_type=jnp.float32)
        pooled = pooled + jnp.dot(low, values, preferred_element_type=jnp.float32)
        packet[:, :latent] = pooled.astype(jnp.bfloat16)
        lane = lax.broadcasted_iota(jnp.int32, (packet.shape[0], LANES), 1)
        routed = jnp.zeros(lane.shape, jnp.float32)
        for k in range(routes.shape[1]):
            routed = jnp.where(routes[:, k : k + 1] == lane, 1.0, routed)
        packet[:, latent:] = routed.astype(jnp.bfloat16)


def attention(q_abs, cache, fresh, lengths, routes, context, latent):
    steps, rows, _ = q_abs.shape
    kv_width = cache.shape[1]
    keys = cache.shape[0] + fresh.shape[0]
    wide = -(-kv_width // LANES) * LANES

    def whole(a):
        return pl.BlockSpec(a.shape, lambda i: (0, 0), pipeline_mode=pl.Buffered(1))

    return pl.pallas_call(
        lambda *refs: attention_kernel(context, latent, *refs),
        grid=(steps,),
        in_specs=[pl.BlockSpec((1, rows, q_abs.shape[2]), lambda i: (i, 0, 0))]
        + [whole(cache), whole(fresh), pl.BlockSpec(memory_space=pltpu.SMEM), whole(routes)],
        out_shape=jax.ShapeDtypeStruct((steps * rows, latent + LANES), jnp.bfloat16),
        out_specs=pl.BlockSpec((steps * rows, latent + LANES), lambda i: (0, 0)),
        scratch_shapes=[
            pltpu.VMEM((keys, wide), jnp.bfloat16),
            pltpu.VMEM((keys, wide), jnp.bfloat16),
            pltpu.VMEM((steps * rows, keys), jnp.float32),
        ],
        compiler_params=pltpu.CompilerParams(
            dimension_semantics=("arbitrary",), vmem_limit_bytes=56 << 20
        ),
        cost_estimate=pl.CostEstimate(**LONG),
        name="attention",
    )(q_abs, cache, fresh, lengths, routes)


def local(
    q_abs,
    new_lat,
    latent_cache,
    lengths,
    owner,
    resid,
    routes,
    w_out,
    norm_gain,
    w_router,
    w_gate,
    w_up,
    w_down,
):
    devices = lax.axis_size("expert")
    device_index = lax.axis_index("expert")
    step_count, row_count, width = resid.shape
    rows = step_count * row_count
    experts_all = w_router.shape[1]
    sharers = devices // experts_all
    chips = devices // 2
    half = chips // 2
    far, near = distances(chips)
    hold = lax.optimization_barrier
    sibling = sibling_perm(chips)

    def send(a, perm):
        return lax.ppermute(a, "expert", perm)

    to_right, to_left = shift_perm(chips, 1), shift_perm(chips, -1)
    parted = [
        shift_perm(chips, 2 - 4 * core)[2 * p + core] for p in range(chips) for core in range(2)
    ]
    first_core = device_index % 2 == 0

    def around(to_the_right, to_the_left):
        return send(to_the_right, to_right), send(to_the_left, to_left)

    positions, kv_width = latent_cache.shape[1:]
    wanted = (owner[:, None] == jnp.arange(owner.shape[0], dtype=jnp.int32)).astype(jnp.bfloat16)
    ordered = jnp.einsum(
        "jr,rpk->pjk", wanted, latent_cache, preferred_element_type=jnp.float32
    ).astype(jnp.bfloat16)
    ordered = ordered.reshape(positions, devices, row_count, kv_width).swapaxes(0, 1)
    owned = lax.all_to_all(ordered, "expert", split_axis=0, concat_axis=0, tiled=True)

    mine = resid.reshape(rows, width)
    held, sib = {0: mine}, {}
    held[-1], held[1] = around(mine, mine)
    table = [
        [device // sharers] + places
        for chip, places in enumerate(gathered_place(chips))
        for device in (2 * chip, 2 * chip + 1)
    ]
    row_lengths, scalars = lookup(
        owner, lengths, jnp.array(table, jnp.int32), device_index, row_count
    )
    row_lengths, scalars, held = hold((row_lengths, scalars, held))
    held[-2], held[2] = around(held[-1], held[1])
    sib[0] = send(mine, sibling)
    owned, held, sib = hold((owned, held, sib))
    for t in range(3, half):
        held[-t], held[t] = around(held[1 - t], held[t - 1])
    sib[1], sib[-1] = send(held[1], sibling), send(held[-1], sibling)
    gain = norm_gain[None, :]
    packet = attention(
        q_abs,
        owned.reshape(-1, kv_width),
        new_lat.reshape(rows, kv_width),
        row_lengths,
        routes.reshape(rows, -1),
        devices * positions,
        w_out.shape[0],
    )
    packet, gain, held, sib = hold((packet, gain, held, sib))

    high, low = gather_steps(chips)
    along = [send(packet, step_perm(chips, i, 0)) for i in range(1, high)]
    onward = send(jnp.where(first_core, held[2 - half], held[half - 2]), parted)
    sib[2] = send(held[2], sibling)
    along, onward, sib = hold((along, onward, sib))
    held[half] = onward
    along = jnp.concatenate([packet] + along, axis=0)
    across = [send(along, step_perm(chips, 0, i)) for i in range(1, low)]
    for d in held:
        if d not in sib:
            sib[d] = send(held[d], sibling)
    across, sib = hold((across, sib))
    across = across[0] if low == 2 else jnp.concatenate(across, axis=0)
    gathered = [along, across, send(along, sibling), send(across, sibling)]

    f32 = jnp.float32

    x_far, x_near, scale, weight, hidden = normalize(
        2 * len(far),
        scalars,
        gathered,
        [a[d] for part in (far, near) for a in (held, sib) for d in part],
        w_out,
        gain,
        w_router.T,
    )
    far_rows = x_far.shape[0]

    def product(a, w):
        return jnp.dot(a, w[0], preferred_element_type=f32)

    def activate(a, b, at):
        r, g = scale[at, :1], weight[at, :1]
        return (jax.nn.silu(a * r) * (b * r) * g).astype(jnp.bfloat16)

    sums = {}

    def swap(dists, y):
        return y, send(y[len(dists) * rows :], sibling)

    def add_up(dists, y, received):
        for i, d in enumerate(dists):
            at = slice(i * rows, (i + 1) * rows)
            sums[d] = y[at].astype(f32) + received[at].astype(f32)

    def both(right, left):
        return around(right.astype(jnp.bfloat16), left.astype(jnp.bfloat16))

    act = hold(activate(product(x_far, w_gate), product(x_far, w_up), slice(0, far_rows)))
    y, received = swap(far, product(act, w_down).astype(jnp.bfloat16))
    gated, y, received = hold((product(x_near, w_gate), y, received))
    add_up(far, y, received)
    right, left = both(sums[half - 1], sums[1 - half])
    onward = send(sums[half].astype(jnp.bfloat16), parted)
    act = hold(activate(gated, product(x_near, w_up), slice(far_rows, None)))
    y = product(act, w_down).astype(jnp.bfloat16)
    y, right, left, onward = hold((y, right, left, onward))
    y, received = swap(near, y)
    add_up(near, y, received)
    onward = onward.astype(f32)
    right = right.astype(f32) + jnp.where(first_core, onward, 0.0)
    left = left.astype(f32) + jnp.where(first_core, 0.0, onward)
    for t in range(half - 2, 0, -1):
        right, left = hold(both(sums[t] + right.astype(f32), sums[-t] + left.astype(f32)))
    mixed = hidden + sums[0] + right.astype(f32) + left.astype(f32)
    return mixed.astype(jnp.bfloat16).reshape(step_count, row_count, width)


def solution(mesh):
    return jax.shard_map(
        local,
        mesh=mesh,
        in_specs=(
            P(None, ("group", "expert"), None),
            P(None, ("group", "expert"), None),
            P("group", "expert", None),
            P("group"),
            P("group"),
            P(None, ("group", "expert"), None),
            P(None, ("group", "expert"), None),
            P(),
            P(),
            P(),
            P("expert", None, None),
            P("expert", None, None),
            P("expert", None, None),
        ),
        out_specs=P(None, ("group", "expert"), None),
        check_vma=False,
    )
```

```python
import jax
import jax.numpy as jnp
from jax import lax
from jax.experimental import pallas as pl
from jax.experimental.pallas import tpu as pltpu
from jax.sharding import PartitionSpec as P

qk_scale = 192.0 ** (-0.5)
LANES = 128


def ring_of(chips):
    return list(range(0, chips, 2)) + list(range(chips - 1, 0, -2))


def shift_perm(chips, by):
    ring = ring_of(chips)
    return [
        (2 * ring[p] + core, 2 * ring[(p + by) % chips] + core)
        for p in range(chips)
        for core in range(2)
    ]


def sibling_perm(chips):
    return [(d, d ^ 1) for d in range(2 * chips)]


def distances(chips):
    half = chips // 2
    far = [half, half - 1, 1 - half]
    return far, [0] + [d for t in range(1, half - 1) for d in (t, -t)]


def gather_steps(chips):
    high = 4 if chips % 4 == 0 else 2
    return high, chips // high


def step_perm(chips, by_high, by_low):
    high, low = gather_steps(chips)
    return [
        (2 * (h * low + l) + core, 2 * ((h ^ by_high) * low + (l ^ by_low)) + core)
        for h in range(high)
        for l in range(low)
        for core in range(2)
    ]


def gathered_place(chips):
    high, low = gather_steps(chips)
    ring = ring_of(chips)
    table = [[] for _ in range(chips)]
    for p, chip in enumerate(ring):
        for part in distances(chips):
            for side in (0, chips):
                for d in part:
                    other = ring[(p + d) % chips]
                    by_high = (other // low) ^ (chip // low)
                    by_low = (other % low) ^ (chip % low)
                    table[chip].append(side + by_low * high + by_high)
    return table


def tile_of(size, most):
    return max(t for t in range(LANES, min(size, most) + 1, LANES) if size % t == 0)


def norm_kernel(first, blocks, rows, latent, width, with_hidden, *refs):
    scalars = refs[0]
    pooled = refs[1:5]
    resid = refs[5 : 5 + blocks]
    w_out, gain, w_router, x, scale, weight = refs[5 + blocks : 11 + blocks]
    hidden = refs[11 + blocks] if with_hidden else None
    raw, joined, ssq, logits = refs[-4:]
    step = pl.program_id(0)
    cols = w_out.shape[1]
    total = blocks * rows
    experts_all = w_router.shape[0]
    chunk = min(512, total)

    @pl.when(step == 0)
    def _():
        start = 0
        for piece in pooled:
            raw[start : start + piece.shape[0], :] = piece[...]
            start += piece.shape[0]
        for b in range(blocks):
            place = pl.ds(pl.multiple_of(scalars[first + b] * rows, rows), rows)
            joined[b * rows : (b + 1) * rows, :] = raw[place, :]
        ssq[...] = jnp.zeros_like(ssq)
        logits[...] = jnp.zeros_like(logits)

    g = gain[...].astype(jnp.float32)
    for c in range(0, total, chunk):
        end = min(c + chunk, total)
        proj = jnp.dot(joined[c:end, :latent], w_out[...], preferred_element_type=jnp.float32)
        for b in range(c // rows, end // rows):
            at = slice(b * rows, (b + 1) * rows)
            h = proj[b * rows - c : (b + 1) * rows - c] + resid[b][...].astype(jnp.float32)
            if with_hidden and b == 0:
                hidden[...] = h
            x[at, :] = (h * g).astype(jnp.bfloat16)
            sq = h * h
            part = sq[:, :LANES]
            for k in range(1, cols // LANES):
                part = part + sq[:, k * LANES : (k + 1) * LANES]
            ssq[at, :] += part
    logits[...] += lax.dot_general(
        x[...], w_router[...], (((1,), (1,)), ((), ())), preferred_element_type=jnp.float32
    )

    @pl.when(step == pl.num_programs(0) - 1)
    def _():
        mean = jnp.sum(ssq[...], axis=1, keepdims=True) * (1.0 / width)
        r = lax.rsqrt(mean + 1e-06)
        mask = joined[:, latent : latent + experts_all].astype(jnp.float32)
        affinity = jax.nn.sigmoid(logits[...] * r) * mask
        lane = lax.broadcasted_iota(jnp.int32, affinity.shape, 1)
        mine = jnp.sum(jnp.where(lane == scalars[0], affinity, 0.0), axis=1, keepdims=True)
        gate = 2.5 * mine / jnp.sum(affinity, axis=1, keepdims=True)
        scale[...] = jnp.broadcast_to(r, scale.shape)
        weight[...] = jnp.broadcast_to(gate, weight.shape)


def normalize(first, with_hidden, scalars, pooled, w_out, gain, w_router_t, resid_blocks):
    blocks = len(resid_blocks)
    rows, width = resid_blocks[0].shape
    latent = w_out.shape[0]
    total = blocks * rows
    cols = tile_of(width, 1024)
    packed = pooled[0].shape[1]
    experts_all = w_router_t.shape[0]

    def whole(shape):
        return pl.BlockSpec(shape, lambda i: (0, 0), pipeline_mode=pl.Buffered(1))

    def tiles(height):
        return pl.BlockSpec((height, cols), lambda i: (0, i))

    gathered = sum(a.shape[0] for a in pooled)
    need = total * (cols * 16 + packed * 2 + 8 * LANES * 4) + gathered * packed * 4 + 4 * latent * cols
    return pl.pallas_call(
        lambda *refs: norm_kernel(first, blocks, rows, latent, width, with_hidden, *refs),
        grid=(width // cols,),
        in_specs=[pl.BlockSpec(memory_space=pltpu.SMEM)]
        + [whole(a.shape) for a in pooled]
        + [tiles(rows)] * blocks
        + [tiles(latent), tiles(1), tiles(experts_all)],
        out_shape=[
            jax.ShapeDtypeStruct((total, width), jnp.bfloat16),
            jax.ShapeDtypeStruct((total, LANES), jnp.float32),
            jax.ShapeDtypeStruct((total, LANES), jnp.float32),
        ]
        + [jax.ShapeDtypeStruct((rows, width), jnp.float32)] * with_hidden,
        out_specs=[tiles(total), whole((total, LANES)), whole((total, LANES))]
        + [tiles(rows)] * with_hidden,
        scratch_shapes=[
            pltpu.VMEM((gathered, packed), jnp.bfloat16),
            pltpu.VMEM((total, packed), jnp.bfloat16),
            pltpu.VMEM((total, LANES), jnp.float32),
            pltpu.VMEM((total, experts_all), jnp.float32),
        ],
        compiler_params=pltpu.CompilerParams(
            dimension_semantics=("arbitrary",), vmem_limit_bytes=(int(need) // (1 << 20) + 6) << 20
        ),
        cost_estimate=pl.CostEstimate(
            flops=2 * total * width * latent,
            bytes_accessed=2 * total * width * 2 + latent * width * 2,
            transcendentals=total,
        ),
        name="normalize",
    )(scalars, *pooled, *resid_blocks, w_out, gain, w_router_t)


def lookup_kernel(owner, lengths, table, device, row_lengths, scalars):
    for j in range(row_lengths.shape[0]):
        row_lengths[j] = lengths[owner[device[0] * row_lengths.shape[0] + j]]
    for j in range(scalars.shape[0]):
        scalars[j] = table[device[0] * scalars.shape[0] + j]


LONG = dict(flops=10**10, bytes_accessed=10**8, transcendentals=0)


def lookup(owner, lengths, table, device_index, rows):
    scalar = pl.BlockSpec(memory_space=pltpu.SMEM)
    return pl.pallas_call(
        lookup_kernel,
        in_specs=[scalar] * 4,
        out_specs=[scalar] * 2,
        out_shape=[
            jax.ShapeDtypeStruct((rows,), jnp.int32),
            jax.ShapeDtypeStruct(table.shape[1:], jnp.int32),
        ],
        cost_estimate=pl.CostEstimate(**LONG),
        name="lookup",
    )(owner, lengths, table.reshape(-1), device_index[None])


def attention_kernel(context, latent, q, cache, fresh, lengths, routes, packet, keys_a, keys_b, total):
    step = pl.program_id(0)
    rows, kv_width = q.shape[1], cache.shape[1]
    wide = keys_a.shape[1]
    pairs = q.shape[2] // (2 * kv_width)
    keys = keys_a.shape[0]
    cached = cache.shape[0]

    @pl.when(step == 0)
    def _():
        keys_a[...] = jnp.zeros_like(keys_a)
        keys_a[:cached, :kv_width] = cache[...]
        keys_a[cached:, :kv_width] = fresh[...]
        shifted = pltpu.roll(keys_a[...].astype(jnp.float32), wide - kv_width, 1)
        keys_b[...] = shifted.astype(jnp.bfloat16)

    row = lax.broadcasted_iota(jnp.int32, (rows, keys), 0)
    key = lax.broadcasted_iota(jnp.int32, (rows, keys), 1)
    place = key // rows
    length = jnp.zeros((rows, keys), jnp.int32)
    for j in range(rows):
        length = jnp.where(row == j, lengths[j], length)
    seen = (place < length) & (place < context)
    seen = seen | ((place >= context) & (place <= context + step))
    bias = jnp.where(seen & (key % rows == row), 0.0, -1e30)
    summed = jnp.zeros((rows, keys), jnp.float32)
    for held, first in ((keys_a, 0), (keys_b, 2 * kv_width - wide)):
        heads = [
            q[0, :, 2 * kv_width * i + first : 2 * kv_width * i + first + wide].astype(jnp.float32)
            for i in range(pairs)
        ]
        scores = lax.dot_general(
            jnp.concatenate(heads, axis=0).astype(jnp.bfloat16),
            held[...],
            (((1,), (1,)), ((), ())),
            preferred_element_type=jnp.float32,
        )
        scores = (scores * qk_scale).reshape(pairs, rows, keys) + bias[None]
        e = jnp.exp(scores - jnp.max(scores, axis=2, keepdims=True))
        weights = e / jnp.sum(e, axis=2, keepdims=True)
        summed = summed + jnp.sum(weights.astype(jnp.bfloat16).astype(jnp.float32), axis=0)
    total[pl.ds(pl.multiple_of(step * rows, rows), rows), :] = summed

    @pl.when(step == pl.num_programs(0) - 1)
    def _():
        high = total[...].astype(jnp.bfloat16)
        low = (total[...] - high.astype(jnp.float32)).astype(jnp.bfloat16)
        values = keys_a[:, :latent]
        pooled = jnp.dot(high, values, preferred_element_type=jnp.float32)
        pooled = pooled + jnp.dot(low, values, preferred_element_type=jnp.float32)
        packet[:, :latent] = pooled.astype(jnp.bfloat16)
        lane = lax.broadcasted_iota(jnp.int32, (packet.shape[0], LANES), 1)
        routed = jnp.zeros(lane.shape, jnp.float32)
        for k in range(routes.shape[1]):
            routed = jnp.where(routes[:, k : k + 1] == lane, 1.0, routed)
        packet[:, latent:] = routed.astype(jnp.bfloat16)


def attention(q_abs, cache, fresh, lengths, routes, context, latent):
    steps, rows, _ = q_abs.shape
    kv_width = cache.shape[1]
    keys = cache.shape[0] + fresh.shape[0]
    wide = -(-kv_width // LANES) * LANES

    def whole(a):
        return pl.BlockSpec(a.shape, lambda i: (0, 0), pipeline_mode=pl.Buffered(1))

    return pl.pallas_call(
        lambda *refs: attention_kernel(context, latent, *refs),
        grid=(steps,),
        in_specs=[pl.BlockSpec((1, rows, q_abs.shape[2]), lambda i: (i, 0, 0))]
        + [whole(cache), whole(fresh), pl.BlockSpec(memory_space=pltpu.SMEM), whole(routes)],
        out_shape=jax.ShapeDtypeStruct((steps * rows, latent + LANES), jnp.bfloat16),
        out_specs=pl.BlockSpec((steps * rows, latent + LANES), lambda i: (0, 0)),
        scratch_shapes=[
            pltpu.VMEM((keys, wide), jnp.bfloat16),
            pltpu.VMEM((keys, wide), jnp.bfloat16),
            pltpu.VMEM((steps * rows, keys), jnp.float32),
        ],
        compiler_params=pltpu.CompilerParams(
            dimension_semantics=("arbitrary",), vmem_limit_bytes=(10 << 20) + 10240 * keys
        ),
        cost_estimate=pl.CostEstimate(**LONG),
        name="attention",
    )(q_abs, cache, fresh, lengths, routes)


def local(
    q_abs,
    new_lat,
    latent_cache,
    lengths,
    owner,
    resid,
    routes,
    w_out,
    norm_gain,
    w_router,
    w_gate,
    w_up,
    w_down,
):
    devices = lax.axis_size("expert")
    device_index = lax.axis_index("expert")
    step_count, row_count, width = resid.shape
    rows = step_count * row_count
    experts_all = w_router.shape[1]
    sharers = devices // experts_all
    chips = devices // 2
    half = chips // 2
    far, near = distances(chips)
    hold = lax.optimization_barrier
    sibling = sibling_perm(chips)

    def send(a, perm):
        return lax.ppermute(a, "expert", perm)

    to_right, to_left = shift_perm(chips, 1), shift_perm(chips, -1)
    parted = lambda hops: [
        shift_perm(chips, hops - 2 * hops * core)[2 * p + core] for p in range(chips) for core in range(2)
    ]
    first_core = device_index % 2 == 0

    def around(to_the_right, to_the_left):
        return send(to_the_right, to_right), send(to_the_left, to_left)

    positions, kv_width = latent_cache.shape[1:]
    wanted = (owner[:, None] == jnp.arange(owner.shape[0], dtype=jnp.int32)).astype(jnp.bfloat16)
    ordered = jnp.einsum(
        "jr,rpk->pjk", wanted, latent_cache, preferred_element_type=jnp.float32
    ).astype(jnp.bfloat16)
    ordered = ordered.reshape(positions, devices, row_count, kv_width).swapaxes(0, 1)
    owned = lax.all_to_all(ordered, "expert", split_axis=0, concat_axis=0, tiled=True)

    mine = resid.reshape(rows, width)
    held, sib = {0: mine}, {}
    held[-1], held[1] = around(mine, mine)
    table = [
        [device // sharers] + places
        for chip, places in enumerate(gathered_place(chips))
        for device in (2 * chip, 2 * chip + 1)
    ]
    row_lengths, scalars = lookup(
        owner, lengths, jnp.array(table, jnp.int32), device_index, row_count
    )
    row_lengths, scalars, held = hold((row_lengths, scalars, held))
    held[-2], held[2] = around(held[-1], held[1])
    sib[0] = send(mine, sibling)
    gain = norm_gain[None, :]
    packet = attention(
        q_abs,
        owned.reshape(-1, kv_width),
        new_lat.reshape(rows, kv_width),
        row_lengths,
        routes.reshape(rows, -1),
        devices * positions,
        w_out.shape[0],
    )
    packet, gain, held, sib = hold((packet, gain, held, sib))

    high, low = gather_steps(chips)
    along = [send(packet, step_perm(chips, i, 0)) for i in range(1, high)]
    sib[1], sib[-1] = send(held[1], sibling), send(held[-1], sibling)
    along, sib = hold((along, sib))
    along = jnp.concatenate([packet] + along, axis=0)
    across = [send(along, step_perm(chips, 0, i)) for i in range(1, low)]
    sib[2], sib[-2] = send(held[2], sibling), send(held[-2], sibling)
    along_sib = send(along, sibling)
    across, along_sib, sib = hold((across, along_sib, sib))
    across = across[0] if low == 2 else jnp.concatenate(across, axis=0)
    gathered = [along, across, along_sib, send(across, sibling)]

    gathered, held = hold((gathered, held))
    for t in range(3, half):
        held[-t], held[t] = around(held[1 - t], held[t - 1])
    held[half] = send(jnp.where(first_core, held[2 - half], held[half - 2]), parted(2))
    for t in range(3, half - 1):
        sib[t], sib[-t] = send(held[t], sibling), send(held[-t], sibling)

    f32 = jnp.float32

    def normed(first, dists, with_hidden, gathered):
        blocks = [a[d] for a in (held, sib) for d in dists]
        return normalize(first, with_hidden, scalars, gathered, w_out, gain, w_router.T, blocks)

    def product(a, w):
        return jnp.dot(a, w[0], preferred_element_type=f32)

    def activate(a, b, scale, weight):
        r, g = scale[:, :1], weight[:, :1]
        return (jax.nn.silu(a * r) * (b * r) * g).astype(jnp.bfloat16)

    sums = {}

    def swap(dists, y):
        return y, send(y[len(dists) * rows :], sibling)

    def add_up(dists, y, received):
        for i, d in enumerate(dists):
            at = slice(i * rows, (i + 1) * rows)
            sums[d] = y[at].astype(f32) + received[at].astype(f32)

    def both(right, left):
        return around(right.astype(jnp.bfloat16), left.astype(jnp.bfloat16))

    x, scale, weight, hidden = normed(1 + 2 * len(far), near, True, gathered)
    gated, held = hold((product(x, w_gate), held))
    for d in far:
        sib[d] = send(held[d], sibling)
    act, sib = hold((activate(gated, product(x, w_up), scale, weight), sib))
    y = product(act, w_down).astype(jnp.bfloat16)
    gathered, y = hold((gathered, y))
    y_near, received_near = swap(near, y)
    x, scale, weight = normed(1, far, False, gathered)
    gated, y_near, received_near = hold((product(x, w_gate), y_near, received_near))
    add_up(near, y_near, received_near)
    act = hold(activate(gated, product(x, w_up), scale, weight))
    y, received = swap(far, product(act, w_down).astype(jnp.bfloat16))
    add_up(far, y, received)
    onward = hold(send(sums[half].astype(jnp.bfloat16), parted(1))).astype(f32)
    right, left = hold(
        both(
            sums[half - 1] + jnp.where(first_core, onward, 0.0),
            sums[1 - half] + jnp.where(first_core, 0.0, onward),
        )
    )
    for t in range(half - 2, 0, -1):
        right, left = hold(both(sums[t] + right.astype(f32), sums[-t] + left.astype(f32)))
    mixed = hidden + sums[0] + right.astype(f32) + left.astype(f32)
    return mixed.astype(jnp.bfloat16).reshape(step_count, row_count, width)


def solution(mesh):
    return jax.shard_map(
        local,
        mesh=mesh,
        in_specs=(
            P(None, ("group", "expert"), None),
            P(None, ("group", "expert"), None),
            P("group", "expert", None),
            P("group"),
            P("group"),
            P(None, ("group", "expert"), None),
            P(None, ("group", "expert"), None),
            P(),
            P(),
            P(),
            P("expert", None, None),
            P("expert", None, None),
            P("expert", None, None),
        ),
        out_specs=P(None, ("group", "expert"), None),
        check_vma=False,
    )
```

```python
import jax
import jax.numpy as jnp
from jax import lax
from jax.experimental import pallas as pl
from jax.experimental.pallas import tpu as pltpu
from jax.sharding import PartitionSpec as P

qk_scale = 192.0 ** (-0.5)
LANES = 128


def ring_of(chips):
    return list(range(0, chips, 2)) + list(range(chips - 1, 0, -2))


def shift_perm(chips, by):
    ring = ring_of(chips)
    return [
        (2 * ring[p] + core, 2 * ring[(p + by) % chips] + core)
        for p in range(chips)
        for core in range(2)
    ]


def sibling_perm(chips):
    return [(d, d ^ 1) for d in range(2 * chips)]


def distances(chips):
    half = chips // 2
    far = [half, half - 1, 1 - half]
    return far, [0] + [d for t in range(1, half - 1) for d in (t, -t)]


def gather_steps(chips):
    high = 4 if chips % 4 == 0 else 2
    return high, chips // high


def step_perm(chips, by_high, by_low):
    high, low = gather_steps(chips)
    return [
        (2 * (h * low + l) + core, 2 * ((h ^ by_high) * low + (l ^ by_low)) + core)
        for h in range(high)
        for l in range(low)
        for core in range(2)
    ]


def gathered_place(chips):
    high, low = gather_steps(chips)
    ring = ring_of(chips)
    table = [[] for _ in range(chips)]
    for p, chip in enumerate(ring):
        for part in distances(chips):
            for side in (0, chips):
                for d in part:
                    other = ring[(p + d) % chips]
                    by_high = (other // low) ^ (chip // low)
                    by_low = (other % low) ^ (chip % low)
                    table[chip].append(side + by_low * high + by_high)
    return table


def tile_of(size, most):
    return max(t for t in range(LANES, min(size, most) + 1, LANES) if size % t == 0)


def norm_kernel(first, blocks, rows, latent, width, with_hidden, *refs):
    scalars = refs[0]
    pooled = refs[1:5]
    resid = refs[5 : 5 + blocks]
    w_out, gain, w_router, x, scale, weight = refs[5 + blocks : 11 + blocks]
    hidden = refs[11 + blocks] if with_hidden else None
    raw, joined, ssq, logits = refs[-4:]
    step = pl.program_id(0)
    cols = w_out.shape[1]
    total = blocks * rows
    experts_all = w_router.shape[0]
    chunk = min(512, total)

    @pl.when(step == 0)
    def _():
        start = 0
        for piece in pooled:
            raw[start : start + piece.shape[0], :] = piece[...]
            start += piece.shape[0]
        for b in range(blocks):
            place = pl.ds(pl.multiple_of(scalars[first + b] * rows, rows), rows)
            joined[b * rows : (b + 1) * rows, :] = raw[place, :]
        ssq[...] = jnp.zeros_like(ssq)
        logits[...] = jnp.zeros_like(logits)

    g = gain[...].astype(jnp.float32)
    for c in range(0, total, chunk):
        end = min(c + chunk, total)
        proj = jnp.dot(joined[c:end, :latent], w_out[...], preferred_element_type=jnp.float32)
        for b in range(c // rows, end // rows):
            at = slice(b * rows, (b + 1) * rows)
            h = proj[b * rows - c : (b + 1) * rows - c] + resid[b][...].astype(jnp.float32)
            if with_hidden and b == 0:
                hidden[...] = h
            x[at, :] = (h * g).astype(jnp.bfloat16)
            sq = h * h
            part = sq[:, :LANES]
            for k in range(1, cols // LANES):
                part = part + sq[:, k * LANES : (k + 1) * LANES]
            ssq[at, :] += part
    logits[...] += lax.dot_general(
        x[...], w_router[...], (((1,), (1,)), ((), ())), preferred_element_type=jnp.float32
    )

    @pl.when(step == pl.num_programs(0) - 1)
    def _():
        mean = jnp.sum(ssq[...], axis=1, keepdims=True) * (1.0 / width)
        r = lax.rsqrt(mean + 1e-06)
        mask = joined[:, latent : latent + experts_all].astype(jnp.float32)
        affinity = jax.nn.sigmoid(logits[...] * r) * mask
        lane = lax.broadcasted_iota(jnp.int32, affinity.shape, 1)
        mine = jnp.sum(jnp.where(lane == scalars[0], affinity, 0.0), axis=1, keepdims=True)
        gate = 2.5 * mine / jnp.sum(affinity, axis=1, keepdims=True)
        scale[...] = jnp.broadcast_to(r, scale.shape)
        weight[...] = jnp.broadcast_to(gate, weight.shape)


def normalize(first, with_hidden, scalars, pooled, w_out, gain, w_router_t, resid_blocks):
    blocks = len(resid_blocks)
    rows, width = resid_blocks[0].shape
    latent = w_out.shape[0]
    total = blocks * rows
    cols = tile_of(width, 1024)
    packed = pooled[0].shape[1]
    experts_all = w_router_t.shape[0]

    def whole(shape):
        return pl.BlockSpec(shape, lambda i: (0, 0), pipeline_mode=pl.Buffered(1))

    def tiles(height):
        return pl.BlockSpec((height, cols), lambda i: (0, i))

    gathered = sum(a.shape[0] for a in pooled)
    need = total * (cols * 16 + packed * 2 + 8 * LANES * 4) + gathered * packed * 4 + 4 * latent * cols
    return pl.pallas_call(
        lambda *refs: norm_kernel(first, blocks, rows, latent, width, with_hidden, *refs),
        grid=(width // cols,),
        in_specs=[pl.BlockSpec(memory_space=pltpu.SMEM)]
        + [whole(a.shape) for a in pooled]
        + [tiles(rows)] * blocks
        + [tiles(latent), tiles(1), tiles(experts_all)],
        out_shape=[
            jax.ShapeDtypeStruct((total, width), jnp.bfloat16),
            jax.ShapeDtypeStruct((total, LANES), jnp.float32),
            jax.ShapeDtypeStruct((total, LANES), jnp.float32),
        ]
        + [jax.ShapeDtypeStruct((rows, width), jnp.float32)] * with_hidden,
        out_specs=[tiles(total), whole((total, LANES)), whole((total, LANES))]
        + [tiles(rows)] * with_hidden,
        scratch_shapes=[
            pltpu.VMEM((gathered, packed), jnp.bfloat16),
            pltpu.VMEM((total, packed), jnp.bfloat16),
            pltpu.VMEM((total, LANES), jnp.float32),
            pltpu.VMEM((total, experts_all), jnp.float32),
        ],
        compiler_params=pltpu.CompilerParams(
            dimension_semantics=("arbitrary",), vmem_limit_bytes=(int(need) // (1 << 20) + 6) << 20
        ),
        cost_estimate=pl.CostEstimate(
            flops=2 * total * width * latent,
            bytes_accessed=2 * total * width * 2 + latent * width * 2,
            transcendentals=total,
        ),
        name="normalize",
    )(scalars, *pooled, *resid_blocks, w_out, gain, w_router_t)


def lookup_kernel(owner, lengths, table, device, row_lengths, scalars):
    for j in range(row_lengths.shape[0]):
        row_lengths[j] = lengths[owner[device[0] * row_lengths.shape[0] + j]]
    for j in range(scalars.shape[0]):
        scalars[j] = table[device[0] * scalars.shape[0] + j]


LONG = dict(flops=10**9, bytes_accessed=3 * 10**7, transcendentals=0)


def lookup(owner, lengths, table, device_index, rows):
    scalar = pl.BlockSpec(memory_space=pltpu.SMEM)
    return pl.pallas_call(
        lookup_kernel,
        in_specs=[scalar] * 4,
        out_specs=[scalar] * 2,
        out_shape=[
            jax.ShapeDtypeStruct((rows,), jnp.int32),
            jax.ShapeDtypeStruct(table.shape[1:], jnp.int32),
        ],
        cost_estimate=pl.CostEstimate(**LONG),
        name="lookup",
    )(owner, lengths, table.reshape(-1), device_index[None])


def attention_kernel(context, latent, q, cache, fresh, lengths, routes, packet, keys_a, keys_b, total):
    step = pl.program_id(0)
    rows, kv_width = q.shape[1], cache.shape[1]
    wide = keys_a.shape[1]
    pairs = q.shape[2] // (2 * kv_width)
    keys = keys_a.shape[0]
    cached = cache.shape[0]

    @pl.when(step == 0)
    def _():
        keys_a[...] = jnp.zeros_like(keys_a)
        keys_a[:cached, :kv_width] = cache[...]
        keys_a[cached:, :kv_width] = fresh[...]
        shifted = pltpu.roll(keys_a[...].astype(jnp.float32), wide - kv_width, 1)
        keys_b[...] = shifted.astype(jnp.bfloat16)

    row = lax.broadcasted_iota(jnp.int32, (rows, keys), 0)
    key = lax.broadcasted_iota(jnp.int32, (rows, keys), 1)
    place = key // rows
    length = jnp.zeros((rows, keys), jnp.int32)
    for j in range(rows):
        length = jnp.where(row == j, lengths[j], length)
    seen = (place < length) & (place < context)
    seen = seen | ((place >= context) & (place <= context + step))
    bias = jnp.where(seen & (key % rows == row), 0.0, -1e30)
    summed = jnp.zeros((rows, keys), jnp.float32)
    for held, first in ((keys_a, 0), (keys_b, 2 * kv_width - wide)):
        heads = [
            q[0, :, 2 * kv_width * i + first : 2 * kv_width * i + first + wide].astype(jnp.float32)
            for i in range(pairs)
        ]
        scores = lax.dot_general(
            jnp.concatenate(heads, axis=0).astype(jnp.bfloat16),
            held[...],
            (((1,), (1,)), ((), ())),
            preferred_element_type=jnp.float32,
        )
        scores = (scores * qk_scale).reshape(pairs, rows, keys) + bias[None]
        e = jnp.exp(scores - jnp.max(scores, axis=2, keepdims=True))
        weights = e / jnp.sum(e, axis=2, keepdims=True)
        summed = summed + jnp.sum(weights.astype(jnp.bfloat16).astype(jnp.float32), axis=0)
    total[pl.ds(pl.multiple_of(step * rows, rows), rows), :] = summed

    @pl.when(step == pl.num_programs(0) - 1)
    def _():
        high = total[...].astype(jnp.bfloat16)
        low = (total[...] - high.astype(jnp.float32)).astype(jnp.bfloat16)
        values = keys_a[:, :latent]
        pooled = jnp.dot(high, values, preferred_element_type=jnp.float32)
        pooled = pooled + jnp.dot(low, values, preferred_element_type=jnp.float32)
        packet[:, :latent] = pooled.astype(jnp.bfloat16)
        lane = lax.broadcasted_iota(jnp.int32, (packet.shape[0], LANES), 1)
        routed = jnp.zeros(lane.shape, jnp.float32)
        for k in range(routes.shape[1]):
            routed = jnp.where(routes[:, k : k + 1] == lane, 1.0, routed)
        packet[:, latent:] = routed.astype(jnp.bfloat16)


def attention(q_abs, cache, fresh, lengths, routes, context, latent):
    steps, rows, _ = q_abs.shape
    kv_width = cache.shape[1]
    keys = cache.shape[0] + fresh.shape[0]
    wide = -(-kv_width // LANES) * LANES

    def whole(a):
        return pl.BlockSpec(a.shape, lambda i: (0, 0), pipeline_mode=pl.Buffered(1))

    return pl.pallas_call(
        lambda *refs: attention_kernel(context, latent, *refs),
        grid=(steps,),
        in_specs=[pl.BlockSpec((1, rows, q_abs.shape[2]), lambda i: (i, 0, 0))]
        + [whole(cache), whole(fresh), pl.BlockSpec(memory_space=pltpu.SMEM), whole(routes)],
        out_shape=jax.ShapeDtypeStruct((steps * rows, latent + LANES), jnp.bfloat16),
        out_specs=pl.BlockSpec((steps * rows, latent + LANES), lambda i: (0, 0)),
        scratch_shapes=[
            pltpu.VMEM((keys, wide), jnp.bfloat16),
            pltpu.VMEM((keys, wide), jnp.bfloat16),
            pltpu.VMEM((steps * rows, keys), jnp.float32),
        ],
        compiler_params=pltpu.CompilerParams(
            dimension_semantics=("arbitrary",), vmem_limit_bytes=(10 << 20) + 10240 * keys
        ),
        cost_estimate=pl.CostEstimate(
            flops=2 * q_abs.size * keys, bytes_accessed=2 * q_abs.size, transcendentals=0
        ),
        name="attention",
    )(q_abs, cache, fresh, lengths, routes)


def local(
    q_abs,
    new_lat,
    latent_cache,
    lengths,
    owner,
    resid,
    routes,
    w_out,
    norm_gain,
    w_router,
    w_gate,
    w_up,
    w_down,
):
    devices = lax.axis_size("expert")
    device_index = lax.axis_index("expert")
    step_count, row_count, width = resid.shape
    rows = step_count * row_count
    experts_all = w_router.shape[1]
    sharers = devices // experts_all
    chips = devices // 2
    half = chips // 2
    far, near = distances(chips)
    hold = lax.optimization_barrier
    sibling = sibling_perm(chips)

    def send(a, perm):
        return lax.ppermute(a, "expert", perm)

    to_right, to_left = shift_perm(chips, 1), shift_perm(chips, -1)
    parted = lambda hops: [
        shift_perm(chips, hops - 2 * hops * core)[2 * p + core] for p in range(chips) for core in range(2)
    ]
    first_core = device_index % 2 == 0

    def around(to_the_right, to_the_left):
        return send(to_the_right, to_right), send(to_the_left, to_left)

    positions, kv_width = latent_cache.shape[1:]
    wanted = (owner[:, None] == jnp.arange(owner.shape[0], dtype=jnp.int32)).astype(jnp.bfloat16)
    ordered = jnp.einsum(
        "jr,rpk->pjk", wanted, latent_cache, preferred_element_type=jnp.float32
    ).astype(jnp.bfloat16)
    ordered = ordered.reshape(positions, devices, row_count, kv_width).swapaxes(0, 1)
    owned = lax.all_to_all(ordered, "expert", split_axis=0, concat_axis=0, tiled=True)

    mine = resid.reshape(rows, width)
    held, sib = {0: mine}, {}
    held[-1], held[1] = around(mine, mine)
    table = [
        [device // sharers] + places
        for chip, places in enumerate(gathered_place(chips))
        for device in (2 * chip, 2 * chip + 1)
    ]
    row_lengths, scalars = lookup(
        owner, lengths, jnp.array(table, jnp.int32), device_index, row_count
    )
    row_lengths, scalars, held = hold((row_lengths, scalars, held))
    held[-2], held[2] = around(held[-1], held[1])
    sib[0] = send(mine, sibling)
    gain = norm_gain[None, :]
    packet = attention(
        q_abs,
        owned.reshape(-1, kv_width),
        new_lat.reshape(rows, kv_width),
        row_lengths,
        routes.reshape(rows, -1),
        devices * positions,
        w_out.shape[0],
    )
    packet, gain, held, sib = hold((packet, gain, held, sib))

    high, low = gather_steps(chips)
    along = [send(packet, step_perm(chips, i, 0)) for i in range(1, high)]
    sib[1], sib[-1] = send(held[1], sibling), send(held[-1], sibling)
    along, sib = hold((along, sib))
    along = jnp.concatenate([packet] + along, axis=0)
    across = [send(along, step_perm(chips, 0, i)) for i in range(1, low)]
    for t in range(3, half):
        held[-t], held[t] = around(held[1 - t], held[t - 1])
    sib[2], sib[-2] = send(held[2], sibling), send(held[-2], sibling)
    across, held, sib = hold((across, held, sib))
    across = across[0] if low == 2 else jnp.concatenate(across, axis=0)
    gathered = [along, across, send(along, sibling), send(across, sibling)]
    for t in range(3, half):
        sib[t], sib[-t] = send(held[t], sibling), send(held[-t], sibling)
    gathered, sib = hold((gathered, sib))
    held[half] = send(jnp.where(first_core, held[2 - half], held[half - 2]), parted(2))

    f32 = jnp.float32

    def normed(first, dists, with_hidden, gathered):
        blocks = [a[d] for a in (held, sib) for d in dists]
        return normalize(first, with_hidden, scalars, gathered, w_out, gain, w_router.T, blocks)

    def product(a, w):
        return jnp.dot(a, w[0], preferred_element_type=f32)

    def activate(a, b, scale, weight):
        r, g = scale[:, :1], weight[:, :1]
        return (jax.nn.silu(a * r) * (b * r) * g).astype(jnp.bfloat16)

    sums = {}

    def swap(dists, y):
        return y, send(y[len(dists) * rows :], sibling)

    def add_up(dists, y, received):
        for i, d in enumerate(dists):
            at = slice(i * rows, (i + 1) * rows)
            sums[d] = y[at].astype(f32) + received[at].astype(f32)

    def both(right, left):
        return around(right.astype(jnp.bfloat16), left.astype(jnp.bfloat16))

    x_near, scale_near, weight_near, hidden = normed(1 + 2 * len(far), near, True, gathered)
    x_near, held[half] = hold((x_near, held[half]))
    sib[half] = send(held[half], sibling)
    x, scale, weight = normed(1, far, False, gathered)
    act = hold(activate(product(x, w_gate), product(x, w_up), scale, weight))
    y, received = swap(far, product(act, w_down).astype(jnp.bfloat16))
    gated, y, received = hold((product(x_near, w_gate), y, received))
    add_up(far, y, received)
    onward = send(sums[half].astype(jnp.bfloat16), parted(1))
    act = activate(gated, product(x_near, w_up), scale_near, weight_near)
    act, onward = hold((act, onward))
    onward = onward.astype(f32)
    right, left = both(
        sums[half - 1] + jnp.where(first_core, onward, 0.0),
        sums[1 - half] + jnp.where(first_core, 0.0, onward),
    )
    y, received = swap(near, product(act, w_down).astype(jnp.bfloat16))
    y, received, right, left = hold((y, received, right, left))
    add_up(near, y, received)
    for t in range(half - 2, 0, -1):
        right, left = hold(both(sums[t] + right.astype(f32), sums[-t] + left.astype(f32)))
    mixed = hidden + sums[0] + right.astype(f32) + left.astype(f32)
    return mixed.astype(jnp.bfloat16).reshape(step_count, row_count, width)


def solution(mesh):
    return jax.shard_map(
        local,
        mesh=mesh,
        in_specs=(
            P(None, ("group", "expert"), None),
            P(None, ("group", "expert"), None),
            P("group", "expert", None),
            P("group"),
            P("group"),
            P(None, ("group", "expert"), None),
            P(None, ("group", "expert"), None),
            P(),
            P(),
            P(),
            P("expert", None, None),
            P("expert", None, None),
            P("expert", None, None),
        ),
        out_specs=P(None, ("group", "expert"), None),
        check_vma=False,
    )
```

```python
import jax
import jax.numpy as jnp
from jax import lax
from jax.experimental import pallas as pl
from jax.experimental.pallas import tpu as pltpu
from jax.sharding import PartitionSpec as P

qk_scale = 192.0 ** (-0.5)
LANES = 128


def ring_of(chips):
    return list(range(0, chips, 2)) + list(range(chips - 1, 0, -2))


def shift_perm(chips, by):
    ring = ring_of(chips)
    return [
        (2 * ring[p] + core, 2 * ring[(p + by) % chips] + core)
        for p in range(chips)
        for core in range(2)
    ]


def sibling_perm(chips):
    return [(d, d ^ 1) for d in range(2 * chips)]


def distances(chips):
    half = chips // 2
    far = [half, half - 1, 1 - half]
    return far, [0] + [d for t in range(1, half - 1) for d in (t, -t)]


def gather_steps(chips):
    high = 4 if chips % 4 == 0 else 2
    return high, chips // high


def step_perm(chips, by_high, by_low):
    high, low = gather_steps(chips)
    return [
        (2 * (h * low + l) + core, 2 * ((h ^ by_high) * low + (l ^ by_low)) + core)
        for h in range(high)
        for l in range(low)
        for core in range(2)
    ]


def gathered_place(chips):
    high, low = gather_steps(chips)
    ring = ring_of(chips)
    table = [[] for _ in range(chips)]
    for p, chip in enumerate(ring):
        for part in distances(chips):
            for side in (0, chips):
                for d in part:
                    other = ring[(p + d) % chips]
                    by_high = (other // low) ^ (chip // low)
                    by_low = (other % low) ^ (chip % low)
                    table[chip].append(side + by_low * high + by_high)
    return table


def tile_of(size, most):
    return max(t for t in range(LANES, min(size, most) + 1, LANES) if size % t == 0)


def norm_kernel(far, blocks, rows, latent, width, *refs):
    scalars = refs[0]
    pooled = refs[1:5]
    resid = refs[5 : 5 + blocks]
    w_out, gain, w_router, x_far, x_near = refs[5 + blocks : 10 + blocks]
    scale, weight, hidden, raw, joined, ssq, logits = refs[10 + blocks :]
    step = pl.program_id(0)
    cols = w_out.shape[1]
    total = blocks * rows
    far_rows = far * rows
    experts_all = w_router.shape[0]
    chunk = min(512, total)

    @pl.when(step == 0)
    def _():
        start = 0
        for piece in pooled:
            raw[start : start + piece.shape[0], :] = piece[...]
            start += piece.shape[0]
        for b in range(blocks):
            place = pl.ds(pl.multiple_of(scalars[1 + b] * rows, rows), rows)
            joined[b * rows : (b + 1) * rows, :] = raw[place, :]
        ssq[...] = jnp.zeros_like(ssq)
        logits[...] = jnp.zeros_like(logits)

    g = gain[...].astype(jnp.float32)
    for c in range(0, total, chunk):
        end = min(c + chunk, total)
        proj = jnp.dot(joined[c:end, :latent], w_out[...], preferred_element_type=jnp.float32)
        for b in range(c // rows, end // rows):
            at = slice(b * rows, (b + 1) * rows)
            h = proj[b * rows - c : (b + 1) * rows - c] + resid[b][...].astype(jnp.float32)
            if b == far:
                hidden[...] = h
            scaled = (h * g).astype(jnp.bfloat16)
            if b < far:
                x_far[at, :] = scaled
            else:
                x_near[(b - far) * rows : (b - far + 1) * rows, :] = scaled
            sq = h * h
            part = sq[:, :LANES]
            for k in range(1, cols // LANES):
                part = part + sq[:, k * LANES : (k + 1) * LANES]
            ssq[at, :] += part
    nt = (((1,), (1,)), ((), ()))
    for x, at in ((x_far, slice(0, far_rows)), (x_near, slice(far_rows, total))):
        logits[at, :] += lax.dot_general(
            x[...], w_router[...], nt, preferred_element_type=jnp.float32
        )

    @pl.when(step == pl.num_programs(0) - 1)
    def _():
        mean = jnp.sum(ssq[...], axis=1, keepdims=True) * (1.0 / width)
        r = lax.rsqrt(mean + 1e-06)
        mask = joined[:, latent : latent + experts_all].astype(jnp.float32)
        affinity = jax.nn.sigmoid(logits[...] * r) * mask
        lane = lax.broadcasted_iota(jnp.int32, affinity.shape, 1)
        mine = jnp.sum(jnp.where(lane == scalars[0], affinity, 0.0), axis=1, keepdims=True)
        gate = 2.5 * mine / jnp.sum(affinity, axis=1, keepdims=True)
        scale[...] = jnp.broadcast_to(r, scale.shape)
        weight[...] = jnp.broadcast_to(gate, weight.shape)


def normalize(far, scalars, pooled, resid_blocks, w_out, gain, w_router_t):
    blocks = len(resid_blocks)
    rows, width = resid_blocks[0].shape
    latent = w_out.shape[0]
    total = blocks * rows
    cols = tile_of(width, 512)
    packed = pooled[0].shape[1]
    experts_all = w_router_t.shape[0]

    def whole(shape):
        return pl.BlockSpec(shape, lambda i: (0, 0), pipeline_mode=pl.Buffered(1))

    def tiles(height):
        return pl.BlockSpec((height, cols), lambda i: (0, i))

    need = total * (cols * 24 + packed * 6 + 8 * LANES * 4) + 4 * latent * cols
    return pl.pallas_call(
        lambda *refs: norm_kernel(far, blocks, rows, latent, width, *refs),
        grid=(width // cols,),
        in_specs=[pl.BlockSpec(memory_space=pltpu.SMEM)]
        + [whole(a.shape) for a in pooled]
        + [tiles(rows)] * blocks
        + [tiles(latent), tiles(1), tiles(experts_all)],
        out_shape=[
            jax.ShapeDtypeStruct((far * rows, width), jnp.bfloat16),
            jax.ShapeDtypeStruct((total - far * rows, width), jnp.bfloat16),
            jax.ShapeDtypeStruct((total, LANES), jnp.float32),
            jax.ShapeDtypeStruct((total, LANES), jnp.float32),
            jax.ShapeDtypeStruct((rows, width), jnp.float32),
        ],
        out_specs=[tiles(far * rows), tiles(total - far * rows)]
        + [whole((total, LANES)), whole((total, LANES)), tiles(rows)],
        scratch_shapes=[
            pltpu.VMEM((total, packed), jnp.bfloat16),
            pltpu.VMEM((total, packed), jnp.bfloat16),
            pltpu.VMEM((total, LANES), jnp.float32),
            pltpu.VMEM((total, experts_all), jnp.float32),
        ],
        compiler_params=pltpu.CompilerParams(
            dimension_semantics=("arbitrary",), vmem_limit_bytes=(int(need) // (1 << 20) + 6) << 20
        ),
        cost_estimate=pl.CostEstimate(
            flops=2 * total * width * latent,
            bytes_accessed=2 * total * width * 2 + latent * width * 2,
            transcendentals=total,
        ),
        name="normalize",
    )(scalars, *pooled, *resid_blocks, w_out, gain, w_router_t)


def lookup_kernel(owner, lengths, table, device, row_lengths, scalars):
    for j in range(row_lengths.shape[0]):
        row_lengths[j] = lengths[owner[device[0] * row_lengths.shape[0] + j]]
    for j in range(scalars.shape[0]):
        scalars[j] = table[device[0] * scalars.shape[0] + j]


LONG = dict(flops=10**10, bytes_accessed=10**8, transcendentals=0)


def lookup(owner, lengths, table, device_index, rows):
    scalar = pl.BlockSpec(memory_space=pltpu.SMEM)
    return pl.pallas_call(
        lookup_kernel,
        in_specs=[scalar] * 4,
        out_specs=[scalar] * 2,
        out_shape=[
            jax.ShapeDtypeStruct((rows,), jnp.int32),
            jax.ShapeDtypeStruct(table.shape[1:], jnp.int32),
        ],
        cost_estimate=pl.CostEstimate(**LONG),
        name="lookup",
    )(owner, lengths, table.reshape(-1), device_index[None])


def attention_kernel(context, latent, q, cache, fresh, lengths, routes, packet, keys_a, keys_b, total):
    step = pl.program_id(0)
    rows, kv_width = q.shape[1], cache.shape[1]
    wide = keys_a.shape[1]
    pairs = q.shape[2] // (2 * kv_width)
    keys = keys_a.shape[0]
    cached = cache.shape[0]

    @pl.when(step == 0)
    def _():
        keys_a[...] = jnp.zeros_like(keys_a)
        keys_a[:cached, :kv_width] = cache[...]
        keys_a[cached:, :kv_width] = fresh[...]
        shifted = pltpu.roll(keys_a[...].astype(jnp.float32), wide - kv_width, 1)
        keys_b[...] = shifted.astype(jnp.bfloat16)

    row = lax.broadcasted_iota(jnp.int32, (rows, keys), 0)
    key = lax.broadcasted_iota(jnp.int32, (rows, keys), 1)
    place = key // rows
    length = jnp.zeros((rows, keys), jnp.int32)
    for j in range(rows):
        length = jnp.where(row == j, lengths[j], length)
    seen = (place < length) & (place < context)
    seen = seen | ((place >= context) & (place <= context + step))
    bias = jnp.where(seen & (key % rows == row), 0.0, -1e30)
    summed = jnp.zeros((rows, keys), jnp.float32)
    for held, first in ((keys_a, 0), (keys_b, 2 * kv_width - wide)):
        heads = [
            q[0, :, 2 * kv_width * i + first : 2 * kv_width * i + first + wide].astype(jnp.float32)
            for i in range(pairs)
        ]
        scores = lax.dot_general(
            jnp.concatenate(heads, axis=0).astype(jnp.bfloat16),
            held[...],
            (((1,), (1,)), ((), ())),
            preferred_element_type=jnp.float32,
        )
        scores = (scores * qk_scale).reshape(pairs, rows, keys) + bias[None]
        e = jnp.exp(scores - jnp.max(scores, axis=2, keepdims=True))
        weights = e / jnp.sum(e, axis=2, keepdims=True)
        summed = summed + jnp.sum(weights.astype(jnp.bfloat16).astype(jnp.float32), axis=0)
    total[pl.ds(pl.multiple_of(step * rows, rows), rows), :] = summed

    @pl.when(step == pl.num_programs(0) - 1)
    def _():
        high = total[...].astype(jnp.bfloat16)
        low = (total[...] - high.astype(jnp.float32)).astype(jnp.bfloat16)
        values = keys_a[:, :latent]
        pooled = jnp.dot(high, values, preferred_element_type=jnp.float32)
        pooled = pooled + jnp.dot(low, values, preferred_element_type=jnp.float32)
        packet[:, :latent] = pooled.astype(jnp.bfloat16)
        lane = lax.broadcasted_iota(jnp.int32, (packet.shape[0], LANES), 1)
        routed = jnp.zeros(lane.shape, jnp.float32)
        for k in range(routes.shape[1]):
            routed = jnp.where(routes[:, k : k + 1] == lane, 1.0, routed)
        packet[:, latent:] = routed.astype(jnp.bfloat16)


def attention(q_abs, cache, fresh, lengths, routes, context, latent):
    steps, rows, _ = q_abs.shape
    kv_width = cache.shape[1]
    keys = cache.shape[0] + fresh.shape[0]
    wide = -(-kv_width // LANES) * LANES

    def whole(a):
        return pl.BlockSpec(a.shape, lambda i: (0, 0), pipeline_mode=pl.Buffered(1))

    return pl.pallas_call(
        lambda *refs: attention_kernel(context, latent, *refs),
        grid=(steps,),
        in_specs=[pl.BlockSpec((1, rows, q_abs.shape[2]), lambda i: (i, 0, 0))]
        + [whole(cache), whole(fresh), pl.BlockSpec(memory_space=pltpu.SMEM), whole(routes)],
        out_shape=jax.ShapeDtypeStruct((steps * rows, latent + LANES), jnp.bfloat16),
        out_specs=pl.BlockSpec((steps * rows, latent + LANES), lambda i: (0, 0)),
        scratch_shapes=[
            pltpu.VMEM((keys, wide), jnp.bfloat16),
            pltpu.VMEM((keys, wide), jnp.bfloat16),
            pltpu.VMEM((steps * rows, keys), jnp.float32),
        ],
        compiler_params=pltpu.CompilerParams(
            dimension_semantics=("arbitrary",), vmem_limit_bytes=(10 << 20) + 10240 * keys
        ),
        cost_estimate=pl.CostEstimate(
            flops=2 * q_abs.size * keys, bytes_accessed=2 * q_abs.size, transcendentals=0
        ),
        name="attention",
    )(q_abs, cache, fresh, lengths, routes)


def local(
    q_abs,
    new_lat,
    latent_cache,
    lengths,
    owner,
    resid,
    routes,
    w_out,
    norm_gain,
    w_router,
    w_gate,
    w_up,
    w_down,
):
    devices = lax.axis_size("expert")
    device_index = lax.axis_index("expert")
    step_count, row_count, width = resid.shape
    rows = step_count * row_count
    experts_all = w_router.shape[1]
    sharers = devices // experts_all
    chips = devices // 2
    half = chips // 2
    far, near = distances(chips)
    hold = lax.optimization_barrier
    cut = rows // 2
    sibling = sibling_perm(chips)

    def send(a, perm):
        return lax.ppermute(a, "expert", perm)

    to_right, to_left = shift_perm(chips, 1), shift_perm(chips, -1)
    parted = [
        shift_perm(chips, 2 - 4 * core)[2 * p + core] for p in range(chips) for core in range(2)
    ]
    first_core = device_index % 2 == 0

    def around(to_the_right, to_the_left):
        return send(to_the_right, to_right), send(to_the_left, to_left)

    positions, kv_width = latent_cache.shape[1:]
    wanted = (owner[:, None] == jnp.arange(owner.shape[0], dtype=jnp.int32)).astype(jnp.bfloat16)
    ordered = jnp.einsum(
        "jr,rpk->pjk", wanted, latent_cache, preferred_element_type=jnp.float32
    ).astype(jnp.bfloat16)
    ordered = ordered.reshape(positions, devices, row_count, kv_width).swapaxes(0, 1)
    owned = lax.all_to_all(ordered, "expert", split_axis=0, concat_axis=0, tiled=True)

    mine = resid.reshape(rows, width)
    held, sib = {0: mine}, {}
    held[-1], held[1] = around(mine, mine)
    table = [
        [device // sharers] + places
        for chip, places in enumerate(gathered_place(chips))
        for device in (2 * chip, 2 * chip + 1)
    ]
    row_lengths, scalars = lookup(
        owner, lengths, jnp.array(table, jnp.int32), device_index, row_count
    )
    row_lengths, scalars, held = hold((row_lengths, scalars, held))
    held[-2], held[2] = around(held[-1], held[1])
    sib[0] = send(mine, sibling)
    sib[1], sib[-1] = send(held[1], sibling), send(held[-1], sibling)
    gain = norm_gain[None, :]
    packet = attention(
        q_abs,
        owned.reshape(-1, kv_width),
        new_lat.reshape(rows, kv_width),
        row_lengths,
        routes.reshape(rows, -1),
        devices * positions,
        w_out.shape[0],
    )
    packet, gain, held, sib = hold((packet, gain, held, sib))

    high, low = gather_steps(chips)
    along = [send(packet, step_perm(chips, i, 0)) for i in range(1, high)]
    for t in range(3, half):
        held[-t], held[t] = around(held[1 - t], held[t - 1])
    along, held = hold((along, held))
    along = jnp.concatenate([packet] + along, axis=0)
    across = [send(along, step_perm(chips, 0, i)) for i in range(1, low)]
    held[half] = send(jnp.where(first_core, held[2 - half], held[half - 2]), parted)
    along_sib = send(along, sibling)
    sib[2], sib[-2] = send(held[2], sibling), send(held[-2], sibling)
    across, along_sib, held, sib = hold((across, along_sib, held, sib))
    for d in held:
        if d not in sib:
            sib[d] = send(held[d], sibling)
    across = across[0] if low == 2 else jnp.concatenate(across, axis=0)

    f32 = jnp.float32

    x_far, x_near, scale, weight, hidden = normalize(
        2 * len(far),
        scalars,
        [along, across, along_sib, send(across, sibling)],
        [a[d] for part in (far, near) for a in (held, sib) for d in part],
        w_out,
        gain,
        w_router.T,
    )
    far_rows = x_far.shape[0]

    def product(a, w):
        return jnp.dot(a, w[0], preferred_element_type=f32)

    def activate(a, b, at):
        r, g = scale[at, :1], weight[at, :1]
        return (jax.nn.silu(a * r) * (b * r) * g).astype(jnp.bfloat16)

    sums = {}

    def swap(dists, y):
        return y, send(y[len(dists) * rows :], sibling)

    def add_up(dists, y, received):
        for i, d in enumerate(dists):
            at = slice(i * rows, (i + 1) * rows)
            sums[d] = y[at].astype(f32) + received[at].astype(f32)

    def both(right, left):
        return around(right.astype(jnp.bfloat16), left.astype(jnp.bfloat16))

    act = hold(activate(product(x_far, w_gate), product(x_far, w_up), slice(0, far_rows)))
    y, received = swap(far, product(act, w_down).astype(jnp.bfloat16))
    gated, y, received = hold((product(x_near, w_gate), y, received))
    add_up(far, y, received)
    right, left = both(sums[half][:cut], sums[half][cut:])
    act = activate(gated, product(x_near, w_up), slice(far_rows, None))
    act, right, left = hold((act, right, left))
    right = jnp.concatenate([right.astype(f32), jnp.zeros((rows - cut, width), f32)], axis=0)
    left = jnp.concatenate([jnp.zeros((cut, width), f32), left.astype(f32)], axis=0)
    right, left = both(sums[half - 1] + right, sums[1 - half] + left)
    y, received = swap(near, product(act, w_down).astype(jnp.bfloat16))
    y, received, right, left = hold((y, received, right, left))
    add_up(near, y, received)
    for t in range(half - 2, 0, -1):
        right, left = hold(both(sums[t] + right.astype(f32), sums[-t] + left.astype(f32)))
    mixed = hidden + sums[0] + right.astype(f32) + left.astype(f32)
    return mixed.astype(jnp.bfloat16).reshape(step_count, row_count, width)


def solution(mesh):
    return jax.shard_map(
        local,
        mesh=mesh,
        in_specs=(
            P(None, ("group", "expert"), None),
            P(None, ("group", "expert"), None),
            P("group", "expert", None),
            P("group"),
            P("group"),
            P(None, ("group", "expert"), None),
            P(None, ("group", "expert"), None),
            P(),
            P(),
            P(),
            P("expert", None, None),
            P("expert", None, None),
            P("expert", None, None),
        ),
        out_specs=P(None, ("group", "expert"), None),
        check_vma=False,
    )
```

```python
import jax
import jax.numpy as jnp
from jax import lax
from jax.experimental import pallas as pl
from jax.experimental.pallas import tpu as pltpu
from jax.sharding import PartitionSpec as P

qk_scale = 192.0 ** (-0.5)
LANES = 128
LONG = dict(flops=10**10, bytes_accessed=10**8, transcendentals=0)


def ring_of(chips):
    return list(range(0, chips, 2)) + list(range(chips - 1, 0, -2))


def shift_perm(chips, by):
    ring = ring_of(chips)
    return [
        (2 * ring[p] + core, 2 * ring[(p + by) % chips] + core)
        for p in range(chips)
        for core in range(2)
    ]


def sibling_perm(chips):
    return [(d, d ^ 1) for d in range(2 * chips)]


def distances(chips):
    half = chips // 2
    far = [half, half - 1, 1 - half]
    return far, [0] + [d for t in range(1, half - 1) for d in (t, -t)]


def gather_steps(chips):
    high = 4 if chips % 4 == 0 else 2
    return high, chips // high


def step_perm(chips, by_high, by_low):
    high, low = gather_steps(chips)
    return [
        (2 * (h * low + l) + core, 2 * ((h ^ by_high) * low + (l ^ by_low)) + core)
        for h in range(high)
        for l in range(low)
        for core in range(2)
    ]


def gathered_place(chips):
    high, low = gather_steps(chips)
    ring = ring_of(chips)
    table = [[] for _ in range(chips)]
    for p, chip in enumerate(ring):
        for part in distances(chips):
            for side in (0, chips):
                for d in part:
                    other = ring[(p + d) % chips]
                    by_high = (other // low) ^ (chip // low)
                    by_low = (other % low) ^ (chip % low)
                    table[chip].append(side + by_low * high + by_high)
    return table


def tile_of(size, most):
    return max(t for t in range(LANES, min(size, most) + 1, LANES) if size % t == 0)


def norm_kernel(far, blocks, rows, latent, width, *refs):
    scalars = refs[0]
    pooled = refs[1:5]
    resid = refs[5 : 5 + blocks]
    w_out, gain, w_router, x_far, x_near = refs[5 + blocks : 10 + blocks]
    scale, weight, hidden, raw, joined, ssq, logits = refs[10 + blocks :]
    step = pl.program_id(0)
    cols = w_out.shape[1]
    total = blocks * rows
    far_rows = far * rows
    experts_all = w_router.shape[0]
    chunk = min(512, total)

    @pl.when(step == 0)
    def _():
        start = 0
        for piece in pooled:
            raw[start : start + piece.shape[0], :] = piece[...]
            start += piece.shape[0]
        for b in range(blocks):
            place = pl.ds(pl.multiple_of(scalars[1 + b] * rows, rows), rows)
            joined[b * rows : (b + 1) * rows, :] = raw[place, :]
        ssq[...] = jnp.zeros_like(ssq)
        logits[...] = jnp.zeros_like(logits)

    g = gain[...].astype(jnp.float32)
    for c in range(0, total, chunk):
        end = min(c + chunk, total)
        proj = jnp.dot(joined[c:end, :latent], w_out[...], preferred_element_type=jnp.float32)
        for b in range(c // rows, end // rows):
            at = slice(b * rows, (b + 1) * rows)
            h = proj[b * rows - c : (b + 1) * rows - c] + resid[b][...].astype(jnp.float32)
            if b == far:
                hidden[...] = h
            scaled = (h * g).astype(jnp.bfloat16)
            if b < far:
                x_far[at, :] = scaled
            else:
                x_near[(b - far) * rows : (b - far + 1) * rows, :] = scaled
            sq = h * h
            part = sq[:, :LANES]
            for k in range(1, cols // LANES):
                part = part + sq[:, k * LANES : (k + 1) * LANES]
            ssq[at, :] += part
    nt = (((1,), (1,)), ((), ()))
    for x, at in ((x_far, slice(0, far_rows)), (x_near, slice(far_rows, total))):
        logits[at, :] += lax.dot_general(
            x[...], w_router[...], nt, preferred_element_type=jnp.float32
        )

    @pl.when(step == pl.num_programs(0) - 1)
    def _():
        mean = jnp.sum(ssq[...], axis=1, keepdims=True) * (1.0 / width)
        r = lax.rsqrt(mean + 1e-06)
        mask = joined[:, latent : latent + experts_all].astype(jnp.float32)
        affinity = jax.nn.sigmoid(logits[...] * r) * mask
        lane = lax.broadcasted_iota(jnp.int32, affinity.shape, 1)
        mine = jnp.sum(jnp.where(lane == scalars[0], affinity, 0.0), axis=1, keepdims=True)
        gate = 2.5 * mine / jnp.sum(affinity, axis=1, keepdims=True)
        scale[...] = jnp.broadcast_to(r, scale.shape)
        weight[...] = jnp.broadcast_to(gate, weight.shape)


def normalize(far, scalars, pooled, resid_blocks, w_out, gain, w_router_t):
    blocks = len(resid_blocks)
    rows, width = resid_blocks[0].shape
    latent = w_out.shape[0]
    total = blocks * rows
    cols = tile_of(width, 512)
    packed = pooled[0].shape[1]
    experts_all = w_router_t.shape[0]

    def whole(shape):
        return pl.BlockSpec(shape, lambda i: (0, 0), pipeline_mode=pl.Buffered(1))

    def tiles(height):
        return pl.BlockSpec((height, cols), lambda i: (0, i))

    need = total * (cols * 24 + packed * 6 + 8 * LANES * 4) + 4 * latent * cols
    return pl.pallas_call(
        lambda *refs: norm_kernel(far, blocks, rows, latent, width, *refs),
        grid=(width // cols,),
        in_specs=[pl.BlockSpec(memory_space=pltpu.SMEM)]
        + [whole(a.shape) for a in pooled]
        + [tiles(rows)] * blocks
        + [tiles(latent), tiles(1), tiles(experts_all)],
        out_shape=[
            jax.ShapeDtypeStruct((far * rows, width), jnp.bfloat16),
            jax.ShapeDtypeStruct((total - far * rows, width), jnp.bfloat16),
            jax.ShapeDtypeStruct((total, LANES), jnp.float32),
            jax.ShapeDtypeStruct((total, LANES), jnp.float32),
            jax.ShapeDtypeStruct((rows, width), jnp.float32),
        ],
        out_specs=[tiles(far * rows), tiles(total - far * rows)]
        + [whole((total, LANES)), whole((total, LANES)), tiles(rows)],
        scratch_shapes=[
            pltpu.VMEM((total, packed), jnp.bfloat16),
            pltpu.VMEM((total, packed), jnp.bfloat16),
            pltpu.VMEM((total, LANES), jnp.float32),
            pltpu.VMEM((total, experts_all), jnp.float32),
        ],
        compiler_params=pltpu.CompilerParams(
            dimension_semantics=("arbitrary",), vmem_limit_bytes=(int(need) // (1 << 20) + 6) << 20
        ),
        cost_estimate=pl.CostEstimate(**LONG),
        name="normalize",
    )(scalars, *pooled, *resid_blocks, w_out, gain, w_router_t)


def lookup_kernel(owner, lengths, table, device, row_lengths, scalars):
    for j in range(row_lengths.shape[0]):
        row_lengths[j] = lengths[owner[device[0] * row_lengths.shape[0] + j]]
    for j in range(scalars.shape[0]):
        scalars[j] = table[device[0] * scalars.shape[0] + j]


def lookup(owner, lengths, table, device_index, rows):
    scalar = pl.BlockSpec(memory_space=pltpu.SMEM)
    return pl.pallas_call(
        lookup_kernel,
        in_specs=[scalar] * 4,
        out_specs=[scalar] * 2,
        out_shape=[
            jax.ShapeDtypeStruct((rows,), jnp.int32),
            jax.ShapeDtypeStruct(table.shape[1:], jnp.int32),
        ],
        cost_estimate=pl.CostEstimate(**LONG),
        name="lookup",
    )(owner, lengths, table.reshape(-1), device_index[None])


def attention_kernel(context, latent, q, cache, fresh, lengths, routes, packet, keys_a, keys_b, total):
    step = pl.program_id(0)
    rows, kv_width = q.shape[1], cache.shape[1]
    wide = keys_a.shape[1]
    pairs = q.shape[2] // (2 * kv_width)
    keys = keys_a.shape[0]
    cached = cache.shape[0]

    @pl.when(step == 0)
    def _():
        keys_a[...] = jnp.zeros_like(keys_a)
        keys_a[:cached, :kv_width] = cache[...]
        keys_a[cached:, :kv_width] = fresh[...]
        shifted = pltpu.roll(keys_a[...].astype(jnp.float32), wide - kv_width, 1)
        keys_b[...] = shifted.astype(jnp.bfloat16)

    row = lax.broadcasted_iota(jnp.int32, (rows, keys), 0)
    key = lax.broadcasted_iota(jnp.int32, (rows, keys), 1)
    place = key // rows
    length = jnp.zeros((rows, keys), jnp.int32)
    for j in range(rows):
        length = jnp.where(row == j, lengths[j], length)
    seen = (place < length) & (place < context)
    seen = seen | ((place >= context) & (place <= context + step))
    bias = jnp.where(seen & (key % rows == row), 0.0, -1e30)
    summed = jnp.zeros((rows, keys), jnp.float32)
    for held, first in ((keys_a, 0), (keys_b, 2 * kv_width - wide)):
        heads = [
            q[0, :, 2 * kv_width * i + first : 2 * kv_width * i + first + wide].astype(jnp.float32)
            for i in range(pairs)
        ]
        scores = lax.dot_general(
            jnp.concatenate(heads, axis=0).astype(jnp.bfloat16),
            held[...],
            (((1,), (1,)), ((), ())),
            preferred_element_type=jnp.float32,
        )
        scores = (scores * qk_scale).reshape(pairs, rows, keys) + bias[None]
        e = jnp.exp(scores - jnp.max(scores, axis=2, keepdims=True))
        weights = e / jnp.sum(e, axis=2, keepdims=True)
        summed = summed + jnp.sum(weights.astype(jnp.bfloat16).astype(jnp.float32), axis=0)
    total[pl.ds(pl.multiple_of(step * rows, rows), rows), :] = summed

    @pl.when(step == pl.num_programs(0) - 1)
    def _():
        high = total[...].astype(jnp.bfloat16)
        low = (total[...] - high.astype(jnp.float32)).astype(jnp.bfloat16)
        values = keys_a[:, :latent]
        pooled = jnp.dot(high, values, preferred_element_type=jnp.float32)
        pooled = pooled + jnp.dot(low, values, preferred_element_type=jnp.float32)
        packet[:, :latent] = pooled.astype(jnp.bfloat16)
        lane = lax.broadcasted_iota(jnp.int32, (packet.shape[0], LANES), 1)
        routed = jnp.zeros(lane.shape, jnp.float32)
        for k in range(routes.shape[1]):
            routed = jnp.where(routes[:, k : k + 1] == lane, 1.0, routed)
        packet[:, latent:] = routed.astype(jnp.bfloat16)


def attention(q_abs, cache, fresh, lengths, routes, context, latent):
    steps, rows, _ = q_abs.shape
    kv_width = cache.shape[1]
    keys = cache.shape[0] + fresh.shape[0]
    wide = -(-kv_width // LANES) * LANES

    def whole(a):
        return pl.BlockSpec(a.shape, lambda i: (0, 0), pipeline_mode=pl.Buffered(1))

    return pl.pallas_call(
        lambda *refs: attention_kernel(context, latent, *refs),
        grid=(steps,),
        in_specs=[pl.BlockSpec((1, rows, q_abs.shape[2]), lambda i: (i, 0, 0))]
        + [whole(cache), whole(fresh), pl.BlockSpec(memory_space=pltpu.SMEM), whole(routes)],
        out_shape=jax.ShapeDtypeStruct((steps * rows, latent + LANES), jnp.bfloat16),
        out_specs=pl.BlockSpec((steps * rows, latent + LANES), lambda i: (0, 0)),
        scratch_shapes=[
            pltpu.VMEM((keys, wide), jnp.bfloat16),
            pltpu.VMEM((keys, wide), jnp.bfloat16),
            pltpu.VMEM((steps * rows, keys), jnp.float32),
        ],
        compiler_params=pltpu.CompilerParams(
            dimension_semantics=("arbitrary",), vmem_limit_bytes=(10 << 20) + 10240 * keys
        ),
        cost_estimate=pl.CostEstimate(**LONG),
        name="attention",
    )(q_abs, cache, fresh, lengths, routes)


def local(
    q_abs,
    new_lat,
    latent_cache,
    lengths,
    owner,
    resid,
    routes,
    w_out,
    norm_gain,
    w_router,
    w_gate,
    w_up,
    w_down,
):
    devices = lax.axis_size("expert")
    device_index = lax.axis_index("expert")
    step_count, row_count, width = resid.shape
    rows = step_count * row_count
    experts_all = w_router.shape[1]
    sharers = devices // experts_all
    chips = devices // 2
    half = chips // 2
    far, near = distances(chips)
    hold = lax.optimization_barrier
    cut = rows // 2
    sibling = sibling_perm(chips)

    def send(a, perm):
        return lax.ppermute(a, "expert", perm)

    to_right, to_left = shift_perm(chips, 1), shift_perm(chips, -1)
    parted = [
        shift_perm(chips, 2 - 4 * core)[2 * p + core] for p in range(chips) for core in range(2)
    ]
    first_core = device_index % 2 == 0

    def around(to_the_right, to_the_left):
        return send(to_the_right, to_right), send(to_the_left, to_left)

    positions, kv_width = latent_cache.shape[1:]
    wanted = (owner[:, None] == jnp.arange(owner.shape[0], dtype=jnp.int32)).astype(jnp.bfloat16)
    ordered = jnp.einsum(
        "jr,rpk->pjk", wanted, latent_cache, preferred_element_type=jnp.float32
    ).astype(jnp.bfloat16)
    ordered = ordered.reshape(positions, devices, row_count, kv_width).swapaxes(0, 1)
    owned = lax.all_to_all(ordered, "expert", split_axis=0, concat_axis=0, tiled=True)

    mine = resid.reshape(rows, width)
    held, sib = {0: mine}, {}
    held[-1], held[1] = around(mine, mine)
    table = [
        [device // sharers] + places
        for chip, places in enumerate(gathered_place(chips))
        for device in (2 * chip, 2 * chip + 1)
    ]
    row_lengths, scalars = lookup(
        owner, lengths, jnp.array(table, jnp.int32), device_index, row_count
    )
    row_lengths, scalars, held = hold((row_lengths, scalars, held))
    held[-2], held[2] = around(held[-1], held[1])
    sib[0] = send(mine, sibling)
    sib[1], sib[-1] = send(held[1], sibling), send(held[-1], sibling)
    gain = norm_gain[None, :]
    packet = attention(
        q_abs,
        owned.reshape(-1, kv_width),
        new_lat.reshape(rows, kv_width),
        row_lengths,
        routes.reshape(rows, -1),
        devices * positions,
        w_out.shape[0],
    )
    packet, gain, held, sib = hold((packet, gain, held, sib))

    high, low = gather_steps(chips)
    along = [send(packet, step_perm(chips, i, 0)) for i in range(1, high)]
    for t in range(3, half):
        held[-t], held[t] = around(held[1 - t], held[t - 1])
    along, held = hold((along, held))
    along = jnp.concatenate([packet] + along, axis=0)
    across = [send(along, step_perm(chips, 0, i)) for i in range(1, low)]
    held[half] = send(jnp.where(first_core, held[2 - half], held[half - 2]), parted)
    along_sib = send(along, sibling)
    sib[2], sib[-2] = send(held[2], sibling), send(held[-2], sibling)
    across, along_sib, held, sib = hold((across, along_sib, held, sib))
    for d in held:
        if d not in sib:
            sib[d] = send(held[d], sibling)
    across = across[0] if low == 2 else jnp.concatenate(across, axis=0)

    f32 = jnp.float32

    x_far, x_near, scale, weight, hidden = normalize(
        2 * len(far),
        scalars,
        [along, across, along_sib, send(across, sibling)],
        [a[d] for part in (far, near) for a in (held, sib) for d in part],
        w_out,
        gain,
        w_router.T,
    )
    far_rows = x_far.shape[0]

    def product(a, w):
        return jnp.dot(a, w[0], preferred_element_type=f32)

    def activate(a, b, at):
        r, g = scale[at, :1], weight[at, :1]
        return (jax.nn.silu(a * r) * (b * r) * g).astype(jnp.bfloat16)

    sums = {}

    def swap(dists, y):
        return y, send(y[len(dists) * rows :], sibling)

    def add_up(dists, y, received):
        for i, d in enumerate(dists):
            at = slice(i * rows, (i + 1) * rows)
            sums[d] = y[at].astype(f32) + received[at].astype(f32)

    def both(right, left):
        return around(right.astype(jnp.bfloat16), left.astype(jnp.bfloat16))

    act = hold(activate(product(x_far, w_gate), product(x_far, w_up), slice(0, far_rows)))
    y, received = swap(far, product(act, w_down).astype(jnp.bfloat16))
    gated, y, received = hold((product(x_near, w_gate), y, received))
    add_up(far, y, received)
    right, left = both(sums[half][:cut], sums[half][cut:])
    act = activate(gated, product(x_near, w_up), slice(far_rows, None))
    act, right, left = hold((act, right, left))
    right = jnp.concatenate([right.astype(f32), jnp.zeros((rows - cut, width), f32)], axis=0)
    left = jnp.concatenate([jnp.zeros((cut, width), f32), left.astype(f32)], axis=0)
    right, left = both(sums[half - 1] + right, sums[1 - half] + left)
    y, received = swap(near, product(act, w_down).astype(jnp.bfloat16))
    y, received, right, left = hold((y, received, right, left))
    add_up(near, y, received)
    for t in range(half - 2, 0, -1):
        right, left = hold(both(sums[t] + right.astype(f32), sums[-t] + left.astype(f32)))
    mixed = hidden + sums[0] + right.astype(f32) + left.astype(f32)
    return mixed.astype(jnp.bfloat16).reshape(step_count, row_count, width)


def solution(mesh):
    return jax.shard_map(
        local,
        mesh=mesh,
        in_specs=(
            P(None, ("group", "expert"), None),
            P(None, ("group", "expert"), None),
            P("group", "expert", None),
            P("group"),
            P("group"),
            P(None, ("group", "expert"), None),
            P(None, ("group", "expert"), None),
            P(),
            P(),
            P(),
            P("expert", None, None),
            P("expert", None, None),
            P("expert", None, None),
        ),
        out_specs=P(None, ("group", "expert"), None),
        check_vma=False,
    )
```

```python
import jax
import jax.numpy as jnp
from jax import lax
from jax.experimental import pallas as pl
from jax.experimental.pallas import tpu as pltpu
from jax.sharding import PartitionSpec as P

qk_scale = 192.0 ** (-0.5)
LANES = 128


def ring_of(chips):
    return list(range(0, chips, 2)) + list(range(chips - 1, 0, -2))


def shift_perm(chips, by):
    ring = ring_of(chips)
    return [
        (2 * ring[p] + core, 2 * ring[(p + by) % chips] + core)
        for p in range(chips)
        for core in range(2)
    ]


def sibling_perm(chips):
    return [(d, d ^ 1) for d in range(2 * chips)]


def distances(chips):
    half = chips // 2
    far = [half, half - 1, 1 - half]
    return far, [0] + [d for t in range(1, half - 1) for d in (t, -t)]


def gather_steps(chips):
    high = 4 if chips % 4 == 0 else 2
    return high, chips // high


def step_perm(chips, by_high, by_low):
    high, low = gather_steps(chips)
    return [
        (2 * (h * low + l) + core, 2 * ((h ^ by_high) * low + (l ^ by_low)) + core)
        for h in range(high)
        for l in range(low)
        for core in range(2)
    ]


def gathered_place(chips):
    high, low = gather_steps(chips)
    ring = ring_of(chips)
    table = [[] for _ in range(chips)]
    for p, chip in enumerate(ring):
        for part in distances(chips):
            for side in (0, chips):
                for d in part:
                    other = ring[(p + d) % chips]
                    by_high = (other // low) ^ (chip // low)
                    by_low = (other % low) ^ (chip % low)
                    table[chip].append(side + by_low * high + by_high)
    return table


def tile_of(size, most):
    return max(t for t in range(LANES, min(size, most) + 1, LANES) if size % t == 0)


def norm_kernel(far, blocks, rows, latent, width, *refs):
    scalars = refs[0]
    pooled = refs[1:5]
    resid = refs[5 : 5 + blocks]
    w_out, gain, w_router, x_far, x_near = refs[5 + blocks : 10 + blocks]
    scale, weight, hidden, raw, joined, ssq, logits = refs[10 + blocks :]
    step = pl.program_id(0)
    cols = w_out.shape[1]
    total = blocks * rows
    far_rows = far * rows
    experts_all = w_router.shape[0]
    chunk = min(512, total)

    @pl.when(step == 0)
    def _():
        start = 0
        for piece in pooled:
            raw[start : start + piece.shape[0], :] = piece[...]
            start += piece.shape[0]
        for b in range(blocks):
            place = pl.ds(pl.multiple_of(scalars[1 + b] * rows, rows), rows)
            joined[b * rows : (b + 1) * rows, :] = raw[place, :]
        ssq[...] = jnp.zeros_like(ssq)
        logits[...] = jnp.zeros_like(logits)

    g = gain[...].astype(jnp.float32)
    for c in range(0, total, chunk):
        end = min(c + chunk, total)
        proj = jnp.dot(joined[c:end, :latent], w_out[...], preferred_element_type=jnp.float32)
        for b in range(c // rows, end // rows):
            at = slice(b * rows, (b + 1) * rows)
            h = proj[b * rows - c : (b + 1) * rows - c] + resid[b][...].astype(jnp.float32)
            if b == far:
                hidden[...] = h
            scaled = (h * g).astype(jnp.bfloat16)
            if b < far:
                x_far[at, :] = scaled
            else:
                x_near[(b - far) * rows : (b - far + 1) * rows, :] = scaled
            sq = h * h
            part = sq[:, :LANES]
            for k in range(1, cols // LANES):
                part = part + sq[:, k * LANES : (k + 1) * LANES]
            ssq[at, :] += part
    nt = (((1,), (1,)), ((), ()))
    for x, at in ((x_far, slice(0, far_rows)), (x_near, slice(far_rows, total))):
        logits[at, :] += lax.dot_general(
            x[...], w_router[...], nt, preferred_element_type=jnp.float32
        )

    @pl.when(step == pl.num_programs(0) - 1)
    def _():
        mean = jnp.sum(ssq[...], axis=1, keepdims=True) * (1.0 / width)
        r = lax.rsqrt(mean + 1e-06)
        mask = joined[:, latent : latent + experts_all].astype(jnp.float32)
        affinity = jax.nn.sigmoid(logits[...] * r) * mask
        lane = lax.broadcasted_iota(jnp.int32, affinity.shape, 1)
        mine = jnp.sum(jnp.where(lane == scalars[0], affinity, 0.0), axis=1, keepdims=True)
        gate = 2.5 * mine / jnp.sum(affinity, axis=1, keepdims=True)
        scale[...] = jnp.broadcast_to(r, scale.shape)
        weight[...] = jnp.broadcast_to(gate, weight.shape)


def normalize(far, scalars, pooled, resid_blocks, w_out, gain, w_router_t):
    blocks = len(resid_blocks)
    rows, width = resid_blocks[0].shape
    latent = w_out.shape[0]
    total = blocks * rows
    cols = tile_of(width, 512)
    packed = pooled[0].shape[1]
    experts_all = w_router_t.shape[0]

    def whole(shape):
        return pl.BlockSpec(shape, lambda i: (0, 0), pipeline_mode=pl.Buffered(1))

    def tiles(height):
        return pl.BlockSpec((height, cols), lambda i: (0, i))

    need = total * (cols * 24 + packed * 6 + 8 * LANES * 4) + 4 * latent * cols
    return pl.pallas_call(
        lambda *refs: norm_kernel(far, blocks, rows, latent, width, *refs),
        grid=(width // cols,),
        in_specs=[pl.BlockSpec(memory_space=pltpu.SMEM)]
        + [whole(a.shape) for a in pooled]
        + [tiles(rows)] * blocks
        + [tiles(latent), tiles(1), tiles(experts_all)],
        out_shape=[
            jax.ShapeDtypeStruct((far * rows, width), jnp.bfloat16),
            jax.ShapeDtypeStruct((total - far * rows, width), jnp.bfloat16),
            jax.ShapeDtypeStruct((total, LANES), jnp.float32),
            jax.ShapeDtypeStruct((total, LANES), jnp.float32),
            jax.ShapeDtypeStruct((rows, width), jnp.float32),
        ],
        out_specs=[tiles(far * rows), tiles(total - far * rows)]
        + [whole((total, LANES)), whole((total, LANES)), tiles(rows)],
        scratch_shapes=[
            pltpu.VMEM((total, packed), jnp.bfloat16),
            pltpu.VMEM((total, packed), jnp.bfloat16),
            pltpu.VMEM((total, LANES), jnp.float32),
            pltpu.VMEM((total, experts_all), jnp.float32),
        ],
        compiler_params=pltpu.CompilerParams(
            dimension_semantics=("arbitrary",), vmem_limit_bytes=(int(need) // (1 << 20) + 6) << 20
        ),
        cost_estimate=pl.CostEstimate(
            flops=2 * total * width * latent,
            bytes_accessed=2 * total * width * 2 + latent * width * 2,
            transcendentals=total,
        ),
        name="normalize",
    )(scalars, *pooled, *resid_blocks, w_out, gain, w_router_t)


def lookup_kernel(owner, lengths, table, device, row_lengths, scalars):
    for j in range(row_lengths.shape[0]):
        row_lengths[j] = lengths[owner[device[0] * row_lengths.shape[0] + j]]
    for j in range(scalars.shape[0]):
        scalars[j] = table[device[0] * scalars.shape[0] + j]


LONG = dict(flops=10**10, bytes_accessed=10**8, transcendentals=0)


def lookup(owner, lengths, table, device_index, rows):
    scalar = pl.BlockSpec(memory_space=pltpu.SMEM)
    return pl.pallas_call(
        lookup_kernel,
        in_specs=[scalar] * 4,
        out_specs=[scalar] * 2,
        out_shape=[
            jax.ShapeDtypeStruct((rows,), jnp.int32),
            jax.ShapeDtypeStruct(table.shape[1:], jnp.int32),
        ],
        cost_estimate=pl.CostEstimate(**LONG),
        name="lookup",
    )(owner, lengths, table.reshape(-1), device_index[None])


def attention_kernel(context, latent, q, cache, fresh, lengths, routes, packet, keys_a, keys_b, total):
    step = pl.program_id(0)
    rows, kv_width = q.shape[1], cache.shape[1]
    wide = keys_a.shape[1]
    pairs = q.shape[2] // (2 * kv_width)
    keys = keys_a.shape[0]
    cached = cache.shape[0]

    @pl.when(step == 0)
    def _():
        keys_a[...] = jnp.zeros_like(keys_a)
        keys_a[:cached, :kv_width] = cache[...]
        keys_a[cached:, :kv_width] = fresh[...]
        shifted = pltpu.roll(keys_a[...].astype(jnp.float32), wide - kv_width, 1)
        keys_b[...] = shifted.astype(jnp.bfloat16)

    row = lax.broadcasted_iota(jnp.int32, (rows, keys), 0)
    key = lax.broadcasted_iota(jnp.int32, (rows, keys), 1)
    place = key // rows
    length = jnp.zeros((rows, keys), jnp.int32)
    for j in range(rows):
        length = jnp.where(row == j, lengths[j], length)
    seen = (place < length) & (place < context)
    seen = seen | ((place >= context) & (place <= context + step))
    bias = jnp.where(seen & (key % rows == row), 0.0, -1e30)
    summed = jnp.zeros((rows, keys), jnp.float32)
    for held, first in ((keys_a, 0), (keys_b, 2 * kv_width - wide)):
        heads = [
            q[0, :, 2 * kv_width * i + first : 2 * kv_width * i + first + wide].astype(jnp.float32)
            for i in range(pairs)
        ]
        scores = lax.dot_general(
            jnp.concatenate(heads, axis=0).astype(jnp.bfloat16),
            held[...],
            (((1,), (1,)), ((), ())),
            preferred_element_type=jnp.float32,
        )
        scores = (scores * qk_scale).reshape(pairs, rows, keys) + bias[None]
        e = jnp.exp(scores - jnp.max(scores, axis=2, keepdims=True))
        weights = e / jnp.sum(e, axis=2, keepdims=True)
        summed = summed + jnp.sum(weights.astype(jnp.bfloat16).astype(jnp.float32), axis=0)
    total[pl.ds(pl.multiple_of(step * rows, rows), rows), :] = summed

    @pl.when(step == pl.num_programs(0) - 1)
    def _():
        high = total[...].astype(jnp.bfloat16)
        low = (total[...] - high.astype(jnp.float32)).astype(jnp.bfloat16)
        values = keys_a[:, :latent]
        pooled = jnp.dot(high, values, preferred_element_type=jnp.float32)
        pooled = pooled + jnp.dot(low, values, preferred_element_type=jnp.float32)
        packet[:, :latent] = pooled.astype(jnp.bfloat16)
        lane = lax.broadcasted_iota(jnp.int32, (packet.shape[0], LANES), 1)
        routed = jnp.zeros(lane.shape, jnp.float32)
        for k in range(routes.shape[1]):
            routed = jnp.where(routes[:, k : k + 1] == lane, 1.0, routed)
        packet[:, latent:] = routed.astype(jnp.bfloat16)


def attention(q_abs, cache, fresh, lengths, routes, context, latent):
    steps, rows, _ = q_abs.shape
    kv_width = cache.shape[1]
    keys = cache.shape[0] + fresh.shape[0]
    wide = -(-kv_width // LANES) * LANES

    def whole(a):
        return pl.BlockSpec(a.shape, lambda i: (0, 0), pipeline_mode=pl.Buffered(1))

    return pl.pallas_call(
        lambda *refs: attention_kernel(context, latent, *refs),
        grid=(steps,),
        in_specs=[pl.BlockSpec((1, rows, q_abs.shape[2]), lambda i: (i, 0, 0))]
        + [whole(cache), whole(fresh), pl.BlockSpec(memory_space=pltpu.SMEM), whole(routes)],
        out_shape=jax.ShapeDtypeStruct((steps * rows, latent + LANES), jnp.bfloat16),
        out_specs=pl.BlockSpec((steps * rows, latent + LANES), lambda i: (0, 0)),
        scratch_shapes=[
            pltpu.VMEM((keys, wide), jnp.bfloat16),
            pltpu.VMEM((keys, wide), jnp.bfloat16),
            pltpu.VMEM((steps * rows, keys), jnp.float32),
        ],
        compiler_params=pltpu.CompilerParams(
            dimension_semantics=("arbitrary",), vmem_limit_bytes=(10 << 20) + 10240 * keys
        ),
        cost_estimate=pl.CostEstimate(
            flops=2 * q_abs.size * keys, bytes_accessed=2 * q_abs.size, transcendentals=0
        ),
        name="attention",
    )(q_abs, cache, fresh, lengths, routes)


def local(
    q_abs,
    new_lat,
    latent_cache,
    lengths,
    owner,
    resid,
    routes,
    w_out,
    norm_gain,
    w_router,
    w_gate,
    w_up,
    w_down,
):
    devices = lax.axis_size("expert")
    device_index = lax.axis_index("expert")
    step_count, row_count, width = resid.shape
    rows = step_count * row_count
    experts_all = w_router.shape[1]
    sharers = devices // experts_all
    chips = devices // 2
    half = chips // 2
    far, near = distances(chips)
    hold = lax.optimization_barrier
    stay = lambda a: pltpu.with_memory_space_constraint(a, pltpu.HBM)
    cut = rows // 2
    sibling = sibling_perm(chips)

    def send(a, perm):
        return lax.ppermute(a, "expert", perm)

    to_right, to_left = shift_perm(chips, 1), shift_perm(chips, -1)
    parted = [
        shift_perm(chips, 2 - 4 * core)[2 * p + core] for p in range(chips) for core in range(2)
    ]
    first_core = device_index % 2 == 0

    def around(to_the_right, to_the_left):
        return send(to_the_right, to_right), send(to_the_left, to_left)

    positions, kv_width = latent_cache.shape[1:]
    wanted = (owner[:, None] == jnp.arange(owner.shape[0], dtype=jnp.int32)).astype(jnp.bfloat16)
    ordered = jnp.einsum(
        "jr,rpk->pjk", wanted, latent_cache, preferred_element_type=jnp.float32
    ).astype(jnp.bfloat16)
    ordered = ordered.reshape(positions, devices, row_count, kv_width).swapaxes(0, 1)
    owned = lax.all_to_all(ordered, "expert", split_axis=0, concat_axis=0, tiled=True)

    mine = resid.reshape(rows, width)
    held, sib = {0: mine}, {}
    held[-1], held[1] = around(mine, mine)
    table = [
        [device // sharers] + places
        for chip, places in enumerate(gathered_place(chips))
        for device in (2 * chip, 2 * chip + 1)
    ]
    row_lengths, scalars = lookup(
        owner, lengths, jnp.array(table, jnp.int32), device_index, row_count
    )
    row_lengths, scalars, held = hold((row_lengths, scalars, held))
    held[-2], held[2] = around(held[-1], held[1])
    sib[0] = send(mine, sibling)
    sib[1], sib[-1] = send(held[1], sibling), send(held[-1], sibling)
    gain = norm_gain[None, :]
    packet = attention(
        q_abs,
        owned.reshape(-1, kv_width),
        new_lat.reshape(rows, kv_width),
        stay(row_lengths),
        routes.reshape(rows, -1),
        devices * positions,
        w_out.shape[0],
    )
    packet, gain, held, sib = hold((packet, gain, held, sib))

    high, low = gather_steps(chips)
    along = [send(packet, step_perm(chips, i, 0)) for i in range(1, high)]
    for t in range(3, half):
        held[-t], held[t] = around(held[1 - t], held[t - 1])
    along, held = hold((along, held))
    along = jnp.concatenate([packet] + along, axis=0)
    across = [send(along, step_perm(chips, 0, i)) for i in range(1, low)]
    held[half] = send(jnp.where(first_core, held[2 - half], held[half - 2]), parted)
    along_sib = send(along, sibling)
    sib[2], sib[-2] = send(held[2], sibling), send(held[-2], sibling)
    across, along_sib, held, sib = hold((across, along_sib, held, sib))
    for d in held:
        if d not in sib:
            sib[d] = send(held[d], sibling)
    across = across[0] if low == 2 else jnp.concatenate(across, axis=0)

    f32 = jnp.float32
    held[0] = stay(held[0])

    x_far, x_near, scale, weight, hidden = normalize(
        2 * len(far),
        stay(scalars),
        [along, across, along_sib, send(across, sibling)],
        [a[d] for part in (far, near) for a in (held, sib) for d in part],
        stay(w_out),
        gain,
        stay(w_router.T),
    )
    far_rows = x_far.shape[0]

    def product(a, w):
        return jnp.dot(a, w[0], preferred_element_type=f32)

    def activate(a, b, at):
        r, g = scale[at, :1], weight[at, :1]
        return (jax.nn.silu(a * r) * (b * r) * g).astype(jnp.bfloat16)

    sums = {}

    def swap(dists, y):
        return y, send(y[len(dists) * rows :], sibling)

    def add_up(dists, y, received):
        for i, d in enumerate(dists):
            at = slice(i * rows, (i + 1) * rows)
            sums[d] = y[at].astype(f32) + received[at].astype(f32)

    def both(right, left):
        return around(right.astype(jnp.bfloat16), left.astype(jnp.bfloat16))

    act = hold(activate(product(x_far, w_gate), product(x_far, w_up), slice(0, far_rows)))
    y, received = swap(far, product(act, w_down).astype(jnp.bfloat16))
    gated, y, received = hold((product(x_near, w_gate), y, received))
    add_up(far, y, received)
    right, left = both(sums[half][:cut], sums[half][cut:])
    act = activate(gated, product(x_near, w_up), slice(far_rows, None))
    act, right, left = hold((act, right, left))
    right = jnp.concatenate([right.astype(f32), jnp.zeros((rows - cut, width), f32)], axis=0)
    left = jnp.concatenate([jnp.zeros((cut, width), f32), left.astype(f32)], axis=0)
    right, left = both(sums[half - 1] + right, sums[1 - half] + left)
    y, received = swap(near, product(act, w_down).astype(jnp.bfloat16))
    y, received, right, left = hold((y, received, right, left))
    add_up(near, y, received)
    for t in range(half - 2, 0, -1):
        right, left = hold(both(sums[t] + right.astype(f32), sums[-t] + left.astype(f32)))
    mixed = hidden + sums[0] + right.astype(f32) + left.astype(f32)
    return mixed.astype(jnp.bfloat16).reshape(step_count, row_count, width)


def solution(mesh):
    return jax.shard_map(
        local,
        mesh=mesh,
        in_specs=(
            P(None, ("group", "expert"), None),
            P(None, ("group", "expert"), None),
            P("group", "expert", None),
            P("group"),
            P("group"),
            P(None, ("group", "expert"), None),
            P(None, ("group", "expert"), None),
            P(),
            P(),
            P(),
            P("expert", None, None),
            P("expert", None, None),
            P("expert", None, None),
        ),
        out_specs=P(None, ("group", "expert"), None),
        check_vma=False,
    )
```

```python
import jax
import jax.numpy as jnp
from jax import lax
from jax.experimental import pallas as pl
from jax.experimental.pallas import tpu as pltpu
from jax.sharding import PartitionSpec as P

qk_scale = 192.0 ** (-0.5)
LANES = 128


def ring_of(chips):
    return list(range(0, chips, 2)) + list(range(chips - 1, 0, -2))


def shift_perm(chips, by):
    ring = ring_of(chips)
    return [
        (2 * ring[p] + core, 2 * ring[(p + by) % chips] + core)
        for p in range(chips)
        for core in range(2)
    ]


def sibling_perm(chips):
    return [(d, d ^ 1) for d in range(2 * chips)]


def distances(chips):
    half = chips // 2
    far = [half, half - 1, 1 - half]
    return far, [0] + [d for t in range(1, half - 1) for d in (t, -t)]


def gather_steps(chips):
    high = 4 if chips % 4 == 0 else 2
    return high, chips // high


def step_perm(chips, by_high, by_low):
    high, low = gather_steps(chips)
    return [
        (2 * (h * low + l) + core, 2 * ((h ^ by_high) * low + (l ^ by_low)) + core)
        for h in range(high)
        for l in range(low)
        for core in range(2)
    ]


def gathered_place(chips):
    high, low = gather_steps(chips)
    ring = ring_of(chips)
    table = [[] for _ in range(chips)]
    for p, chip in enumerate(ring):
        for part in distances(chips):
            for side in (0, chips):
                for d in part:
                    other = ring[(p + d) % chips]
                    by_high = (other // low) ^ (chip // low)
                    by_low = (other % low) ^ (chip % low)
                    table[chip].append(side + by_low * high + by_high)
    return table


def tile_of(size, most):
    return max(t for t in range(LANES, min(size, most) + 1, LANES) if size % t == 0)


def norm_kernel(far, blocks, rows, latent, width, *refs):
    scalars = refs[0]
    pooled = refs[1:5]
    resid = refs[5 : 5 + blocks]
    w_out, gain, w_router, x_far, x_near = refs[5 + blocks : 10 + blocks]
    scale, weight, hidden, raw, joined, ssq, logits = refs[10 + blocks :]
    step = pl.program_id(0)
    cols = w_out.shape[1]
    total = blocks * rows
    far_rows = far * rows
    experts_all = w_router.shape[0]
    chunk = min(512, total)

    @pl.when(step == 0)
    def _():
        start = 0
        for piece in pooled:
            raw[start : start + piece.shape[0], :] = piece[...]
            start += piece.shape[0]
        for b in range(blocks):
            place = pl.ds(pl.multiple_of(scalars[1 + b] * rows, rows), rows)
            joined[b * rows : (b + 1) * rows, :] = raw[place, :]
        ssq[...] = jnp.zeros_like(ssq)
        logits[...] = jnp.zeros_like(logits)

    g = gain[...].astype(jnp.float32)
    for c in range(0, total, chunk):
        end = min(c + chunk, total)
        proj = jnp.dot(joined[c:end, :latent], w_out[...], preferred_element_type=jnp.float32)
        for b in range(c // rows, end // rows):
            at = slice(b * rows, (b + 1) * rows)
            h = proj[b * rows - c : (b + 1) * rows - c] + resid[b][...].astype(jnp.float32)
            if b == far:
                hidden[...] = h
            scaled = (h * g).astype(jnp.bfloat16)
            if b < far:
                x_far[at, :] = scaled
            else:
                x_near[(b - far) * rows : (b - far + 1) * rows, :] = scaled
            sq = h * h
            part = sq[:, :LANES]
            for k in range(1, cols // LANES):
                part = part + sq[:, k * LANES : (k + 1) * LANES]
            ssq[at, :] += part
    nt = (((1,), (1,)), ((), ()))
    for x, at in ((x_far, slice(0, far_rows)), (x_near, slice(far_rows, total))):
        logits[at, :] += lax.dot_general(
            x[...], w_router[...], nt, preferred_element_type=jnp.float32
        )

    @pl.when(step == pl.num_programs(0) - 1)
    def _():
        mean = jnp.sum(ssq[...], axis=1, keepdims=True) * (1.0 / width)
        r = lax.rsqrt(mean + 1e-06)
        mask = joined[:, latent : latent + experts_all].astype(jnp.float32)
        affinity = jax.nn.sigmoid(logits[...] * r) * mask
        lane = lax.broadcasted_iota(jnp.int32, affinity.shape, 1)
        mine = jnp.sum(jnp.where(lane == scalars[0], affinity, 0.0), axis=1, keepdims=True)
        gate = 2.5 * mine / jnp.sum(affinity, axis=1, keepdims=True)
        scale[...] = jnp.broadcast_to(r, scale.shape)
        weight[...] = jnp.broadcast_to(gate, weight.shape)


def normalize(far, scalars, pooled, resid_blocks, w_out, gain, w_router_t):
    blocks = len(resid_blocks)
    rows, width = resid_blocks[0].shape
    latent = w_out.shape[0]
    total = blocks * rows
    cols = tile_of(width, 1024)
    packed = pooled[0].shape[1]
    experts_all = w_router_t.shape[0]

    def whole(shape):
        return pl.BlockSpec(shape, lambda i: (0, 0), pipeline_mode=pl.Buffered(1))

    def tiles(height):
        return pl.BlockSpec((height, cols), lambda i: (0, i))

    need = total * (cols * 16 + packed * 6 + 8 * LANES * 4) + 4 * latent * cols
    return pl.pallas_call(
        lambda *refs: norm_kernel(far, blocks, rows, latent, width, *refs),
        grid=(width // cols,),
        in_specs=[pl.BlockSpec(memory_space=pltpu.SMEM)]
        + [whole(a.shape) for a in pooled]
        + [tiles(rows)] * blocks
        + [tiles(latent), tiles(1), tiles(experts_all)],
        out_shape=[
            jax.ShapeDtypeStruct((far * rows, width), jnp.bfloat16),
            jax.ShapeDtypeStruct((total - far * rows, width), jnp.bfloat16),
            jax.ShapeDtypeStruct((total, LANES), jnp.float32),
            jax.ShapeDtypeStruct((total, LANES), jnp.float32),
            jax.ShapeDtypeStruct((rows, width), jnp.float32),
        ],
        out_specs=[tiles(far * rows), tiles(total - far * rows)]
        + [whole((total, LANES)), whole((total, LANES)), tiles(rows)],
        scratch_shapes=[
            pltpu.VMEM((total, packed), jnp.bfloat16),
            pltpu.VMEM((total, packed), jnp.bfloat16),
            pltpu.VMEM((total, LANES), jnp.float32),
            pltpu.VMEM((total, experts_all), jnp.float32),
        ],
        compiler_params=pltpu.CompilerParams(
            dimension_semantics=("arbitrary",), vmem_limit_bytes=(int(need) // (1 << 20) + 6) << 20
        ),
        cost_estimate=pl.CostEstimate(
            flops=2 * total * width * latent,
            bytes_accessed=4 * total * width * 2 + latent * width * 2,
            transcendentals=total,
        ),
        name="normalize",
    )(scalars, *pooled, *resid_blocks, w_out, gain, w_router_t)


def lookup_kernel(owner, lengths, table, device, row_lengths, scalars):
    for j in range(row_lengths.shape[0]):
        row_lengths[j] = lengths[owner[device[0] * row_lengths.shape[0] + j]]
    for j in range(scalars.shape[0]):
        scalars[j] = table[device[0] * scalars.shape[0] + j]


LONG = dict(flops=10**10, bytes_accessed=10**8, transcendentals=0)


def lookup(owner, lengths, table, device_index, rows):
    scalar = pl.BlockSpec(memory_space=pltpu.SMEM)
    return pl.pallas_call(
        lookup_kernel,
        in_specs=[scalar] * 4,
        out_specs=[scalar] * 2,
        out_shape=[
            jax.ShapeDtypeStruct((rows,), jnp.int32),
            jax.ShapeDtypeStruct(table.shape[1:], jnp.int32),
        ],
        cost_estimate=pl.CostEstimate(**LONG),
        name="lookup",
    )(owner, lengths, table.reshape(-1), device_index[None])


def attention_kernel(context, latent, q, cache, fresh, lengths, routes, packet, keys_a, keys_b, total):
    step = pl.program_id(0)
    rows, kv_width = q.shape[1], cache.shape[1]
    wide = keys_a.shape[1]
    pairs = q.shape[2] // (2 * kv_width)
    keys = keys_a.shape[0]
    cached = cache.shape[0]

    @pl.when(step == 0)
    def _():
        keys_a[...] = jnp.zeros_like(keys_a)
        keys_a[:cached, :kv_width] = cache[...]
        keys_a[cached:, :kv_width] = fresh[...]
        shifted = pltpu.roll(keys_a[...].astype(jnp.float32), wide - kv_width, 1)
        keys_b[...] = shifted.astype(jnp.bfloat16)

    row = lax.broadcasted_iota(jnp.int32, (rows, keys), 0)
    key = lax.broadcasted_iota(jnp.int32, (rows, keys), 1)
    place = key // rows
    length = jnp.zeros((rows, keys), jnp.int32)
    for j in range(rows):
        length = jnp.where(row == j, lengths[j], length)
    seen = (place < length) & (place < context)
    seen = seen | ((place >= context) & (place <= context + step))
    bias = jnp.where(seen & (key % rows == row), 0.0, -1e30)
    summed = jnp.zeros((rows, keys), jnp.float32)
    for held, first in ((keys_a, 0), (keys_b, 2 * kv_width - wide)):
        heads = [
            q[0, :, 2 * kv_width * i + first : 2 * kv_width * i + first + wide].astype(jnp.float32)
            for i in range(pairs)
        ]
        scores = lax.dot_general(
            jnp.concatenate(heads, axis=0).astype(jnp.bfloat16),
            held[...],
            (((1,), (1,)), ((), ())),
            preferred_element_type=jnp.float32,
        )
        scores = (scores * qk_scale).reshape(pairs, rows, keys) + bias[None]
        e = jnp.exp(scores - jnp.max(scores, axis=2, keepdims=True))
        weights = e / jnp.sum(e, axis=2, keepdims=True)
        summed = summed + jnp.sum(weights.astype(jnp.bfloat16).astype(jnp.float32), axis=0)
    total[pl.ds(pl.multiple_of(step * rows, rows), rows), :] = summed

    @pl.when(step == pl.num_programs(0) - 1)
    def _():
        high = total[...].astype(jnp.bfloat16)
        low = (total[...] - high.astype(jnp.float32)).astype(jnp.bfloat16)
        values = keys_a[:, :latent]
        pooled = jnp.dot(high, values, preferred_element_type=jnp.float32)
        pooled = pooled + jnp.dot(low, values, preferred_element_type=jnp.float32)
        packet[:, :latent] = pooled.astype(jnp.bfloat16)
        lane = lax.broadcasted_iota(jnp.int32, (packet.shape[0], LANES), 1)
        routed = jnp.zeros(lane.shape, jnp.float32)
        for k in range(routes.shape[1]):
            routed = jnp.where(routes[:, k : k + 1] == lane, 1.0, routed)
        packet[:, latent:] = routed.astype(jnp.bfloat16)


def attention(q_abs, cache, fresh, lengths, routes, context, latent):
    steps, rows, _ = q_abs.shape
    kv_width = cache.shape[1]
    keys = cache.shape[0] + fresh.shape[0]
    wide = -(-kv_width // LANES) * LANES

    def whole(a):
        return pl.BlockSpec(a.shape, lambda i: (0, 0), pipeline_mode=pl.Buffered(1))

    return pl.pallas_call(
        lambda *refs: attention_kernel(context, latent, *refs),
        grid=(steps,),
        in_specs=[pl.BlockSpec((1, rows, q_abs.shape[2]), lambda i: (i, 0, 0))]
        + [whole(cache), whole(fresh), pl.BlockSpec(memory_space=pltpu.SMEM), whole(routes)],
        out_shape=jax.ShapeDtypeStruct((steps * rows, latent + LANES), jnp.bfloat16),
        out_specs=pl.BlockSpec((steps * rows, latent + LANES), lambda i: (0, 0)),
        scratch_shapes=[
            pltpu.VMEM((keys, wide), jnp.bfloat16),
            pltpu.VMEM((keys, wide), jnp.bfloat16),
            pltpu.VMEM((steps * rows, keys), jnp.float32),
        ],
        compiler_params=pltpu.CompilerParams(
            dimension_semantics=("arbitrary",), vmem_limit_bytes=(10 << 20) + 10240 * keys
        ),
        cost_estimate=pl.CostEstimate(
            flops=2 * q_abs.size * keys, bytes_accessed=2 * q_abs.size, transcendentals=0
        ),
        name="attention",
    )(q_abs, cache, fresh, lengths, routes)


def local(
    q_abs,
    new_lat,
    latent_cache,
    lengths,
    owner,
    resid,
    routes,
    w_out,
    norm_gain,
    w_router,
    w_gate,
    w_up,
    w_down,
):
    devices = lax.axis_size("expert")
    device_index = lax.axis_index("expert")
    step_count, row_count, width = resid.shape
    rows = step_count * row_count
    experts_all = w_router.shape[1]
    sharers = devices // experts_all
    chips = devices // 2
    half = chips // 2
    far, near = distances(chips)
    hold = lax.optimization_barrier
    stay = lambda a: pltpu.with_memory_space_constraint(a, pltpu.HBM)
    cut = rows // 2
    sibling = sibling_perm(chips)

    def send(a, perm):
        return lax.ppermute(a, "expert", perm)

    to_right, to_left = shift_perm(chips, 1), shift_perm(chips, -1)
    parted = [
        shift_perm(chips, 2 - 4 * core)[2 * p + core] for p in range(chips) for core in range(2)
    ]
    first_core = device_index % 2 == 0

    def around(to_the_right, to_the_left):
        return send(to_the_right, to_right), send(to_the_left, to_left)

    positions, kv_width = latent_cache.shape[1:]
    wanted = (owner[:, None] == jnp.arange(owner.shape[0], dtype=jnp.int32)).astype(jnp.bfloat16)
    ordered = jnp.einsum(
        "jr,rpk->pjk", wanted, latent_cache, preferred_element_type=jnp.float32
    ).astype(jnp.bfloat16)
    ordered = ordered.reshape(positions, devices, row_count, kv_width).swapaxes(0, 1)
    owned = lax.all_to_all(ordered, "expert", split_axis=0, concat_axis=0, tiled=True)

    mine = resid.reshape(rows, width)
    held, sib = {0: mine}, {}
    held[-1], held[1] = around(mine, mine)
    table = [
        [device // sharers] + places
        for chip, places in enumerate(gathered_place(chips))
        for device in (2 * chip, 2 * chip + 1)
    ]
    row_lengths, scalars = lookup(
        owner, lengths, jnp.array(table, jnp.int32), device_index, row_count
    )
    row_lengths, scalars, held = hold((row_lengths, scalars, held))
    held[-2], held[2] = around(held[-1], held[1])
    sib[0] = send(mine, sibling)
    sib[1], sib[-1] = send(held[1], sibling), send(held[-1], sibling)
    gain = norm_gain[None, :]
    packet = attention(
        q_abs,
        owned.reshape(-1, kv_width),
        new_lat.reshape(rows, kv_width),
        stay(row_lengths),
        routes.reshape(rows, -1),
        devices * positions,
        w_out.shape[0],
    )
    packet, gain, held, sib = hold((packet, gain, held, sib))

    high, low = gather_steps(chips)
    along = [send(packet, step_perm(chips, i, 0)) for i in range(1, high)]
    for t in range(3, half):
        held[-t], held[t] = around(held[1 - t], held[t - 1])
    along, held = hold((along, held))
    along = jnp.concatenate([packet] + along, axis=0)
    across = [send(along, step_perm(chips, 0, i)) for i in range(1, low)]
    held[half] = send(jnp.where(first_core, held[2 - half], held[half - 2]), parted)
    along_sib = send(along, sibling)
    sib[2], sib[-2] = send(held[2], sibling), send(held[-2], sibling)
    across, along_sib, held, sib = hold((across, along_sib, held, sib))
    for d in held:
        if d not in sib:
            sib[d] = send(held[d], sibling)
    across = across[0] if low == 2 else jnp.concatenate(across, axis=0)

    f32 = jnp.float32
    held[0] = stay(held[0])

    x_far, x_near, scale, weight, hidden = normalize(
        2 * len(far),
        stay(scalars),
        [along, across, along_sib, send(across, sibling)],
        [a[d] for part in (far, near) for a in (held, sib) for d in part],
        stay(w_out),
        gain,
        stay(w_router.T),
    )
    far_rows = x_far.shape[0]

    def product(a, w):
        return jnp.dot(a, w[0], preferred_element_type=f32)

    def activate(a, b, at):
        r, g = scale[at, :1], weight[at, :1]
        return (jax.nn.silu(a * r) * (b * r) * g).astype(jnp.bfloat16)

    sums = {}

    def swap(dists, y):
        return y, send(y[len(dists) * rows :], sibling)

    def add_up(dists, y, received):
        for i, d in enumerate(dists):
            at = slice(i * rows, (i + 1) * rows)
            sums[d] = y[at].astype(f32) + received[at].astype(f32)

    def both(right, left):
        return around(right.astype(jnp.bfloat16), left.astype(jnp.bfloat16))

    act = hold(activate(product(x_far, w_gate), product(x_far, w_up), slice(0, far_rows)))
    y, received = swap(far, product(act, w_down).astype(jnp.bfloat16))
    gated, y, received = hold((product(x_near, w_gate), y, received))
    add_up(far, y, received)
    right, left = both(sums[half][:cut], sums[half][cut:])
    act = activate(gated, product(x_near, w_up), slice(far_rows, None))
    act, right, left = hold((act, right, left))
    right = jnp.concatenate([right.astype(f32), jnp.zeros((rows - cut, width), f32)], axis=0)
    left = jnp.concatenate([jnp.zeros((cut, width), f32), left.astype(f32)], axis=0)
    right, left = both(sums[half - 1] + right, sums[1 - half] + left)
    y, received = swap(near, product(act, w_down).astype(jnp.bfloat16))
    y, received, right, left = hold((y, received, right, left))
    add_up(near, y, received)
    for t in range(half - 2, 0, -1):
        right, left = hold(both(sums[t] + right.astype(f32), sums[-t] + left.astype(f32)))
    mixed = hidden + sums[0] + right.astype(f32) + left.astype(f32)
    return mixed.astype(jnp.bfloat16).reshape(step_count, row_count, width)


def solution(mesh):
    return jax.shard_map(
        local,
        mesh=mesh,
        in_specs=(
            P(None, ("group", "expert"), None),
            P(None, ("group", "expert"), None),
            P("group", "expert", None),
            P("group"),
            P("group"),
            P(None, ("group", "expert"), None),
            P(None, ("group", "expert"), None),
            P(),
            P(),
            P(),
            P("expert", None, None),
            P("expert", None, None),
            P("expert", None, None),
        ),
        out_specs=P(None, ("group", "expert"), None),
        check_vma=False,
    )
```

```python
import jax
import jax.numpy as jnp
from jax import lax
from jax.experimental import pallas as pl
from jax.experimental.pallas import tpu as pltpu
from jax.sharding import PartitionSpec as P

qk_scale = 192.0 ** (-0.5)
LANES = 128


def ring_of(chips):
    return list(range(0, chips, 2)) + list(range(chips - 1, 0, -2))


def shift_perm(chips, by):
    ring = ring_of(chips)
    return [
        (2 * ring[p] + core, 2 * ring[(p + by) % chips] + core)
        for p in range(chips)
        for core in range(2)
    ]


def sibling_perm(chips):
    return [(d, d ^ 1) for d in range(2 * chips)]


def distances(chips):
    half = chips // 2
    far = [half, half - 1, 1 - half]
    return far, [0] + [d for t in range(1, half - 1) for d in (t, -t)]


def gather_steps(chips):
    high = 4 if chips % 4 == 0 else 2
    return high, chips // high


def step_perm(chips, by_high, by_low):
    high, low = gather_steps(chips)
    return [
        (2 * (h * low + l) + core, 2 * ((h ^ by_high) * low + (l ^ by_low)) + core)
        for h in range(high)
        for l in range(low)
        for core in range(2)
    ]


def gathered_place(chips):
    high, low = gather_steps(chips)
    ring = ring_of(chips)
    table = [[] for _ in range(chips)]
    for p, chip in enumerate(ring):
        for part in distances(chips):
            for side in (0, chips):
                for d in part:
                    other = ring[(p + d) % chips]
                    by_high = (other // low) ^ (chip // low)
                    by_low = (other % low) ^ (chip % low)
                    table[chip].append(side + by_low * high + by_high)
    return table


def tile_of(size, most):
    return max(t for t in range(LANES, min(size, most) + 1, LANES) if size % t == 0)


def norm_kernel(far, blocks, rows, latent, width, *refs):
    scalars = refs[0]
    pooled = refs[1:5]
    resid = refs[5 : 5 + blocks]
    w_out, gain, w_router, x_far, x_near = refs[5 + blocks : 10 + blocks]
    scale, weight, hidden, raw, joined, ssq, logits = refs[10 + blocks :]
    step = pl.program_id(0)
    cols = w_out.shape[1]
    total = blocks * rows
    far_rows = far * rows
    experts_all = w_router.shape[0]
    chunk = min(512, total)

    @pl.when(step == 0)
    def _():
        start = 0
        for piece in pooled:
            raw[start : start + piece.shape[0], :] = piece[...]
            start += piece.shape[0]
        for b in range(blocks):
            place = pl.ds(pl.multiple_of(scalars[1 + b] * rows, rows), rows)
            joined[b * rows : (b + 1) * rows, :] = raw[place, :]
        ssq[...] = jnp.zeros_like(ssq)
        logits[...] = jnp.zeros_like(logits)

    g = gain[...].astype(jnp.float32)
    for c in range(0, total, chunk):
        end = min(c + chunk, total)
        proj = jnp.dot(joined[c:end, :latent], w_out[...], preferred_element_type=jnp.float32)
        for b in range(c // rows, end // rows):
            at = slice(b * rows, (b + 1) * rows)
            h = proj[b * rows - c : (b + 1) * rows - c] + resid[b][...].astype(jnp.float32)
            if b == far:
                hidden[...] = h
            scaled = (h * g).astype(jnp.bfloat16)
            if b < far:
                x_far[at, :] = scaled
            else:
                x_near[(b - far) * rows : (b - far + 1) * rows, :] = scaled
            sq = h * h
            part = sq[:, :LANES]
            for k in range(1, cols // LANES):
                part = part + sq[:, k * LANES : (k + 1) * LANES]
            ssq[at, :] += part
    nt = (((1,), (1,)), ((), ()))
    for x, at in ((x_far, slice(0, far_rows)), (x_near, slice(far_rows, total))):
        logits[at, :] += lax.dot_general(
            x[...], w_router[...], nt, preferred_element_type=jnp.float32
        )

    @pl.when(step == pl.num_programs(0) - 1)
    def _():
        mean = jnp.sum(ssq[...], axis=1, keepdims=True) * (1.0 / width)
        r = lax.rsqrt(mean + 1e-06)
        mask = joined[:, latent : latent + experts_all].astype(jnp.float32)
        affinity = jax.nn.sigmoid(logits[...] * r) * mask
        lane = lax.broadcasted_iota(jnp.int32, affinity.shape, 1)
        mine = jnp.sum(jnp.where(lane == scalars[0], affinity, 0.0), axis=1, keepdims=True)
        gate = 2.5 * mine / jnp.sum(affinity, axis=1, keepdims=True)
        scale[...] = jnp.broadcast_to(r, scale.shape)
        weight[...] = jnp.broadcast_to(gate, weight.shape)


def normalize(far, scalars, pooled, resid_blocks, w_out, gain, w_router_t):
    blocks = len(resid_blocks)
    rows, width = resid_blocks[0].shape
    latent = w_out.shape[0]
    total = blocks * rows
    cols = tile_of(width, 1024)
    packed = pooled[0].shape[1]
    experts_all = w_router_t.shape[0]

    def whole(shape):
        return pl.BlockSpec(shape, lambda i: (0, 0), pipeline_mode=pl.Buffered(1))

    def tiles(height):
        return pl.BlockSpec((height, cols), lambda i: (0, i))

    need = total * (cols * 16 + packed * 6 + 8 * LANES * 4) + 4 * latent * cols
    return pl.pallas_call(
        lambda *refs: norm_kernel(far, blocks, rows, latent, width, *refs),
        grid=(width // cols,),
        in_specs=[pl.BlockSpec(memory_space=pltpu.SMEM)]
        + [whole(a.shape) for a in pooled]
        + [tiles(rows)] * blocks
        + [tiles(latent), tiles(1), tiles(experts_all)],
        out_shape=[
            jax.ShapeDtypeStruct((far * rows, width), jnp.bfloat16),
            jax.ShapeDtypeStruct((total - far * rows, width), jnp.bfloat16),
            jax.ShapeDtypeStruct((total, LANES), jnp.float32),
            jax.ShapeDtypeStruct((total, LANES), jnp.float32),
            jax.ShapeDtypeStruct((rows, width), jnp.float32),
        ],
        out_specs=[tiles(far * rows), tiles(total - far * rows)]
        + [whole((total, LANES)), whole((total, LANES)), tiles(rows)],
        scratch_shapes=[
            pltpu.VMEM((total, packed), jnp.bfloat16),
            pltpu.VMEM((total, packed), jnp.bfloat16),
            pltpu.VMEM((total, LANES), jnp.float32),
            pltpu.VMEM((total, experts_all), jnp.float32),
        ],
        compiler_params=pltpu.CompilerParams(
            dimension_semantics=("arbitrary",), vmem_limit_bytes=(int(need) // (1 << 20) + 6) << 20
        ),
        cost_estimate=pl.CostEstimate(
            flops=2 * total * width * latent,
            bytes_accessed=4 * total * width * 2 + latent * width * 2,
            transcendentals=total,
        ),
        name="normalize",
    )(scalars, *pooled, *resid_blocks, w_out, gain, w_router_t)


def lookup_kernel(owner, lengths, table, device, row_lengths, scalars):
    for j in range(row_lengths.shape[0]):
        row_lengths[j] = lengths[owner[device[0] * row_lengths.shape[0] + j]]
    for j in range(scalars.shape[0]):
        scalars[j] = table[device[0] * scalars.shape[0] + j]


LONG = dict(flops=10**10, bytes_accessed=10**8, transcendentals=0)


def lookup(owner, lengths, table, device_index, rows):
    scalar = pl.BlockSpec(memory_space=pltpu.SMEM)
    return pl.pallas_call(
        lookup_kernel,
        in_specs=[scalar] * 4,
        out_specs=[scalar] * 2,
        out_shape=[
            jax.ShapeDtypeStruct((rows,), jnp.int32),
            jax.ShapeDtypeStruct(table.shape[1:], jnp.int32),
        ],
        cost_estimate=pl.CostEstimate(**LONG),
        name="lookup",
    )(owner, lengths, table.reshape(-1), device_index[None])


def attention_kernel(context, latent, q, cache, fresh, lengths, routes, packet, keys_a, keys_b, total):
    step = pl.program_id(0)
    rows, kv_width = q.shape[1], cache.shape[1]
    wide = keys_a.shape[1]
    pairs = q.shape[2] // (2 * kv_width)
    keys = keys_a.shape[0]
    cached = cache.shape[0]

    @pl.when(step == 0)
    def _():
        keys_a[...] = jnp.zeros_like(keys_a)
        keys_a[:cached, :kv_width] = cache[...]
        keys_a[cached:, :kv_width] = fresh[...]
        shifted = pltpu.roll(keys_a[...].astype(jnp.float32), wide - kv_width, 1)
        keys_b[...] = shifted.astype(jnp.bfloat16)

    row = lax.broadcasted_iota(jnp.int32, (rows, keys), 0)
    key = lax.broadcasted_iota(jnp.int32, (rows, keys), 1)
    place = key // rows
    length = jnp.zeros((rows, keys), jnp.int32)
    for j in range(rows):
        length = jnp.where(row == j, lengths[j], length)
    seen = (place < length) & (place < context)
    seen = seen | ((place >= context) & (place <= context + step))
    bias = jnp.where(seen & (key % rows == row), 0.0, -1e30)
    summed = jnp.zeros((rows, keys), jnp.float32)
    for held, first in ((keys_a, 0), (keys_b, 2 * kv_width - wide)):
        heads = [
            q[0, :, 2 * kv_width * i + first : 2 * kv_width * i + first + wide].astype(jnp.float32)
            for i in range(pairs)
        ]
        scores = lax.dot_general(
            jnp.concatenate(heads, axis=0).astype(jnp.bfloat16),
            held[...],
            (((1,), (1,)), ((), ())),
            preferred_element_type=jnp.float32,
        )
        scores = (scores * qk_scale).reshape(pairs, rows, keys) + bias[None]
        e = jnp.exp(scores - jnp.max(scores, axis=2, keepdims=True))
        weights = e / jnp.sum(e, axis=2, keepdims=True)
        summed = summed + jnp.sum(weights.astype(jnp.bfloat16).astype(jnp.float32), axis=0)
    total[pl.ds(pl.multiple_of(step * rows, rows), rows), :] = summed

    @pl.when(step == pl.num_programs(0) - 1)
    def _():
        high = total[...].astype(jnp.bfloat16)
        low = (total[...] - high.astype(jnp.float32)).astype(jnp.bfloat16)
        values = keys_a[:, :latent]
        pooled = jnp.dot(high, values, preferred_element_type=jnp.float32)
        pooled = pooled + jnp.dot(low, values, preferred_element_type=jnp.float32)
        packet[:, :latent] = pooled.astype(jnp.bfloat16)
        lane = lax.broadcasted_iota(jnp.int32, (packet.shape[0], LANES), 1)
        routed = jnp.zeros(lane.shape, jnp.float32)
        for k in range(routes.shape[1]):
            routed = jnp.where(routes[:, k : k + 1] == lane, 1.0, routed)
        packet[:, latent:] = routed.astype(jnp.bfloat16)


def attention(q_abs, cache, fresh, lengths, routes, context, latent):
    steps, rows, _ = q_abs.shape
    kv_width = cache.shape[1]
    keys = cache.shape[0] + fresh.shape[0]
    wide = -(-kv_width // LANES) * LANES

    def whole(a):
        return pl.BlockSpec(a.shape, lambda i: (0, 0), pipeline_mode=pl.Buffered(1))

    return pl.pallas_call(
        lambda *refs: attention_kernel(context, latent, *refs),
        grid=(steps,),
        in_specs=[pl.BlockSpec((1, rows, q_abs.shape[2]), lambda i: (i, 0, 0))]
        + [whole(cache), whole(fresh), pl.BlockSpec(memory_space=pltpu.SMEM), whole(routes)],
        out_shape=jax.ShapeDtypeStruct((steps * rows, latent + LANES), jnp.bfloat16),
        out_specs=pl.BlockSpec((steps * rows, latent + LANES), lambda i: (0, 0)),
        scratch_shapes=[
            pltpu.VMEM((keys, wide), jnp.bfloat16),
            pltpu.VMEM((keys, wide), jnp.bfloat16),
            pltpu.VMEM((steps * rows, keys), jnp.float32),
        ],
        compiler_params=pltpu.CompilerParams(
            dimension_semantics=("arbitrary",), vmem_limit_bytes=(10 << 20) + 10240 * keys
        ),
        cost_estimate=pl.CostEstimate(
            flops=2 * q_abs.size * keys, bytes_accessed=2 * q_abs.size, transcendentals=0
        ),
        name="attention",
    )(q_abs, cache, fresh, lengths, routes)


def local(
    q_abs,
    new_lat,
    latent_cache,
    lengths,
    owner,
    resid,
    routes,
    w_out,
    norm_gain,
    w_router,
    w_gate,
    w_up,
    w_down,
):
    devices = lax.axis_size("expert")
    device_index = lax.axis_index("expert")
    step_count, row_count, width = resid.shape
    rows = step_count * row_count
    experts_all = w_router.shape[1]
    sharers = devices // experts_all
    chips = devices // 2
    half = chips // 2
    far, near = distances(chips)
    hold = lax.optimization_barrier
    stay = lambda a: pltpu.with_memory_space_constraint(a, pltpu.HBM)
    cut = rows // 2
    sibling = sibling_perm(chips)

    def send(a, perm):
        return lax.ppermute(a, "expert", perm)

    to_right, to_left = shift_perm(chips, 1), shift_perm(chips, -1)
    parted = [
        shift_perm(chips, 2 - 4 * core)[2 * p + core] for p in range(chips) for core in range(2)
    ]
    first_core = device_index % 2 == 0

    def around(to_the_right, to_the_left):
        return send(to_the_right, to_right), send(to_the_left, to_left)

    positions, kv_width = latent_cache.shape[1:]
    wanted = (owner[:, None] == jnp.arange(owner.shape[0], dtype=jnp.int32)).astype(jnp.bfloat16)
    ordered = jnp.einsum(
        "jr,rpk->pjk", wanted, latent_cache, preferred_element_type=jnp.float32
    ).astype(jnp.bfloat16)
    ordered = ordered.reshape(positions, devices, row_count, kv_width).swapaxes(0, 1)
    owned = lax.all_to_all(ordered, "expert", split_axis=0, concat_axis=0, tiled=True)

    mine = resid.reshape(rows, width)
    held, sib = {0: mine}, {}
    held[-1], held[1] = around(mine, mine)
    table = [
        [device // sharers] + places
        for chip, places in enumerate(gathered_place(chips))
        for device in (2 * chip, 2 * chip + 1)
    ]
    row_lengths, scalars = lookup(
        owner, lengths, jnp.array(table, jnp.int32), device_index, row_count
    )
    row_lengths, scalars, held = hold((row_lengths, scalars, held))
    held[-2], held[2] = around(held[-1], held[1])
    sib[0] = send(mine, sibling)
    sib[1], sib[-1] = send(held[1], sibling), send(held[-1], sibling)
    gain = norm_gain[None, :]
    packet = attention(
        q_abs,
        owned.reshape(-1, kv_width),
        new_lat.reshape(rows, kv_width),
        stay(row_lengths),
        routes.reshape(rows, -1),
        devices * positions,
        w_out.shape[0],
    )
    packet, gain, held, sib = hold((packet, gain, held, sib))

    high, low = gather_steps(chips)
    along = [send(packet, step_perm(chips, i, 0)) for i in range(1, high)]
    for t in range(3, half):
        held[-t], held[t] = around(held[1 - t], held[t - 1])
    along, held = hold((along, held))
    along = jnp.concatenate([packet] + along, axis=0)
    along, w_gate = hold((along, w_gate))
    w_gate = jnp.where(device_index >= 0, w_gate, jnp.zeros_like(w_gate))
    across = [send(along, step_perm(chips, 0, i)) for i in range(1, low)]
    held[half] = send(jnp.where(first_core, held[2 - half], held[half - 2]), parted)
    along_sib = send(along, sibling)
    sib[2], sib[-2] = send(held[2], sibling), send(held[-2], sibling)
    across, along_sib, held, sib, w_gate = hold((across, along_sib, held, sib, w_gate))
    for d in held:
        if d not in sib:
            sib[d] = send(held[d], sibling)
    across = across[0] if low == 2 else jnp.concatenate(across, axis=0)

    f32 = jnp.float32
    held[0] = stay(held[0])

    x_far, x_near, scale, weight, hidden = normalize(
        2 * len(far),
        stay(scalars),
        [along, across, along_sib, send(across, sibling)],
        [a[d] for part in (far, near) for a in (held, sib) for d in part],
        stay(w_out),
        gain,
        stay(w_router.T),
    )
    far_rows = x_far.shape[0]

    def product(a, w):
        return jnp.dot(a, w[0], preferred_element_type=f32)

    def activate(a, b, at):
        r, g = scale[at, :1], weight[at, :1]
        return (jax.nn.silu(a * r) * (b * r) * g).astype(jnp.bfloat16)

    sums = {}

    def swap(dists, y):
        return y, send(y[len(dists) * rows :], sibling)

    def add_up(dists, y, received):
        for i, d in enumerate(dists):
            at = slice(i * rows, (i + 1) * rows)
            sums[d] = y[at].astype(f32) + received[at].astype(f32)

    def both(right, left):
        return around(right.astype(jnp.bfloat16), left.astype(jnp.bfloat16))

    act = hold(activate(product(x_far, w_gate), product(x_far, w_up), slice(0, far_rows)))
    y, received = swap(far, product(act, w_down).astype(jnp.bfloat16))
    gated, y, received = hold((product(x_near, w_gate), y, received))
    add_up(far, y, received)
    right, left = both(sums[half][:cut], sums[half][cut:])
    act = activate(gated, product(x_near, w_up), slice(far_rows, None))
    act, right, left = hold((act, right, left))
    right = jnp.concatenate([right.astype(f32), jnp.zeros((rows - cut, width), f32)], axis=0)
    left = jnp.concatenate([jnp.zeros((cut, width), f32), left.astype(f32)], axis=0)
    right, left = both(sums[half - 1] + right, sums[1 - half] + left)
    y, received = swap(near, product(act, w_down).astype(jnp.bfloat16))
    y, received, right, left = hold((y, received, right, left))
    add_up(near, y, received)
    for t in range(half - 2, 0, -1):
        right, left = hold(both(sums[t] + right.astype(f32), sums[-t] + left.astype(f32)))
    mixed = hidden + sums[0] + right.astype(f32) + left.astype(f32)
    return mixed.astype(jnp.bfloat16).reshape(step_count, row_count, width)


def solution(mesh):
    return jax.shard_map(
        local,
        mesh=mesh,
        in_specs=(
            P(None, ("group", "expert"), None),
            P(None, ("group", "expert"), None),
            P("group", "expert", None),
            P("group"),
            P("group"),
            P(None, ("group", "expert"), None),
            P(None, ("group", "expert"), None),
            P(),
            P(),
            P(),
            P("expert", None, None),
            P("expert", None, None),
            P("expert", None, None),
        ),
        out_specs=P(None, ("group", "expert"), None),
        check_vma=False,
    )
```

```python
import jax
import jax.numpy as jnp
from jax import lax
from jax.experimental import pallas as pl
from jax.experimental.pallas import tpu as pltpu
from jax.sharding import PartitionSpec as P

qk_scale = 192.0 ** (-0.5)
LANES = 128


def ring_of(chips):
    return list(range(0, chips, 2)) + list(range(chips - 1, 0, -2))


def shift_perm(chips, by):
    ring = ring_of(chips)
    return [
        (2 * ring[p] + core, 2 * ring[(p + by) % chips] + core)
        for p in range(chips)
        for core in range(2)
    ]


def sibling_perm(chips):
    return [(d, d ^ 1) for d in range(2 * chips)]


def distances(chips):
    half = chips // 2
    far = [half, half - 1, 1 - half]
    return far, [0] + [d for t in range(1, half - 1) for d in (t, -t)]


def gather_steps(chips):
    high = 4 if chips % 4 == 0 else 2
    return high, chips // high


def step_perm(chips, by_high, by_low):
    high, low = gather_steps(chips)
    return [
        (2 * (h * low + l) + core, 2 * ((h ^ by_high) * low + (l ^ by_low)) + core)
        for h in range(high)
        for l in range(low)
        for core in range(2)
    ]


def gathered_place(chips):
    high, low = gather_steps(chips)
    ring = ring_of(chips)
    table = [[] for _ in range(chips)]
    for p, chip in enumerate(ring):
        for part in distances(chips):
            for side in (0, chips):
                for d in part:
                    other = ring[(p + d) % chips]
                    by_high = (other // low) ^ (chip // low)
                    by_low = (other % low) ^ (chip % low)
                    table[chip].append(side + by_low * high + by_high)
    return table


def tile_of(size, most):
    return max(t for t in range(LANES, min(size, most) + 1, LANES) if size % t == 0)


def norm_kernel(far, blocks, rows, latent, width, *refs):
    scalars = refs[0]
    pooled = refs[1:5]
    resid = refs[5 : 5 + blocks]
    w_out, gain, w_router, x_far, x_near = refs[5 + blocks : 10 + blocks]
    scale, weight, hidden, raw, joined, ssq, logits = refs[10 + blocks :]
    step = pl.program_id(0)
    cols = w_out.shape[1]
    total = blocks * rows
    far_rows = far * rows
    experts_all = w_router.shape[0]
    chunk = min(512, total)

    @pl.when(step == 0)
    def _():
        start = 0
        for piece in pooled:
            raw[start : start + piece.shape[0], :] = piece[...]
            start += piece.shape[0]
        for b in range(blocks):
            place = pl.ds(pl.multiple_of(scalars[1 + b] * rows, rows), rows)
            joined[b * rows : (b + 1) * rows, :] = raw[place, :]
        ssq[...] = jnp.zeros_like(ssq)
        logits[...] = jnp.zeros_like(logits)

    g = gain[...].astype(jnp.float32)
    for c in range(0, total, chunk):
        end = min(c + chunk, total)
        proj = jnp.dot(joined[c:end, :latent], w_out[...], preferred_element_type=jnp.float32)
        for b in range(c // rows, end // rows):
            at = slice(b * rows, (b + 1) * rows)
            h = proj[b * rows - c : (b + 1) * rows - c] + resid[b][...].astype(jnp.float32)
            if b == far:
                hidden[...] = h
            scaled = (h * g).astype(jnp.bfloat16)
            if b < far:
                x_far[at, :] = scaled
            else:
                x_near[(b - far) * rows : (b - far + 1) * rows, :] = scaled
            sq = h * h
            part = sq[:, :LANES]
            for k in range(1, cols // LANES):
                part = part + sq[:, k * LANES : (k + 1) * LANES]
            ssq[at, :] += part
    nt = (((1,), (1,)), ((), ()))
    for x, at in ((x_far, slice(0, far_rows)), (x_near, slice(far_rows, total))):
        logits[at, :] += lax.dot_general(
            x[...], w_router[...], nt, preferred_element_type=jnp.float32
        )

    @pl.when(step == pl.num_programs(0) - 1)
    def _():
        mean = jnp.sum(ssq[...], axis=1, keepdims=True) * (1.0 / width)
        r = lax.rsqrt(mean + 1e-06)
        mask = joined[:, latent : latent + experts_all].astype(jnp.float32)
        affinity = jax.nn.sigmoid(logits[...] * r) * mask
        lane = lax.broadcasted_iota(jnp.int32, affinity.shape, 1)
        mine = jnp.sum(jnp.where(lane == scalars[0], affinity, 0.0), axis=1, keepdims=True)
        gate = 2.5 * mine / jnp.sum(affinity, axis=1, keepdims=True)
        scale[...] = jnp.broadcast_to(r, scale.shape)
        weight[...] = jnp.broadcast_to(gate, weight.shape)


def normalize(far, scalars, pooled, resid_blocks, w_out, gain, w_router_t):
    blocks = len(resid_blocks)
    rows, width = resid_blocks[0].shape
    latent = w_out.shape[0]
    total = blocks * rows
    cols = tile_of(width, 1024)
    packed = pooled[0].shape[1]
    experts_all = w_router_t.shape[0]

    def whole(shape):
        return pl.BlockSpec(shape, lambda i: (0, 0), pipeline_mode=pl.Buffered(1))

    def tiles(height):
        return pl.BlockSpec((height, cols), lambda i: (0, i))

    need = total * (cols * 16 + packed * 6 + 8 * LANES * 4) + 4 * latent * cols
    return pl.pallas_call(
        lambda *refs: norm_kernel(far, blocks, rows, latent, width, *refs),
        grid=(width // cols,),
        in_specs=[pl.BlockSpec(memory_space=pltpu.SMEM)]
        + [whole(a.shape) for a in pooled]
        + [tiles(rows)] * blocks
        + [tiles(latent), tiles(1), tiles(experts_all)],
        out_shape=[
            jax.ShapeDtypeStruct((far * rows, width), jnp.bfloat16),
            jax.ShapeDtypeStruct((total - far * rows, width), jnp.bfloat16),
            jax.ShapeDtypeStruct((total, LANES), jnp.float32),
            jax.ShapeDtypeStruct((total, LANES), jnp.float32),
            jax.ShapeDtypeStruct((rows, width), jnp.float32),
        ],
        out_specs=[tiles(far * rows), tiles(total - far * rows)]
        + [whole((total, LANES)), whole((total, LANES)), tiles(rows)],
        scratch_shapes=[
            pltpu.VMEM((total, packed), jnp.bfloat16),
            pltpu.VMEM((total, packed), jnp.bfloat16),
            pltpu.VMEM((total, LANES), jnp.float32),
            pltpu.VMEM((total, experts_all), jnp.float32),
        ],
        compiler_params=pltpu.CompilerParams(
            dimension_semantics=("arbitrary",), vmem_limit_bytes=(int(need) // (1 << 20) + 6) << 20
        ),
        cost_estimate=pl.CostEstimate(
            flops=2 * total * width * latent,
            bytes_accessed=4 * total * width * 2 + latent * width * 2,
            transcendentals=total,
        ),
        name="normalize",
    )(scalars, *pooled, *resid_blocks, w_out, gain, w_router_t)


def lookup_kernel(owner, lengths, table, device, row_lengths, scalars):
    for j in range(row_lengths.shape[0]):
        row_lengths[j] = lengths[owner[device[0] * row_lengths.shape[0] + j]]
    for j in range(scalars.shape[0]):
        scalars[j] = table[device[0] * scalars.shape[0] + j]


LONG = dict(flops=10**10, bytes_accessed=10**8, transcendentals=0)


def lookup(owner, lengths, table, device_index, rows):
    scalar = pl.BlockSpec(memory_space=pltpu.SMEM)
    return pl.pallas_call(
        lookup_kernel,
        in_specs=[scalar] * 4,
        out_specs=[scalar] * 2,
        out_shape=[
            jax.ShapeDtypeStruct((rows,), jnp.int32),
            jax.ShapeDtypeStruct(table.shape[1:], jnp.int32),
        ],
        cost_estimate=pl.CostEstimate(**LONG),
        name="lookup",
    )(owner, lengths, table.reshape(-1), device_index[None])


def attention_kernel(context, latent, q, cache, fresh, lengths, routes, packet, keys_a, keys_b, total):
    step = pl.program_id(0)
    rows, kv_width = q.shape[1], cache.shape[1]
    wide = keys_a.shape[1]
    pairs = q.shape[2] // (2 * kv_width)
    keys = keys_a.shape[0]
    cached = cache.shape[0]

    @pl.when(step == 0)
    def _():
        keys_a[...] = jnp.zeros_like(keys_a)
        keys_a[:cached, :kv_width] = cache[...]
        keys_a[cached:, :kv_width] = fresh[...]
        shifted = pltpu.roll(keys_a[...].astype(jnp.float32), wide - kv_width, 1)
        keys_b[...] = shifted.astype(jnp.bfloat16)

    row = lax.broadcasted_iota(jnp.int32, (rows, keys), 0)
    key = lax.broadcasted_iota(jnp.int32, (rows, keys), 1)
    place = key // rows
    length = jnp.zeros((rows, keys), jnp.int32)
    for j in range(rows):
        length = jnp.where(row == j, lengths[j], length)
    seen = (place < length) & (place < context)
    seen = seen | ((place >= context) & (place <= context + step))
    bias = jnp.where(seen & (key % rows == row), 0.0, -1e30)
    summed = jnp.zeros((rows, keys), jnp.float32)
    for held, first in ((keys_a, 0), (keys_b, 2 * kv_width - wide)):
        heads = [
            q[0, :, 2 * kv_width * i + first : 2 * kv_width * i + first + wide].astype(jnp.float32)
            for i in range(pairs)
        ]
        scores = lax.dot_general(
            jnp.concatenate(heads, axis=0).astype(jnp.bfloat16),
            held[...],
            (((1,), (1,)), ((), ())),
            preferred_element_type=jnp.float32,
        )
        scores = (scores * qk_scale).reshape(pairs, rows, keys) + bias[None]
        e = jnp.exp(scores - jnp.max(scores, axis=2, keepdims=True))
        weights = e / jnp.sum(e, axis=2, keepdims=True)
        summed = summed + jnp.sum(weights.astype(jnp.bfloat16).astype(jnp.float32), axis=0)
    total[pl.ds(pl.multiple_of(step * rows, rows), rows), :] = summed

    @pl.when(step == pl.num_programs(0) - 1)
    def _():
        high = total[...].astype(jnp.bfloat16)
        low = (total[...] - high.astype(jnp.float32)).astype(jnp.bfloat16)
        values = keys_a[:, :latent]
        pooled = jnp.dot(high, values, preferred_element_type=jnp.float32)
        pooled = pooled + jnp.dot(low, values, preferred_element_type=jnp.float32)
        packet[:, :latent] = pooled.astype(jnp.bfloat16)
        lane = lax.broadcasted_iota(jnp.int32, (packet.shape[0], LANES), 1)
        routed = jnp.zeros(lane.shape, jnp.float32)
        for k in range(routes.shape[1]):
            routed = jnp.where(routes[:, k : k + 1] == lane, 1.0, routed)
        packet[:, latent:] = routed.astype(jnp.bfloat16)


def attention(q_abs, cache, fresh, lengths, routes, context, latent):
    steps, rows, _ = q_abs.shape
    kv_width = cache.shape[1]
    keys = cache.shape[0] + fresh.shape[0]
    wide = -(-kv_width // LANES) * LANES

    def whole(a):
        return pl.BlockSpec(a.shape, lambda i: (0, 0), pipeline_mode=pl.Buffered(1))

    return pl.pallas_call(
        lambda *refs: attention_kernel(context, latent, *refs),
        grid=(steps,),
        in_specs=[pl.BlockSpec((1, rows, q_abs.shape[2]), lambda i: (i, 0, 0))]
        + [whole(cache), whole(fresh), pl.BlockSpec(memory_space=pltpu.SMEM), whole(routes)],
        out_shape=jax.ShapeDtypeStruct((steps * rows, latent + LANES), jnp.bfloat16),
        out_specs=pl.BlockSpec((steps * rows, latent + LANES), lambda i: (0, 0)),
        scratch_shapes=[
            pltpu.VMEM((keys, wide), jnp.bfloat16),
            pltpu.VMEM((keys, wide), jnp.bfloat16),
            pltpu.VMEM((steps * rows, keys), jnp.float32),
        ],
        compiler_params=pltpu.CompilerParams(
            dimension_semantics=("arbitrary",), vmem_limit_bytes=(10 << 20) + 10240 * keys
        ),
        cost_estimate=pl.CostEstimate(
            flops=2 * q_abs.size * keys, bytes_accessed=2 * q_abs.size, transcendentals=0
        ),
        name="attention",
    )(q_abs, cache, fresh, lengths, routes)


def local(
    q_abs,
    new_lat,
    latent_cache,
    lengths,
    owner,
    resid,
    routes,
    w_out,
    norm_gain,
    w_router,
    w_gate,
    w_up,
    w_down,
):
    devices = lax.axis_size("expert")
    device_index = lax.axis_index("expert")
    step_count, row_count, width = resid.shape
    rows = step_count * row_count
    experts_all = w_router.shape[1]
    sharers = devices // experts_all
    chips = devices // 2
    half = chips // 2
    far, near = distances(chips)
    hold = lax.optimization_barrier
    stay = lambda a: pltpu.with_memory_space_constraint(a, pltpu.HBM)
    cut = rows // 2
    sibling = sibling_perm(chips)

    def send(a, perm):
        return lax.ppermute(a, "expert", perm)

    to_right, to_left = shift_perm(chips, 1), shift_perm(chips, -1)
    parted = [
        shift_perm(chips, 1 - 2 * core)[2 * p + core] for p in range(chips) for core in range(2)
    ]
    first_core = device_index % 2 == 0

    def around(to_the_right, to_the_left):
        return send(to_the_right, to_right), send(to_the_left, to_left)

    positions, kv_width = latent_cache.shape[1:]
    wanted = (owner[:, None] == jnp.arange(owner.shape[0], dtype=jnp.int32)).astype(jnp.bfloat16)
    ordered = jnp.einsum(
        "jr,rpk->pjk", wanted, latent_cache, preferred_element_type=jnp.float32
    ).astype(jnp.bfloat16)
    ordered = ordered.reshape(positions, devices, row_count, kv_width).swapaxes(0, 1)
    owned = lax.all_to_all(ordered, "expert", split_axis=0, concat_axis=0, tiled=True)

    mine = resid.reshape(rows, width)
    held, sib = {0: mine}, {}
    held[-1], held[1] = around(mine, mine)
    table = [
        [device // sharers] + places
        for chip, places in enumerate(gathered_place(chips))
        for device in (2 * chip, 2 * chip + 1)
    ]
    row_lengths, scalars = lookup(
        owner, lengths, jnp.array(table, jnp.int32), device_index, row_count
    )
    row_lengths, scalars, held = hold((row_lengths, scalars, held))
    held[-2], held[2] = around(held[-1], held[1])
    sib[0] = send(mine, sibling)
    sib[1], sib[-1] = send(held[1], sibling), send(held[-1], sibling)
    gain = norm_gain[None, :]
    packet = attention(
        q_abs,
        owned.reshape(-1, kv_width),
        new_lat.reshape(rows, kv_width),
        stay(row_lengths),
        routes.reshape(rows, -1),
        devices * positions,
        w_out.shape[0],
    )
    packet, gain, held, sib = hold((packet, gain, held, sib))

    high, low = gather_steps(chips)
    along = [send(packet, step_perm(chips, i, 0)) for i in range(1, high)]
    for t in range(3, half):
        held[-t], held[t] = around(held[1 - t], held[t - 1])
    along, held = hold((along, held))
    along = jnp.concatenate([packet] + along, axis=0)
    along, w_gate = hold((along, w_gate))
    w_gate = jnp.where(device_index >= 0, w_gate, jnp.zeros_like(w_gate))
    across = [send(along, step_perm(chips, 0, i)) for i in range(1, low)]
    held[half] = send(jnp.where(first_core, held[1 - half], held[half - 1]), parted)
    along_sib = send(along, sibling)
    sib[2], sib[-2] = send(held[2], sibling), send(held[-2], sibling)
    across, along_sib, held, sib, w_gate = hold((across, along_sib, held, sib, w_gate))
    for d in held:
        if d not in sib:
            sib[d] = send(held[d], sibling)
    across = across[0] if low == 2 else jnp.concatenate(across, axis=0)

    f32 = jnp.float32
    held[0] = stay(held[0])

    x_far, x_near, scale, weight, hidden = normalize(
        2 * len(far),
        stay(scalars),
        [along, across, along_sib, send(across, sibling)],
        [a[d] for part in (far, near) for a in (held, sib) for d in part],
        stay(w_out),
        gain,
        stay(w_router.T),
    )
    far_rows = x_far.shape[0]

    def product(a, w):
        return jnp.dot(a, w[0], preferred_element_type=f32)

    def activate(a, b, at):
        r, g = scale[at, :1], weight[at, :1]
        return (jax.nn.silu(a * r) * (b * r) * g).astype(jnp.bfloat16)

    sums = {}

    def swap(dists, y):
        return y, send(y[len(dists) * rows :], sibling)

    def add_up(dists, y, received):
        for i, d in enumerate(dists):
            at = slice(i * rows, (i + 1) * rows)
            sums[d] = y[at].astype(f32) + received[at].astype(f32)

    def both(right, left):
        return around(right.astype(jnp.bfloat16), left.astype(jnp.bfloat16))

    act = hold(activate(product(x_far, w_gate), product(x_far, w_up), slice(0, far_rows)))
    y, received = swap(far, product(act, w_down).astype(jnp.bfloat16))
    gated, y, received = hold((product(x_near, w_gate), y, received))
    add_up(far, y, received)
    right, left = both(sums[half][:cut], sums[half][cut:])
    act = activate(gated, product(x_near, w_up), slice(far_rows, None))
    act, right, left = hold((act, right, left))
    right = jnp.concatenate([right.astype(f32), jnp.zeros((rows - cut, width), f32)], axis=0)
    left = jnp.concatenate([jnp.zeros((cut, width), f32), left.astype(f32)], axis=0)
    right, left = both(sums[half - 1] + right, sums[1 - half] + left)
    y, received = swap(near, product(act, w_down).astype(jnp.bfloat16))
    y, received, right, left = hold((y, received, right, left))
    add_up(near, y, received)
    for t in range(half - 2, 0, -1):
        right, left = hold(both(sums[t] + right.astype(f32), sums[-t] + left.astype(f32)))
    mixed = hidden + sums[0] + right.astype(f32) + left.astype(f32)
    return mixed.astype(jnp.bfloat16).reshape(step_count, row_count, width)


def solution(mesh):
    return jax.shard_map(
        local,
        mesh=mesh,
        in_specs=(
            P(None, ("group", "expert"), None),
            P(None, ("group", "expert"), None),
            P("group", "expert", None),
            P("group"),
            P("group"),
            P(None, ("group", "expert"), None),
            P(None, ("group", "expert"), None),
            P(),
            P(),
            P(),
            P("expert", None, None),
            P("expert", None, None),
            P("expert", None, None),
        ),
        out_specs=P(None, ("group", "expert"), None),
        check_vma=False,
    )
```

```python
import jax
import jax.numpy as jnp
from jax import lax
from jax.experimental import pallas as pl
from jax.experimental.pallas import tpu as pltpu
from jax.sharding import PartitionSpec as P

qk_scale = 192.0 ** (-0.5)
LANES = 128


def ring_of(chips):
    return list(range(0, chips, 2)) + list(range(chips - 1, 0, -2))


def shift_perm(chips, by):
    ring = ring_of(chips)
    return [
        (2 * ring[p] + core, 2 * ring[(p + by) % chips] + core)
        for p in range(chips)
        for core in range(2)
    ]


def sibling_perm(chips):
    return [(d, d ^ 1) for d in range(2 * chips)]


def distances(chips):
    half = chips // 2
    far = [half, half - 1, 1 - half]
    return far, [0] + [d for t in range(1, half - 1) for d in (t, -t)]


def gather_steps(chips):
    high = 4 if chips % 4 == 0 else 2
    return high, chips // high


def step_perm(chips, by_high, by_low):
    high, low = gather_steps(chips)
    return [
        (2 * (h * low + l) + core, 2 * ((h ^ by_high) * low + (l ^ by_low)) + core)
        for h in range(high)
        for l in range(low)
        for core in range(2)
    ]


def gathered_place(chips):
    high, low = gather_steps(chips)
    ring = ring_of(chips)
    table = [[] for _ in range(chips)]
    for p, chip in enumerate(ring):
        for part in distances(chips):
            for side in (0, chips):
                for d in part:
                    other = ring[(p + d) % chips]
                    by_high = (other // low) ^ (chip // low)
                    by_low = (other % low) ^ (chip % low)
                    table[chip].append(side + by_low * high + by_high)
    return table


def tile_of(size, most):
    return max(t for t in range(LANES, min(size, most) + 1, LANES) if size % t == 0)


def norm_kernel(far, blocks, rows, latent, width, *refs):
    scalars = refs[0]
    pooled = refs[1:5]
    resid = refs[5 : 5 + blocks]
    w_out, gain, w_router, x_far, x_near = refs[5 + blocks : 10 + blocks]
    scale, weight, hidden, raw, joined, ssq, logits = refs[10 + blocks :]
    step = pl.program_id(0)
    cols = w_out.shape[1]
    total = blocks * rows
    far_rows = far * rows
    experts_all = w_router.shape[0]
    chunk = min(512, total)

    @pl.when(step == 0)
    def _():
        start = 0
        for piece in pooled:
            raw[start : start + piece.shape[0], :] = piece[...]
            start += piece.shape[0]
        for b in range(blocks):
            place = pl.ds(pl.multiple_of(scalars[1 + b] * rows, rows), rows)
            joined[b * rows : (b + 1) * rows, :] = raw[place, :]
        ssq[...] = jnp.zeros_like(ssq)
        logits[...] = jnp.zeros_like(logits)

    g = gain[...].astype(jnp.float32)
    for c in range(0, total, chunk):
        end = min(c + chunk, total)
        proj = jnp.dot(joined[c:end, :latent], w_out[...], preferred_element_type=jnp.float32)
        for b in range(c // rows, end // rows):
            at = slice(b * rows, (b + 1) * rows)
            h = proj[b * rows - c : (b + 1) * rows - c] + resid[b][...].astype(jnp.float32)
            if b == far:
                hidden[...] = h
            scaled = (h * g).astype(jnp.bfloat16)
            if b < far:
                x_far[at, :] = scaled
            else:
                x_near[(b - far) * rows : (b - far + 1) * rows, :] = scaled
            sq = h * h
            part = sq[:, :LANES]
            for k in range(1, cols // LANES):
                part = part + sq[:, k * LANES : (k + 1) * LANES]
            ssq[at, :] += part
    nt = (((1,), (1,)), ((), ()))
    for x, at in ((x_far, slice(0, far_rows)), (x_near, slice(far_rows, total))):
        logits[at, :] += lax.dot_general(
            x[...], w_router[...], nt, preferred_element_type=jnp.float32
        )

    @pl.when(step == pl.num_programs(0) - 1)
    def _():
        mean = jnp.sum(ssq[...], axis=1, keepdims=True) * (1.0 / width)
        r = lax.rsqrt(mean + 1e-06)
        mask = joined[:, latent : latent + experts_all].astype(jnp.float32)
        affinity = jax.nn.sigmoid(logits[...] * r) * mask
        lane = lax.broadcasted_iota(jnp.int32, affinity.shape, 1)
        mine = jnp.sum(jnp.where(lane == scalars[0], affinity, 0.0), axis=1, keepdims=True)
        gate = 2.5 * mine / jnp.sum(affinity, axis=1, keepdims=True)
        scale[...] = jnp.broadcast_to(r, scale.shape)
        weight[...] = jnp.broadcast_to(gate, weight.shape)


def normalize(far, scalars, pooled, resid_blocks, w_out, gain, w_router_t):
    blocks = len(resid_blocks)
    rows, width = resid_blocks[0].shape
    latent = w_out.shape[0]
    total = blocks * rows
    cols = tile_of(width, 1024)
    packed = pooled[0].shape[1]
    experts_all = w_router_t.shape[0]

    def whole(shape):
        return pl.BlockSpec(shape, lambda i: (0, 0), pipeline_mode=pl.Buffered(1))

    def tiles(height):
        return pl.BlockSpec((height, cols), lambda i: (0, i))

    need = total * (cols * 16 + packed * 6 + 8 * LANES * 4) + 4 * latent * cols
    return pl.pallas_call(
        lambda *refs: norm_kernel(far, blocks, rows, latent, width, *refs),
        grid=(width // cols,),
        in_specs=[pl.BlockSpec(memory_space=pltpu.SMEM)]
        + [whole(a.shape) for a in pooled]
        + [tiles(rows)] * blocks
        + [tiles(latent), tiles(1), tiles(experts_all)],
        out_shape=[
            jax.ShapeDtypeStruct((far * rows, width), jnp.bfloat16),
            jax.ShapeDtypeStruct((total - far * rows, width), jnp.bfloat16),
            jax.ShapeDtypeStruct((total, LANES), jnp.float32),
            jax.ShapeDtypeStruct((total, LANES), jnp.float32),
            jax.ShapeDtypeStruct((rows, width), jnp.float32),
        ],
        out_specs=[tiles(far * rows), tiles(total - far * rows)]
        + [whole((total, LANES)), whole((total, LANES)), tiles(rows)],
        scratch_shapes=[
            pltpu.VMEM((total, packed), jnp.bfloat16),
            pltpu.VMEM((total, packed), jnp.bfloat16),
            pltpu.VMEM((total, LANES), jnp.float32),
            pltpu.VMEM((total, experts_all), jnp.float32),
        ],
        compiler_params=pltpu.CompilerParams(
            dimension_semantics=("arbitrary",), vmem_limit_bytes=(int(need) // (1 << 20) + 3) << 20
        ),
        cost_estimate=pl.CostEstimate(
            flops=2 * total * width * latent,
            bytes_accessed=4 * total * width * 2 + latent * width * 2,
            transcendentals=total,
        ),
        name="normalize",
    )(scalars, *pooled, *resid_blocks, w_out, gain, w_router_t)


def lookup_kernel(owner, lengths, table, device, row_lengths, scalars):
    for j in range(row_lengths.shape[0]):
        row_lengths[j] = lengths[owner[device[0] * row_lengths.shape[0] + j]]
    for j in range(scalars.shape[0]):
        scalars[j] = table[device[0] * scalars.shape[0] + j]


LONG = dict(flops=10**10, bytes_accessed=10**8, transcendentals=0)


def lookup(owner, lengths, table, device_index, rows):
    scalar = pl.BlockSpec(memory_space=pltpu.SMEM)
    return pl.pallas_call(
        lookup_kernel,
        in_specs=[scalar] * 4,
        out_specs=[scalar] * 2,
        out_shape=[
            jax.ShapeDtypeStruct((rows,), jnp.int32),
            jax.ShapeDtypeStruct(table.shape[1:], jnp.int32),
        ],
        cost_estimate=pl.CostEstimate(**LONG),
        name="lookup",
    )(owner, lengths, table.reshape(-1), device_index[None])


def attention_kernel(context, latent, q, cache, fresh, lengths, routes, packet, keys_a, keys_b, total):
    step = pl.program_id(0)
    rows, kv_width = q.shape[1], cache.shape[1]
    wide = keys_a.shape[1]
    pairs = q.shape[2] // (2 * kv_width)
    keys = keys_a.shape[0]
    cached = cache.shape[0]

    @pl.when(step == 0)
    def _():
        keys_a[...] = jnp.zeros_like(keys_a)
        keys_a[:cached, :kv_width] = cache[...]
        keys_a[cached:, :kv_width] = fresh[...]
        shifted = pltpu.roll(keys_a[...].astype(jnp.float32), wide - kv_width, 1)
        keys_b[...] = shifted.astype(jnp.bfloat16)

    row = lax.broadcasted_iota(jnp.int32, (rows, keys), 0)
    key = lax.broadcasted_iota(jnp.int32, (rows, keys), 1)
    place = key // rows
    length = jnp.zeros((rows, keys), jnp.int32)
    for j in range(rows):
        length = jnp.where(row == j, lengths[j], length)
    seen = (place < length) & (place < context)
    seen = seen | ((place >= context) & (place <= context + step))
    bias = jnp.where(seen & (key % rows == row), 0.0, -1e30)
    summed = jnp.zeros((rows, keys), jnp.float32)
    for held, first in ((keys_a, 0), (keys_b, 2 * kv_width - wide)):
        heads = [
            q[0, :, 2 * kv_width * i + first : 2 * kv_width * i + first + wide].astype(jnp.float32)
            for i in range(pairs)
        ]
        scores = lax.dot_general(
            jnp.concatenate(heads, axis=0).astype(jnp.bfloat16),
            held[...],
            (((1,), (1,)), ((), ())),
            preferred_element_type=jnp.float32,
        )
        scores = (scores * qk_scale).reshape(pairs, rows, keys) + bias[None]
        e = jnp.exp(scores - jnp.max(scores, axis=2, keepdims=True))
        weights = e / jnp.sum(e, axis=2, keepdims=True)
        summed = summed + jnp.sum(weights.astype(jnp.bfloat16).astype(jnp.float32), axis=0)
    total[pl.ds(pl.multiple_of(step * rows, rows), rows), :] = summed

    @pl.when(step == pl.num_programs(0) - 1)
    def _():
        high = total[...].astype(jnp.bfloat16)
        low = (total[...] - high.astype(jnp.float32)).astype(jnp.bfloat16)
        values = keys_a[:, :latent]
        pooled = jnp.dot(high, values, preferred_element_type=jnp.float32)
        pooled = pooled + jnp.dot(low, values, preferred_element_type=jnp.float32)
        packet[:, :latent] = pooled.astype(jnp.bfloat16)
        lane = lax.broadcasted_iota(jnp.int32, (packet.shape[0], LANES), 1)
        routed = jnp.zeros(lane.shape, jnp.float32)
        for k in range(routes.shape[1]):
            routed = jnp.where(routes[:, k : k + 1] == lane, 1.0, routed)
        packet[:, latent:] = routed.astype(jnp.bfloat16)


def attention(q_abs, cache, fresh, lengths, routes, context, latent):
    steps, rows, _ = q_abs.shape
    kv_width = cache.shape[1]
    keys = cache.shape[0] + fresh.shape[0]
    wide = -(-kv_width // LANES) * LANES

    def whole(a):
        return pl.BlockSpec(a.shape, lambda i: (0, 0), pipeline_mode=pl.Buffered(1))

    return pl.pallas_call(
        lambda *refs: attention_kernel(context, latent, *refs),
        grid=(steps,),
        in_specs=[pl.BlockSpec((1, rows, q_abs.shape[2]), lambda i: (i, 0, 0))]
        + [whole(cache), whole(fresh), pl.BlockSpec(memory_space=pltpu.SMEM), whole(routes)],
        out_shape=jax.ShapeDtypeStruct((steps * rows, latent + LANES), jnp.bfloat16),
        out_specs=pl.BlockSpec((steps * rows, latent + LANES), lambda i: (0, 0)),
        scratch_shapes=[
            pltpu.VMEM((keys, wide), jnp.bfloat16),
            pltpu.VMEM((keys, wide), jnp.bfloat16),
            pltpu.VMEM((steps * rows, keys), jnp.float32),
        ],
        compiler_params=pltpu.CompilerParams(
            dimension_semantics=("arbitrary",), vmem_limit_bytes=(10 << 20) + 10240 * keys
        ),
        cost_estimate=pl.CostEstimate(
            flops=2 * q_abs.size * keys, bytes_accessed=2 * q_abs.size, transcendentals=0
        ),
        name="attention",
    )(q_abs, cache, fresh, lengths, routes)


def local(
    q_abs,
    new_lat,
    latent_cache,
    lengths,
    owner,
    resid,
    routes,
    w_out,
    norm_gain,
    w_router,
    w_gate,
    w_up,
    w_down,
):
    devices = lax.axis_size("expert")
    device_index = lax.axis_index("expert")
    step_count, row_count, width = resid.shape
    rows = step_count * row_count
    experts_all = w_router.shape[1]
    sharers = devices // experts_all
    chips = devices // 2
    half = chips // 2
    far, near = distances(chips)
    hold = lax.optimization_barrier
    stay = lambda a: pltpu.with_memory_space_constraint(a, pltpu.HBM)
    cut = rows // 2
    sibling = sibling_perm(chips)

    def send(a, perm):
        return lax.ppermute(a, "expert", perm)

    to_right, to_left = shift_perm(chips, 1), shift_perm(chips, -1)
    parted = [
        shift_perm(chips, 1 - 2 * core)[2 * p + core] for p in range(chips) for core in range(2)
    ]
    first_core = device_index % 2 == 0

    def around(to_the_right, to_the_left):
        return send(to_the_right, to_right), send(to_the_left, to_left)

    positions, kv_width = latent_cache.shape[1:]
    wanted = (owner[:, None] == jnp.arange(owner.shape[0], dtype=jnp.int32)).astype(jnp.bfloat16)
    ordered = jnp.einsum(
        "jr,rpk->pjk", wanted, latent_cache, preferred_element_type=jnp.float32
    ).astype(jnp.bfloat16)
    ordered = ordered.reshape(positions, devices, row_count, kv_width).swapaxes(0, 1)
    owned = lax.all_to_all(ordered, "expert", split_axis=0, concat_axis=0, tiled=True)

    mine = resid.reshape(rows, width)
    held, sib = {0: mine}, {}
    held[-1], held[1] = around(mine, mine)
    table = [
        [device // sharers] + places
        for chip, places in enumerate(gathered_place(chips))
        for device in (2 * chip, 2 * chip + 1)
    ]
    row_lengths, scalars = lookup(
        owner, lengths, jnp.array(table, jnp.int32), device_index, row_count
    )
    row_lengths, scalars, held = hold((row_lengths, scalars, held))
    held[-2], held[2] = around(held[-1], held[1])
    sib[0] = send(mine, sibling)
    sib[1], sib[-1] = send(held[1], sibling), send(held[-1], sibling)
    gain = norm_gain[None, :]
    packet = attention(
        q_abs,
        owned.reshape(-1, kv_width),
        new_lat.reshape(rows, kv_width),
        stay(row_lengths),
        routes.reshape(rows, -1),
        devices * positions,
        w_out.shape[0],
    )
    packet, gain, held, sib = hold((packet, gain, held, sib))

    high, low = gather_steps(chips)
    along = [send(packet, step_perm(chips, i, 0)) for i in range(1, high)]
    for t in range(3, half):
        held[-t], held[t] = around(held[1 - t], held[t - 1])
    along, held = hold((along, held))
    along = jnp.concatenate([packet] + along, axis=0)
    along, w_gate = hold((along, w_gate))
    w_gate = jnp.where(device_index >= 0, w_gate, jnp.zeros_like(w_gate))
    across = [send(along, step_perm(chips, 0, i)) for i in range(1, low)]
    held[half] = send(jnp.where(first_core, held[1 - half], held[half - 1]), parted)
    along_sib = send(along, sibling)
    sib[2], sib[-2] = send(held[2], sibling), send(held[-2], sibling)
    across, along_sib, held, sib, w_gate = hold((across, along_sib, held, sib, w_gate))
    for d in held:
        if d not in sib:
            sib[d] = send(held[d], sibling)
    across = across[0] if low == 2 else jnp.concatenate(across, axis=0)

    f32 = jnp.float32
    held[0] = stay(held[0])

    x_far, x_near, scale, weight, hidden = normalize(
        2 * len(far),
        stay(scalars),
        [along, across, along_sib, send(across, sibling)],
        [a[d] for part in (far, near) for a in (held, sib) for d in part],
        stay(w_out),
        gain,
        stay(w_router.T),
    )
    far_rows = x_far.shape[0]

    def product(a, w):
        return jnp.dot(a, w[0], preferred_element_type=f32)

    def activate(a, b, at):
        r, g = scale[at, :1], weight[at, :1]
        return (jax.nn.silu(a * r) * (b * r) * g).astype(jnp.bfloat16)

    sums = {}

    def swap(dists, y):
        return y, send(y[len(dists) * rows :], sibling)

    def add_up(dists, y, received):
        for i, d in enumerate(dists):
            at = slice(i * rows, (i + 1) * rows)
            sums[d] = y[at].astype(f32) + received[at].astype(f32)

    def both(right, left):
        return around(right.astype(jnp.bfloat16), left.astype(jnp.bfloat16))

    act = hold(activate(product(x_far, w_gate), product(x_far, w_up), slice(0, far_rows)))
    y, received = swap(far, product(act, w_down).astype(jnp.bfloat16))
    gated, y, received = hold((product(x_near, w_gate), y, received))
    add_up(far, y, received)
    right, left = both(sums[half][:cut], sums[half][cut:])
    act = activate(gated, product(x_near, w_up), slice(far_rows, None))
    act, right, left = hold((act, right, left))
    right = jnp.concatenate([right.astype(f32), jnp.zeros((rows - cut, width), f32)], axis=0)
    left = jnp.concatenate([jnp.zeros((cut, width), f32), left.astype(f32)], axis=0)
    right, left = both(sums[half - 1] + right, sums[1 - half] + left)
    y, received = swap(near, product(act, w_down).astype(jnp.bfloat16))
    y, received, right, left = hold((y, received, right, left))
    add_up(near, y, received)
    for t in range(half - 2, 0, -1):
        right, left = hold(both(sums[t] + right.astype(f32), sums[-t] + left.astype(f32)))
    mixed = hidden + sums[0] + right.astype(f32) + left.astype(f32)
    return mixed.astype(jnp.bfloat16).reshape(step_count, row_count, width)


def solution(mesh):
    return jax.shard_map(
        local,
        mesh=mesh,
        in_specs=(
            P(None, ("group", "expert"), None),
            P(None, ("group", "expert"), None),
            P("group", "expert", None),
            P("group"),
            P("group"),
            P(None, ("group", "expert"), None),
            P(None, ("group", "expert"), None),
            P(),
            P(),
            P(),
            P("expert", None, None),
            P("expert", None, None),
            P("expert", None, None),
        ),
        out_specs=P(None, ("group", "expert"), None),
        check_vma=False,
    )
```
